32 devices in a mesh: seq: 16 (over z, y, x), head: 2 (over core).
Axes of the slice: x: 2, y: 2, z: 4, core: 2. Of those that a mesh axis runs over, the one named last changes fastest.
Arguments:
- trunk_query: bfloat16 [8192, 16, 128], P('seq', 'head'), may hold values from -5 to 5
- trunk_key: bfloat16 [8192, 16, 128], P('seq', 'head'), may hold values from -5 to 5
- trunk_value: bfloat16 [8192, 16, 128], P('seq', 'head'), may hold values from -5 to 5
- trunk_wquery: bfloat16 [8192, 16, 128], P('seq', 'head'), may hold values from -5 to 5
- trunk_wkey: bfloat16 [8192, 4, 128], P('seq', 'head'), may hold values from -5 to 5
- trunk_wvalue: bfloat16 [8192, 4, 128], P('seq', 'head'), may hold values from -5 to 5
- branch_query: bfloat16 [16384, 16, 128], P('seq', 'head'), may hold values from -5 to 5
- branch_wquery: bfloat16 [16384, 16, 128], P('seq', 'head'), may hold values from -5 to 5
- branch_wkey: bfloat16 [16384, 4, 128], P('seq', 'head'), may hold values from -5 to 5
- branch_wvalue: bfloat16 [16384, 4, 128], P('seq', 'head'), may hold values from -5 to 5
- level_gain: float32 [16, 11], P('head'), may hold values from 0.1 to 1.9
- fork_block: int32 [16], P('seq'), may hold values from 0 to 3
Outputs:
- trunk_out: bfloat16 [8192, 16, 128], P('seq', 'head')
- branch_out: bfloat16 [16384, 16, 128], P('seq', 'head')
The draws below stay inside these ranges and needn't reach their ends.
All inputs are finite; a program needn't handle non-finite values.
Results may differ from the reference program's by a relative error of at most 0.0045.
The reference program's roundings to bfloat16 on the way count: a program that leaves them out, or rounds other values in their place, can miss the bound.
Values may be sent and summed in bfloat16 or wider, within the bound.
No kernel may reach another device: no remote copies, remote signals or barrier semaphores. Data moves between devices by JAX's collectives and lax.ppermute only.
A program may use at most 128 MiB of HBM per device.

```python
import math
from functools import partial
import jax
import jax.numpy as jnp
from jax import lax

DH = 128
BLK = 128
WIN = 512
LEVELS = 11
TOK_DEV = 512
BR_DEV = 1024
NB = 4
H = 16
KVH = 4
TRUNK = 8192
BRANCH = 16384
N_SEQ = 16


def drawn_pair(key, row_count, head_count, kv_groups, head_width, salt):
    base = jax.random.fold_in(key, salt)
    queries = jnp.clip(jax.random.normal(jax.random.fold_in(base, 2), (row_count, head_count, head_width), jnp.float32), -5.0, 5.0)
    key_rows = jnp.clip(jax.random.normal(jax.random.fold_in(base, 3), (row_count, kv_groups, head_width), jnp.float32), -5.0, 5.0)
    return (queries, key_rows)


def draw_trunk_wquery(key, part):
    return drawn_pair(key, TRUNK, H, KVH, DH, 11)[0].astype(jnp.bfloat16)


def draw_trunk_wkey(key, part):
    return drawn_pair(key, TRUNK, H, KVH, DH, 11)[1].astype(jnp.bfloat16)


def draw_branch_wquery(key, part):
    return drawn_pair(key, BRANCH, H, KVH, DH, 23)[0].astype(jnp.bfloat16)


def draw_branch_wkey(key, part):
    return drawn_pair(key, BRANCH, H, KVH, DH, 23)[1].astype(jnp.bfloat16)


def set_ends(values, stream_key, low, largest):
    extent = values.shape
    index_at = [jax.random.randint(jax.random.fold_in(stream_key, axis), (), 0, extent[axis]) for axis in range(len(extent))]
    values = values.at[tuple(index_at)].set(low)
    longest = extent.index(max(extent))
    index_at[longest] = (index_at[longest] + 1) % extent[longest]
    return values.at[tuple(index_at)].set(largest)


def shard_levels(stream_key, shape, pieces, low, high):
    factor_of, own = 1.0, jax.random.fold_in(stream_key, 6)
    for dim, parts in pieces:
        heights = jnp.exp(jax.random.uniform(jax.random.fold_in(own, dim), (parts,), jnp.float32, low / len(pieces), high / len(pieces)))
        factor_of = factor_of * jnp.repeat(heights, shape[dim] // parts).reshape([-1 if axis == dim else 1 for axis in range(len(shape))])
    return factor_of


def centred(own_key, shape, deviation, most, pieces=(), kind=jnp.bfloat16):
    gain = shard_levels(own_key, shape, pieces, -0.22, 0.18) if pieces else 1.0
    drawn = jax.random.normal(own_key, shape, jnp.float32) * deviation * gain
    return jnp.minimum(jnp.maximum(drawn, -most), most).astype(kind)


def setup_inputs(seed: int = 0) -> dict:
    streams_of = jax.random.split(jax.random.key(seed), 13)
    return {
        "trunk_query": centred(streams_of[0], (TRUNK, H, DH), 1.0, 5.0, ((0, 16), (1, 2))),
        "trunk_key": centred(streams_of[1], (TRUNK, H, DH), 1.0, 5.0, ((0, 16), (1, 2))),
        "trunk_value": centred(streams_of[2], (TRUNK, H, DH), 1.0, 5.0, ((0, 16), (1, 2))),
        "trunk_wquery": draw_trunk_wquery(jax.random.fold_in(streams_of[12], 71), 0),
        "trunk_wkey": draw_trunk_wkey(jax.random.fold_in(streams_of[12], 71), 0),
        "trunk_wvalue": centred(streams_of[5], (TRUNK, KVH, DH), 1.0, 5.0, ((0, 16), (1, 2))),
        "branch_query": centred(streams_of[6], (BRANCH, H, DH), 1.0, 5.0, ((0, 16), (1, 2))),
        "branch_wquery": draw_branch_wquery(jax.random.fold_in(streams_of[12], 71), 0),
        "branch_wkey": draw_branch_wkey(jax.random.fold_in(streams_of[12], 71), 0),
        "branch_wvalue": centred(streams_of[9], (BRANCH, KVH, DH), 1.0, 5.0, ((0, 16), (1, 2))),
        "level_gain": jnp.clip(1.0 + 0.18 * jax.random.normal(streams_of[10], (H, LEVELS), jnp.float32), 0.1, 1.9),
        "fork_block": set_ends(jax.random.randint(streams_of[11], (N_SEQ,), 0, NB), jax.random.fold_in(streams_of[11], 1), 0, NB - 1).astype(jnp.int32),
    }


def level_coefficients(level_gain):
    level_index = jnp.arange(LEVELS, dtype=jnp.int32)
    spans = 2.0 ** jnp.maximum(level_index - 1, 0).astype(jnp.float32)
    return level_gain / jnp.sqrt(float(DH * BLK) * spans)[None, :]

def fenwick_step(coefficients, levels, scan_input):
    block_index, queries, key_rows, value_rows = scan_input
    bit_range = jnp.arange(LEVELS - 1, dtype=jnp.int32)
    present = (block_index >> bit_range & 1).astype(jnp.float32)
    attention_probabilities = coefficients[:, 1:] * present[None, :]
    combined = jnp.einsum('hl,lhde->hde', attention_probabilities, levels, precision=lax.Precision.HIGHEST).astype(jnp.bfloat16)
    causal = jnp.arange(BLK)[:, None] >= jnp.arange(BLK)[None, :]
    attention_logits = jnp.einsum('thd,shd->hts', queries.astype(jnp.float32), key_rows.astype(jnp.float32))
    attention_logits = jnp.where(causal[None], attention_logits, 0.0) * coefficients[:, 0][:, None, None]
    inside_weights = lax.optimization_barrier(attention_logits.astype(jnp.bfloat16))
    inside = jnp.einsum('hts,she->the', inside_weights.astype(jnp.float32), value_rows.astype(jnp.float32))
    across = jnp.einsum('thd,hde->the', queries.astype(jnp.float32), combined.astype(jnp.float32))
    block_state = jnp.einsum('thd,the->hde', key_rows.astype(jnp.float32), value_rows.astype(jnp.float32))
    following = block_index + 1
    low_masks = (2 << bit_range) - 1
    below = (block_index & low_masks == low_masks).astype(jnp.float32)
    newest = following & low_masks == 1 << bit_range
    merged = block_state + jnp.einsum('l,lhde->hde', below, levels, precision=lax.Precision.HIGHEST)
    kept = levels * (1.0 - below)[:, None, None, None]
    levels = jnp.where(newest[:, None, None, None], merged[None], kept)
    return (levels, (inside + across, combined))

def window_attend(queries, key_rows, value_rows, offset, first_valid):
    row_count, head_count, head_width = queries.shape
    kv_groups = key_rows.shape[1]
    block_rows = min(512, row_count)
    logit_scale_factor = 1.0 / math.sqrt(head_width)

    def one_block(start_row):
        query_tile_rows = lax.dynamic_slice_in_dim(queries, start_row, block_rows, 0)
        query_tile_rows = query_tile_rows.reshape(block_rows, kv_groups, head_count // kv_groups, head_width)
        key_start = start_row + offset - WIN
        key_tile_rows = lax.dynamic_slice_in_dim(key_rows, key_start, block_rows + WIN, 0)
        value_tile_rows = lax.dynamic_slice_in_dim(value_rows, key_start, block_rows + WIN, 0)
        query_place = start_row + offset + jnp.arange(block_rows, dtype=jnp.int32)
        key_place = key_start + jnp.arange(block_rows + WIN, dtype=jnp.int32)
        allowed = (key_place[None, :] <= query_place[:, None]) & (key_place[None, :] > query_place[:, None] - WIN)
        allowed = allowed & (key_place[None, :] >= first_valid)
        attention_logits = jnp.einsum('nfjx,afx->fjna', query_tile_rows.astype(jnp.float32), key_tile_rows.astype(jnp.float32)) * logit_scale_factor
        attention_logits = jnp.where(allowed[None, None], attention_logits, -1e+30)
        row_max = lax.optimization_barrier(jnp.max(attention_logits, axis=-1, keepdims=True))
        exponent = jnp.exp(attention_logits - row_max)
        row_total = lax.optimization_barrier(jnp.sum(exponent, axis=-1, keepdims=True))
        attention_probabilities = lax.optimization_barrier((exponent / row_total).astype(jnp.bfloat16))
        attended_output = jnp.einsum('yzqa,ayh->qyzh', attention_probabilities.astype(jnp.float32), value_tile_rows.astype(jnp.float32))
        return attended_output.reshape(block_rows, head_count, head_width)
    starts = jnp.arange(row_count // block_rows, dtype=jnp.int32) * block_rows
    return lax.map(one_block, starts).reshape(row_count, head_count, head_width)

def head_norm(output):
    mean_square = lax.optimization_barrier(jnp.mean(output * output, axis=(1, 2), keepdims=True))
    return (output * lax.rsqrt(mean_square + 1e-06)).astype(jnp.bfloat16)

def reference(trunk_query, trunk_key, trunk_value, trunk_wquery, trunk_wkey, trunk_wvalue, branch_query, branch_wquery, branch_wkey, branch_wvalue, level_gain, fork_block):
    coefficients = level_coefficients(level_gain)
    block_total = TRUNK // BLK
    block_shape = (block_total, BLK, H, DH)
    scan_inputs = (jnp.arange(block_total, dtype=jnp.int32), trunk_query.reshape(block_shape), trunk_key.reshape(block_shape), trunk_value.reshape(block_shape))
    empty_levels = jnp.zeros((LEVELS - 1, H, DH, DH), jnp.float32)
    final_levels, (linear_out, mixed) = lax.scan(partial(fenwick_step, coefficients), empty_levels, scan_inputs)
    trunk_linear = linear_out.reshape(TRUNK, H, DH)
    padded_keys = jnp.concatenate([jnp.zeros((WIN, KVH, DH), jnp.bfloat16), trunk_wkey], axis=0)
    padded_values = jnp.concatenate([jnp.zeros((WIN, KVH, DH), jnp.bfloat16), trunk_wvalue], axis=0)
    trunk_window = window_attend(trunk_wquery, padded_keys, padded_values, WIN, WIN)
    trunk_out = head_norm(trunk_linear + trunk_window)
    last_start = (N_SEQ - 1) * NB

    def one_branch(branch_input):
        fork_index, queries, window_queries, window_keys, window_values = branch_input
        end_state = lax.dynamic_index_in_dim(mixed, last_start + fork_index, 0, keepdims=False)
        linear = jnp.einsum('thd,hde->the', queries.astype(jnp.float32), end_state.astype(jnp.float32))
        context_start = ((N_SEQ - 1) * TOK_DEV + fork_index * BLK - WIN).astype(jnp.int32)
        context_keys = lax.dynamic_slice_in_dim(trunk_wkey, context_start, WIN, 0)
        context_values = lax.dynamic_slice_in_dim(trunk_wvalue, context_start, WIN, 0)
        all_keys = jnp.concatenate([context_keys, window_keys], axis=0)
        all_values = jnp.concatenate([context_values, window_values], axis=0)
        window = window_attend(window_queries, all_keys, all_values, WIN, 0)
        return head_norm(linear + window)
    branch_inputs = (fork_block, branch_query.reshape(N_SEQ, BR_DEV, H, DH), branch_wquery.reshape(N_SEQ, BR_DEV, H, DH), branch_wkey.reshape(N_SEQ, BR_DEV, KVH, DH), branch_wvalue.reshape(N_SEQ, BR_DEV, KVH, DH))
    branch_out = lax.map(one_branch, branch_inputs).reshape(BRANCH, H, DH)
    return (trunk_out, branch_out)
```

```python
import functools
import math

import jax
import jax.numpy as jnp
from jax import lax
from jax.experimental import pallas as pl
from jax.experimental.pallas import tpu as pltpu
from jax.sharding import PartitionSpec as P

BLK = 128
WIN = 512
COLS = 4
MASKED = -1e30
F32 = jnp.float32
BF16 = jnp.bfloat16
VMEM_BYTES = 48 * 1024 * 1024


def params():
    return pltpu.CompilerParams(vmem_limit_bytes=VMEM_BYTES)


def smem():
    return pl.BlockSpec(memory_space=pltpu.SMEM)


def gain_factor(level, width):
    return 1.0 / math.sqrt(width * BLK * 2 ** max(level - 1, 0))


def every(rows_ref, wide, count, each):
    return wide[pl.ds(each, rows_ref.shape[0] // count, stride=count), :].astype(BF16)


def state_kernel(depth, heads, gain_ref, k_ref, v_ref, *rest):
    piece_refs, sum_ref, kf, vf, levels = rest[:COLS], rest[COLS], *rest[COLS + 1 :]
    block = pl.program_id(0)
    width = k_ref.shape[1]

    @pl.when(block == 0)
    def _():
        levels[...] = jnp.zeros_like(levels)

    kf[...] = k_ref[...].astype(F32)
    vf[...] = v_ref[...].astype(F32)
    per_piece = heads // COLS
    for h in range(heads):
        k = every(k_ref, kf, heads, h)
        v = every(v_ref, vf, heads, h)
        state = lax.dot_general(k, v, (((0,), (0,)), ((), ())), preferred_element_type=F32)
        before = jnp.zeros_like(state)
        merged = state
        for bit in range(depth):
            held = levels[bit, h]
            present = (block >> bit) & 1
            before = before + held * (present.astype(F32) * gain_ref[h, bit + 1] * gain_factor(bit + 1, width))
            low = (2 << bit) - 1
            merged = merged + held * ((block & low) == low).astype(F32)
        for bit in range(depth):
            low = (2 << bit) - 1
            newest = ((block + 1) & low) == (1 << bit)
            levels[bit, h] = jnp.where(newest, merged, levels[bit, h])
        piece_refs[h // per_piece][0, h % per_piece] = before.astype(BF16)
        sum_ref[h] = merged.astype(BF16)


def block_sums(gain, keys, values, heads, depth):
    blocks = 1 << depth
    rows, width = keys.shape[0] // blocks, keys.shape[1]
    piece = jax.ShapeDtypeStruct((blocks - 1, heads // COLS, width, width), BF16)
    at_block = pl.BlockSpec((rows, width), lambda b: (b, 0))
    return pl.pallas_call(
        functools.partial(state_kernel, depth, heads),
        grid=(blocks,),
        in_specs=[smem(), at_block, at_block],
        out_specs=[
            pl.BlockSpec((1, heads // COLS, width, width), lambda b: (jnp.maximum(b - 1, 0), 0, 0, 0))
        ]
        * COLS
        + [pl.BlockSpec((heads, width, width), lambda b: (0, 0, 0))],
        out_shape=[piece] * COLS + [jax.ShapeDtypeStruct((heads, width, width), BF16)],
        scratch_shapes=[
            pltpu.VMEM((rows, width), F32),
            pltpu.VMEM((rows, width), F32),
            pltpu.VMEM((depth, heads, width, width), F32),
        ],
        compiler_params=params(),
        cost_estimate=pl.CostEstimate(
            flops=2 * keys.size * width, bytes_accessed=4 * keys.size + 2 * heads * width * width * blocks, transcendentals=0
        ),
        name="block_sums",
    )(gain, keys, values)


def cross_kernel(count, depth, width, where_ref, gain_ref, sums_ref, out_ref):
    bits = count.bit_length() - 1
    heads = gain_ref.shape[0]
    head = where_ref[0] * heads // count
    group = [sums_ref[s].astype(F32) for s in range(count)]
    total = [jnp.zeros_like(group[0]) for _ in range(count)]
    for bit in range(bits):
        level = depth + bit + 1
        weight = gain_ref[head, level] * gain_factor(level, width)
        scaled = [g * weight for g in group]
        for d in range(count):
            if d >> bit & 1:
                total[d] = total[d] + scaled[(d >> bit) ^ 1]
        group = [group[2 * i] + group[2 * i + 1] for i in range(len(group) // 2)]
    last = total[count - 1].astype(BF16)
    for d in range(count):
        out_ref[d, 0] = total[d].astype(BF16)
        out_ref[d, 1] = last


def cross_sums(where, gain, sums, depth, width):
    count, rows, lanes = sums.shape
    return pl.pallas_call(
        functools.partial(cross_kernel, count, depth, width),
        in_specs=[smem(), smem(), pl.BlockSpec(memory_space=pltpu.VMEM)],
        out_specs=pl.BlockSpec(memory_space=pltpu.VMEM),
        out_shape=jax.ShapeDtypeStruct((count, 2, rows, lanes), BF16),
        compiler_params=params(),
        cost_estimate=pl.CostEstimate(flops=20 * sums.size, bytes_accessed=6 * sums.size, transcendentals=0),
        name="cross_sums",
    )(where, gain, sums)


def place(src_ref, wide, dst, start, groups):
    tokens = src_ref.shape[0] // groups
    wide[...] = src_ref[...].astype(F32)
    for g in range(groups):
        part = wide[pl.ds(g, tokens, stride=groups), :].astype(BF16)
        dst[g, pl.ds(start, tokens), : src_ref.shape[1]] = part


def window_rows(queries, keys, values, bias=None):
    rows, width = queries.shape
    logits = lax.dot_general(queries, keys, (((1,), (1,)), ((), ())), preferred_element_type=F32)
    row = lax.broadcasted_iota(jnp.int32, (rows, rows), 0)
    col = lax.broadcasted_iota(jnp.int32, (rows, rows), 1)
    first = jnp.where(col > row, logits[:, :rows], MASKED)
    last = jnp.where(col <= row, logits[:, -rows:], MASKED)
    logits = jnp.concatenate([first, logits[:, rows:-rows], last], axis=1)
    if bias is not None:
        logits = logits + bias
    top = jnp.max(logits, axis=1, keepdims=True)
    weights = jnp.exp2((logits - top) * (math.log2(math.e) / math.sqrt(width))).astype(BF16)
    both = jnp.dot(weights, values, preferred_element_type=F32)
    return both[:, :width] / both[:, width:]


def square_sums(total):
    ones = jnp.ones((8, total.shape[1]), F32)
    return lax.dot_general(
        ones, total, (((1,), (1,)), ((), ())), precision=lax.Precision.HIGHEST, preferred_element_type=F32
    )


def far_kernel(heads, groups, q_ref, pk_ref, pv_ref, ck_ref, cv_ref, out_ref, qf, kf, kh, vh, of):
    step = pl.program_id(0)
    width = q_ref.shape[1]

    @pl.when(step == 0)
    def _():
        vh[:, :, width:] = jnp.ones((groups, vh.shape[1], width), BF16)
        place(pk_ref, kf, kh, 0, groups)
        place(ck_ref, kf, kh, WIN, groups)
        place(pv_ref, kf, vh, 0, groups)
        place(cv_ref, kf, vh, WIN, groups)

    qf[...] = q_ref[...].astype(F32)
    base = pl.multiple_of(step * BLK, BLK)
    for h in range(heads):
        g = h * groups // heads
        out = window_rows(
            every(q_ref, qf, heads, h), kh[g, pl.ds(base, WIN + BLK), :], vh[g, pl.ds(base, WIN + BLK), :]
        )
        of[pl.ds(h, BLK, stride=heads), :] = out
    out_ref[...] = of[...]


def attention_cost(tokens, heads, width, extra=0):
    span = WIN + BLK
    return pl.CostEstimate(
        flops=6 * tokens * heads * span * width + extra,
        bytes_accessed=12 * tokens * heads * width,
        transcendentals=tokens * heads * span,
    )


def far_attention(queries, keys, values, heads, groups):
    width = queries.shape[1]
    steps = queries.shape[0] // (BLK * heads) - WIN // BLK
    skip = WIN // BLK
    at_first = pl.BlockSpec((WIN * groups, width), lambda i: (0, 0))
    at_next = pl.BlockSpec((WIN * groups, width), lambda i: (1, 0))
    return pl.pallas_call(
        functools.partial(far_kernel, heads, groups),
        grid=(steps,),
        in_specs=[
            pl.BlockSpec((BLK * heads, width), lambda i: (i + skip, 0)),
            at_first,
            at_first,
            at_next,
            at_next,
        ],
        out_specs=pl.BlockSpec((BLK * heads, width), lambda i: (i, 0)),
        out_shape=jax.ShapeDtypeStruct((steps * BLK * heads, width), F32),
        scratch_shapes=[
            pltpu.VMEM((BLK * heads, width), F32),
            pltpu.VMEM((WIN * groups, width), F32),
            pltpu.VMEM((groups, 2 * WIN, width), BF16),
            pltpu.VMEM((groups, 2 * WIN, 2 * width), BF16),
            pltpu.VMEM((BLK * heads, width), F32),
        ],
        compiler_params=params(),
        cost_estimate=attention_cost(steps * BLK, heads, width),
        name="far_attention",
    )(queries, keys, values, keys, values)


def trunk_kernel(heads, groups, where_ref, gain_ref, q_ref, k_ref, v_ref, wq_ref, pk_ref, pv_ref, ck_ref, cv_ref, cross_ref, *rest):
    piece_refs, out_ref, square_ref = rest[:COLS], rest[COLS], rest[COLS + 1]
    qf, nf, tf, sf, kf, kh, vh, of, cs = rest[COLS + 2 :]
    step = pl.program_id(0)
    width = q_ref.shape[1]

    @pl.when(step == 0)
    def _():
        vh[:, :, width:] = jnp.ones((groups, vh.shape[1], width), BF16)
        place(pk_ref, kf, kh, 0, groups)
        place(ck_ref, kf, kh, WIN, groups)
        place(pv_ref, kf, vh, 0, groups)
        place(cv_ref, kf, vh, WIN, groups)
        cs[...] = cross_ref[:, 0].reshape(heads, width, width)

    qf[...] = wq_ref[...].astype(F32)
    nf[...] = q_ref[...].astype(F32)
    tf[...] = k_ref[...].astype(F32)
    sf[...] = v_ref[...].astype(F32)
    base = pl.multiple_of(step * BLK, BLK)
    span = WIN + BLK
    reach = jnp.where(where_ref[0] == 0, WIN - step * BLK, 0)
    bias = jnp.where(lax.broadcasted_iota(jnp.int32, (1, span), 1) < reach, MASKED, 0.0).astype(F32)
    row = lax.broadcasted_iota(jnp.int32, (BLK, BLK), 0)
    col = lax.broadcasted_iota(jnp.int32, (BLK, BLK), 1)
    inner = (step > 0).astype(F32).astype(BF16)
    total = jnp.zeros((BLK, width), F32)
    per_piece = heads // COLS
    for h in range(heads):
        g = h * groups // heads
        out = window_rows(
            every(wq_ref, qf, heads, h), kh[g, pl.ds(base, span), :], vh[g, pl.ds(base, span), :], bias
        )
        q = every(q_ref, nf, heads, h)
        k = every(k_ref, tf, heads, h)
        v = every(v_ref, sf, heads, h)
        inside = lax.dot_general(q, k, (((1,), (1,)), ((), ())), preferred_element_type=F32)
        inside = jnp.where(col <= row, inside, 0.0) * (gain_ref[h, 0] * gain_factor(0, width))
        left = jnp.concatenate([inside.astype(BF16), q, q], axis=1)
        right = jnp.concatenate([v, cs[h], piece_refs[h // per_piece][0, h % per_piece] * inner], axis=0)
        out = out + jnp.dot(left, right, preferred_element_type=F32)
        total = total + out * out
        of[pl.ds(h, BLK, stride=heads), :] = out
    out_ref[...] = of[...]
    square_ref[0] = square_sums(total)


def trunk_attention(where, gain, q, k, v, wq, pk, pv, ck, cv, cross, pieces, heads, groups):
    width = q.shape[1]
    blocks = q.shape[0] // (BLK * heads)
    at_block = pl.BlockSpec((BLK * heads, width), lambda i: (i, 0))
    whole = pl.BlockSpec((WIN * groups, width), lambda i: (0, 0))
    own = pl.BlockSpec((cross.shape[0], 1, *cross.shape[2:]), lambda i: (0, 0, 0, 0))
    piece = pl.BlockSpec((1, heads // COLS, width, width), lambda i: (jnp.maximum(i - 1, 0), 0, 0, 0))
    wide = pltpu.VMEM((BLK * heads, width), F32)
    return pl.pallas_call(
        functools.partial(trunk_kernel, heads, groups),
        grid=(blocks,),
        in_specs=[smem(), smem()] + [at_block] * 4 + [whole] * 4 + [own] + [piece] * COLS,
        out_specs=[at_block, pl.BlockSpec((1, 8, BLK), lambda i: (i, 0, 0))],
        out_shape=[
            jax.ShapeDtypeStruct(q.shape, F32),
            jax.ShapeDtypeStruct((blocks, 8, BLK), F32),
        ],
        scratch_shapes=[
            wide,
            wide,
            wide,
            wide,
            pltpu.VMEM((WIN * groups, width), F32),
            pltpu.VMEM((groups, 2 * WIN, width), BF16),
            pltpu.VMEM((groups, 2 * WIN, 2 * width), BF16),
            wide,
            pltpu.VMEM((heads, width, width), BF16),
        ],
        compiler_params=params(),
        cost_estimate=attention_cost(blocks * BLK, heads, width, 2 * blocks * BLK * BLK * heads * 4 * width),
        name="trunk_attention",
    )(where, gain, q, k, v, wq, pk, pv, ck, cv, cross, *pieces)


def branch_kernel(heads, groups, where_ref, fork_ref, q_ref, wq_ref, far_ref, ck_ref, cv_ref, cross_ref, *rest):
    kv_refs, piece_refs = rest[:COLS], rest[COLS : 2 * COLS]
    out_ref, square_ref = rest[2 * COLS : 2 * COLS + 2]
    qf, nf, kf, kh, vh, kt, of, es = rest[2 * COLS + 2 :]
    step = pl.program_id(0)
    near = WIN // BLK
    width = q_ref.shape[1]
    fork = fork_ref[0]
    column = where_ref[0] & (COLS - 1)
    span = WIN + BLK
    start = pl.multiple_of(fork * BLK, BLK)

    @pl.when(step == 0)
    def _():
        for i in range(COLS):
            kt[column ^ i] = kv_refs[i][...]
        vh[:, :, width:] = jnp.ones((groups, vh.shape[1], width), BF16)
        place(kt.at[0], kf, vh, 0, groups)
        place(kt.at[1], kf, vh, WIN, groups)
        place(kt.at[2], kf, kh, 0, groups)
        place(kt.at[3], kf, kh, WIN, groups)
        place(ck_ref, kf, kh, pl.multiple_of(start + WIN, BLK), groups)
        place(cv_ref, kf, vh, pl.multiple_of(start + WIN, BLK), groups)
        es[:, :width, :] = cross_ref[:, 0].reshape(heads, width, width)
        inner = (fork > 0).astype(F32).astype(BF16)
        chosen = jnp.maximum(fork - 1, 0)
        per_piece = heads // COLS
        for i in range(COLS):
            mine = (column ^ i) * per_piece
            for j in range(per_piece):
                es[mine + j, width:, :] = piece_refs[i][chosen, j] * inner

    nf[...] = q_ref[...].astype(F32)

    @pl.when(step < near)
    def _():
        qf[...] = wq_ref[...].astype(F32)
        base = pl.multiple_of(start + step * BLK, BLK)
        for h in range(heads):
            g = h * groups // heads
            of[pl.ds(h, BLK, stride=heads), :] = window_rows(
                every(wq_ref, qf, heads, h), kh[g, pl.ds(base, span), :], vh[g, pl.ds(base, span), :]
            )

    @pl.when(step >= near)
    def _():
        of[...] = far_ref[...]

    total = jnp.zeros((BLK, width), F32)
    for h in range(heads):
        q = every(q_ref, nf, heads, h)
        at = pl.ds(h, BLK, stride=heads)
        out = of[at, :] + jnp.dot(jnp.concatenate([q, q], axis=1), es[h], preferred_element_type=F32)
        total = total + out * out
        of[at, :] = out
    out_ref[...] = of[...]
    square_ref[0] = square_sums(total)


def branch_attention(where, fork, q, wq, far, ck, cv, cross, kvs, pieces, heads, groups):
    width = q.shape[1]
    blocks = q.shape[0] // (BLK * heads)
    near = WIN // BLK
    at_block = pl.BlockSpec((BLK * heads, width), lambda i: (i, 0))
    at_near = pl.BlockSpec((BLK * heads, width), lambda i: (jnp.minimum(i, near - 1), 0))
    at_far = pl.BlockSpec((BLK * heads, width), lambda i: (jnp.maximum(i - near, 0), 0))
    whole = pl.BlockSpec((WIN * groups, width), lambda i: (0, 0))
    end = pl.BlockSpec((cross.shape[0], 1, *cross.shape[2:]), lambda i: (0, 1, 0, 0))
    piece = pl.BlockSpec(pieces[0].shape, lambda i: (0, 0, 0, 0))
    wide = pltpu.VMEM((BLK * heads, width), F32)
    return pl.pallas_call(
        functools.partial(branch_kernel, heads, groups),
        grid=(blocks,),
        in_specs=[smem(), smem(), at_block, at_near, at_far, whole, whole, end] + [whole] * COLS + [piece] * COLS,
        out_specs=[at_block, pl.BlockSpec((1, 8, BLK), lambda i: (i, 0, 0))],
        out_shape=[
            jax.ShapeDtypeStruct(q.shape, F32),
            jax.ShapeDtypeStruct((blocks, 8, BLK), F32),
        ],
        scratch_shapes=[
            wide,
            wide,
            pltpu.VMEM((WIN * groups, width), F32),
            pltpu.VMEM((groups, 3 * WIN, width), BF16),
            pltpu.VMEM((groups, 3 * WIN, 2 * width), BF16),
            pltpu.VMEM((COLS, WIN * groups, width), BF16),
            wide,
            pltpu.VMEM((heads, 2 * width, width), BF16),
        ],
        compiler_params=params(),
        cost_estimate=attention_cost(near * BLK, heads, width, 4 * blocks * BLK * heads * width * width),
        name="branch_attention",
    )(where, fork, q, wq, far, ck, cv, cross, *kvs, *pieces)


def norm_kernel(heads, features, full_ref, square_ref, out_ref):
    width = full_ref.shape[1]
    scale = lax.rsqrt(square_ref[0, 0:1, :] / features + 1e-06)
    scale = jnp.broadcast_to(scale, (width, BLK)).T
    full = full_ref[...].reshape(BLK, heads, width)
    out_ref[...] = (full * scale[:, None, :]).astype(BF16).reshape(BLK * heads, width)


def normalize(full, squares, heads, features, name):
    width = full.shape[1]
    blocks = full.shape[0] // (BLK * heads)
    at_block = pl.BlockSpec((BLK * heads, width), lambda i: (i, 0))
    return pl.pallas_call(
        functools.partial(norm_kernel, heads, features),
        grid=(blocks,),
        in_specs=[at_block, pl.BlockSpec((1, 8, BLK), lambda i: (i, 0, 0))],
        out_specs=at_block,
        out_shape=jax.ShapeDtypeStruct(full.shape, BF16),
        compiler_params=params(),
        cost_estimate=pl.CostEstimate(flops=2 * full.size, bytes_accessed=6 * full.size, transcendentals=0),
        name=name,
    )(full, squares)


def shards(
    trunk_query,
    trunk_key,
    trunk_value,
    trunk_wquery,
    trunk_wkey,
    trunk_wvalue,
    branch_query,
    branch_wquery,
    branch_wkey,
    branch_wvalue,
    level_gain,
    fork_block,
):
    tokens, heads, width = trunk_query.shape
    groups = trunk_wkey.shape[1]
    depth = (tokens // BLK).bit_length() - 1
    count = lax.axis_size("seq")
    planes = count // COLS
    features = heads * lax.axis_size("head") * width
    me = lax.axis_index("seq")
    column, plane = me % COLS, me // COLS
    where = me.astype(jnp.int32).reshape(1)
    root = count - 1
    top = planes - 1

    def flat(x):
        return x.reshape(x.shape[0] * x.shape[1], x.shape[2])

    tq, tk, tv, twq = flat(trunk_query), flat(trunk_key), flat(trunk_value), flat(trunk_wquery)
    twk, twv = flat(trunk_wkey), flat(trunk_wvalue)
    bq, bwq, bwk, bwv = flat(branch_query), flat(branch_wquery), flat(branch_wkey), flat(branch_wvalue)

    def send(x, pairs):
        return lax.ppermute(x, "seq", pairs)

    def down(x):
        step = planes // 2
        while step:
            starts = [p for p in range(planes) if (top - p) % (2 * step) == 0 and p >= step]
            pairs = [(p * COLS + c, (p - step) * COLS + c) for p in starts for c in range(COLS)]
            got = send(x, pairs)
            hit = functools.reduce(jnp.logical_or, [plane == p - step for p in starts])
            x = jnp.where(hit, got, x)
            step //= 2
        return x

    def around(x):
        return [x] + [send(x, [(i, i ^ d) for i in range(count)]) for d in range(1, COLS)]

    half = COLS // 2
    got = send(twv, [(root - i, root - i - half) for i in range(half)])
    kvs = around(down(jnp.where(column >= half, twk, got)))
    shift = [(i, i + 1) for i in range(count - 1)]
    pk, pv = send(twk, shift), send(twv, shift)

    *pieces, shard_sum = block_sums(level_gain, tk, tv, heads, depth)
    chosen = pieces[COLS - 1]
    for c in range(COLS - 1):
        got = send(pieces[c], [(root, root - (COLS - 1) + c)])
        chosen = jnp.where(column == c, got, chosen)
    ends = around(down(chosen))

    slices = shard_sum.reshape(count, heads * width // count, width)
    slices = lax.all_to_all(slices, "seq", 0, 0, tiled=True)
    cross = cross_sums(where, level_gain, slices, depth, width)
    cross = lax.all_to_all(cross, "seq", 0, 0, tiled=True)

    far = far_attention(bwq, bwk, bwv, heads, groups)
    trunk_full, trunk_square = trunk_attention(
        where, level_gain, tq, tk, tv, twq, pk, pv, twk, twv, cross, pieces, heads, groups
    )
    trunk_square = lax.psum(trunk_square, "head")
    trunk_out = normalize(trunk_full, trunk_square, heads, features, "trunk_norm")
    branch_full, branch_square = branch_attention(
        where, fork_block, bq, bwq, far, bwk, bwv, cross, kvs, ends, heads, groups
    )
    branch_square = lax.psum(branch_square, "head")
    branch_out = normalize(branch_full, branch_square, heads, features, "branch_norm")
    return trunk_out.reshape(trunk_query.shape), branch_out.reshape(branch_query.shape)


def solution(mesh):
    rows = P("seq", "head", None)
    return jax.shard_map(
        shards,
        mesh=mesh,
        in_specs=(rows,) * 10 + (P("head", None), P("seq")),
        out_specs=(rows, rows),
        check_vma=False,
    )
```

```python
import functools
import math

import jax
import jax.numpy as jnp
from jax import lax
from jax.experimental import pallas as pl
from jax.experimental.pallas import tpu as pltpu
from jax.sharding import PartitionSpec as P

BLK = 128
WIN = 512
COLS = 4
MASKED = -1e30
F32 = jnp.float32
BF16 = jnp.bfloat16
VMEM_BYTES = 60 * 1024 * 1024


def params():
    return pltpu.CompilerParams(vmem_limit_bytes=VMEM_BYTES)


def smem():
    return pl.BlockSpec(memory_space=pltpu.SMEM)


def gain_factor(level, width):
    return 1.0 / math.sqrt(width * BLK * 2 ** max(level - 1, 0))


def every(rows_ref, wide, count, each):
    return wide[pl.ds(each, rows_ref.shape[0] // count, stride=count), :].astype(BF16)


def state_kernel(depth, heads, gain_ref, k_ref, v_ref, *rest):
    piece_refs, sum_ref, kf, vf, levels = rest[:COLS], rest[COLS], *rest[COLS + 1 :]
    block = pl.program_id(0)
    width = k_ref.shape[1]

    @pl.when(block == 0)
    def _():
        levels[...] = jnp.zeros_like(levels)

    kf[...] = k_ref[...].astype(F32)
    vf[...] = v_ref[...].astype(F32)
    per_piece = heads // COLS
    for h in range(heads):
        k = every(k_ref, kf, heads, h)
        v = every(v_ref, vf, heads, h)
        state = lax.dot_general(k, v, (((0,), (0,)), ((), ())), preferred_element_type=F32)
        before = jnp.zeros_like(state)
        merged = state
        for bit in range(depth):
            held = levels[bit, h]
            present = (block >> bit) & 1
            before = before + held * (present.astype(F32) * gain_ref[h, bit + 1] * gain_factor(bit + 1, width))
            low = (2 << bit) - 1
            merged = merged + held * ((block & low) == low).astype(F32)
        for bit in range(depth):
            low = (2 << bit) - 1
            newest = ((block + 1) & low) == (1 << bit)
            levels[bit, h] = jnp.where(newest, merged, levels[bit, h])
        piece_refs[h // per_piece][0, h % per_piece] = before.astype(BF16)
        sum_ref[h] = merged.astype(BF16)


def block_sums(gain, keys, values, heads, depth):
    blocks = 1 << depth
    rows, width = keys.shape[0] // blocks, keys.shape[1]
    piece = jax.ShapeDtypeStruct((blocks - 1, heads // COLS, width, width), BF16)
    at_block = pl.BlockSpec((rows, width), lambda b: (b, 0))
    return pl.pallas_call(
        functools.partial(state_kernel, depth, heads),
        grid=(blocks,),
        in_specs=[smem(), at_block, at_block],
        out_specs=[
            pl.BlockSpec((1, heads // COLS, width, width), lambda b: (jnp.maximum(b - 1, 0), 0, 0, 0))
        ]
        * COLS
        + [pl.BlockSpec((heads, width, width), lambda b: (0, 0, 0))],
        out_shape=[piece] * COLS + [jax.ShapeDtypeStruct((heads, width, width), BF16)],
        scratch_shapes=[
            pltpu.VMEM((rows, width), F32),
            pltpu.VMEM((rows, width), F32),
            pltpu.VMEM((depth, heads, width, width), F32),
        ],
        compiler_params=params(),
        cost_estimate=pl.CostEstimate(
            flops=2 * keys.size * width, bytes_accessed=4 * keys.size + 2 * heads * width * width * blocks, transcendentals=0
        ),
        name="block_sums",
    )(gain, keys, values)


def cross_kernel(count, depth, width, where_ref, gain_ref, sums_ref, out_ref):
    bits = count.bit_length() - 1
    heads = gain_ref.shape[0]
    head = where_ref[0] * heads // count
    group = [sums_ref[s].astype(F32) for s in range(count)]
    total = [jnp.zeros_like(group[0]) for _ in range(count)]
    for bit in range(bits):
        level = depth + bit + 1
        weight = gain_ref[head, level] * gain_factor(level, width)
        scaled = [g * weight for g in group]
        for d in range(count):
            if d >> bit & 1:
                total[d] = total[d] + scaled[(d >> bit) ^ 1]
        group = [group[2 * i] + group[2 * i + 1] for i in range(len(group) // 2)]
    last = total[count - 1].astype(BF16)
    for d in range(count):
        out_ref[d, 0] = total[d].astype(BF16)
        out_ref[d, 1] = last


def cross_sums(where, gain, sums, depth, width):
    count, rows, lanes = sums.shape
    return pl.pallas_call(
        functools.partial(cross_kernel, count, depth, width),
        in_specs=[smem(), smem(), pl.BlockSpec(memory_space=pltpu.VMEM)],
        out_specs=pl.BlockSpec(memory_space=pltpu.VMEM),
        out_shape=jax.ShapeDtypeStruct((count, 2, rows, lanes), BF16),
        compiler_params=params(),
        cost_estimate=pl.CostEstimate(flops=20 * sums.size, bytes_accessed=6 * sums.size, transcendentals=0),
        name="cross_sums",
    )(where, gain, sums)


def place(src_ref, wide, dst, start, groups):
    tokens = src_ref.shape[0] // groups
    wide[...] = src_ref[...].astype(F32)
    for g in range(groups):
        part = wide[pl.ds(g, tokens, stride=groups), :].astype(BF16)
        dst[g, pl.ds(start, tokens), : src_ref.shape[1]] = part


def split_groups(wide):
    rows, width = wide.shape
    pairs = wide.reshape(rows // 16, 16, width)
    low, high = pairs[:, :8], pairs[:, 8:]
    upper = lax.broadcasted_iota(jnp.int32, low.shape, 1) < 4
    first = jnp.where(upper, low, pltpu.roll(high, 4, 1))
    second = jnp.where(upper, pltpu.roll(low, 4, 1), high)
    return [part.reshape(rows // 2, width) for part in (first, second)]


def join_groups(first, second):
    rows, width = first.shape
    first, second = (part.reshape(rows // 8, 8, width) for part in (first, second))
    upper = lax.broadcasted_iota(jnp.int32, first.shape, 1) < 4
    low = jnp.where(upper, first, pltpu.roll(second, 4, 1))
    high = jnp.where(upper, pltpu.roll(first, 4, 1), second)
    return jnp.concatenate([low, high], axis=1).reshape(2 * rows, width)


def window_logits(queries, keys, token, share, bias):
    rows = queries.shape[0]
    logits = lax.dot_general(queries, keys, (((1,), (1,)), ((), ())), preferred_element_type=F32)
    row = token + lax.broadcasted_iota(jnp.int32, (rows, BLK), 0) // share
    col = lax.broadcasted_iota(jnp.int32, (rows, BLK), 1)
    late = col > row
    first = jnp.where(late, logits[:, :BLK], MASKED)
    last = jnp.where(late, MASKED, logits[:, -BLK:])
    logits = jnp.concatenate([first, logits[:, BLK:-BLK], last], axis=1)
    return logits if bias is None else logits + bias


def window_outputs(logits, values, width):
    top = jnp.max(logits, axis=1, keepdims=True)
    weights = jnp.exp2((logits - top) * (math.log2(math.e) / math.sqrt(width))).astype(BF16)
    both = jnp.dot(weights, values, preferred_element_type=F32)
    return both[:, :width] / both[:, width:]


def window_block(q_ref, kh, vh, base, groups, bias=None):
    width = q_ref.shape[1]
    span = WIN + BLK
    share = q_ref.shape[0] // BLK // groups
    parts = [part.astype(BF16) for part in split_groups(q_ref[...].astype(F32))]
    chunks = [(g, c) for g in range(groups) for c in range(0, BLK * share, BLK)]

    def logits_of(chunk):
        g, c = chunk
        return window_logits(parts[g][c : c + BLK], kh[g, pl.ds(base, span), :], c // share, share, bias)

    outs = []
    ahead = logits_of(chunks[0])
    for i, (g, c) in enumerate(chunks):
        now = ahead
        if i + 1 < len(chunks):
            ahead = logits_of(chunks[i + 1])
        outs.append(window_outputs(now, vh[g, pl.ds(base, span), :], width))
    half = len(outs) // 2
    return join_groups(jnp.concatenate(outs[:half], axis=0), jnp.concatenate(outs[half:], axis=0))


def square_sums(full, heads):
    tokens = full.shape[0] // heads
    row = lax.broadcasted_iota(jnp.int32, (tokens, full.shape[0]), 1) // heads
    mine = row == lax.broadcasted_iota(jnp.int32, (tokens, full.shape[0]), 0)
    sums = jnp.dot(mine.astype(BF16), (full * full).astype(BF16), preferred_element_type=F32)
    ones = jnp.ones((8, full.shape[1]), F32)
    return lax.dot_general(
        ones, sums, (((1,), (1,)), ((), ())), precision=lax.Precision.HIGHEST, preferred_element_type=F32
    )


def far_kernel(heads, groups, q_ref, pk_ref, pv_ref, ck_ref, cv_ref, out_ref, kf, kh, vh):
    step = pl.program_id(0)
    width = q_ref.shape[1]

    @pl.when(step == 0)
    def _():
        vh[:, :, width:] = jnp.ones((groups, vh.shape[1], width), BF16)
        place(pk_ref, kf, kh, 0, groups)
        place(ck_ref, kf, kh, WIN, groups)
        place(pv_ref, kf, vh, 0, groups)
        place(cv_ref, kf, vh, WIN, groups)

    out_ref[...] = window_block(q_ref, kh, vh, pl.multiple_of(step * BLK, BLK), groups)


def attention_cost(tokens, heads, width, extra=0):
    span = WIN + BLK
    return pl.CostEstimate(
        flops=6 * tokens * heads * span * width + extra,
        bytes_accessed=12 * tokens * heads * width,
        transcendentals=tokens * heads * span,
    )


def far_attention(queries, keys, values, heads, groups):
    width = queries.shape[1]
    steps = queries.shape[0] // (BLK * heads) - WIN // BLK
    skip = WIN // BLK
    at_first = pl.BlockSpec((WIN * groups, width), lambda i: (0, 0))
    at_next = pl.BlockSpec((WIN * groups, width), lambda i: (1, 0))
    return pl.pallas_call(
        functools.partial(far_kernel, heads, groups),
        grid=(steps,),
        in_specs=[
            pl.BlockSpec((BLK * heads, width), lambda i: (i + skip, 0)),
            at_first,
            at_first,
            at_next,
            at_next,
        ],
        out_specs=pl.BlockSpec((BLK * heads, width), lambda i: (i, 0)),
        out_shape=jax.ShapeDtypeStruct((steps * BLK * heads, width), F32),
        scratch_shapes=[
            pltpu.VMEM((WIN * groups, width), F32),
            pltpu.VMEM((groups, 2 * WIN, width), BF16),
            pltpu.VMEM((groups, 2 * WIN, 2 * width), BF16),
        ],
        compiler_params=params(),
        cost_estimate=attention_cost(steps * BLK, heads, width),
        name="far_attention",
    )(queries, keys, values, keys, values)


def trunk_kernel(heads, groups, where_ref, gain_ref, q_ref, k_ref, v_ref, wq_ref, pk_ref, pv_ref, ck_ref, cv_ref, cross_ref, *rest):
    piece_refs, out_ref, square_ref = rest[:COLS], rest[COLS], rest[COLS + 1]
    nf, tf, sf, kf, kh, vh, of, cs = rest[COLS + 2 :]
    step = pl.program_id(0)
    width = q_ref.shape[1]

    @pl.when(step == 0)
    def _():
        vh[:, :, width:] = jnp.ones((groups, vh.shape[1], width), BF16)
        place(pk_ref, kf, kh, 0, groups)
        place(ck_ref, kf, kh, WIN, groups)
        place(pv_ref, kf, vh, 0, groups)
        place(cv_ref, kf, vh, WIN, groups)
        cs[...] = cross_ref[:, 0].reshape(heads, width, width)

    nf[...] = q_ref[...].astype(F32)
    tf[...] = k_ref[...].astype(F32)
    sf[...] = v_ref[...].astype(F32)
    base = pl.multiple_of(step * BLK, BLK)
    span = WIN + BLK
    reach = jnp.where(where_ref[0] == 0, WIN - step * BLK, 0)
    bias = jnp.where(lax.broadcasted_iota(jnp.int32, (1, span), 1) < reach, MASKED, 0.0).astype(F32)
    row = lax.broadcasted_iota(jnp.int32, (BLK, BLK), 0)
    col = lax.broadcasted_iota(jnp.int32, (BLK, BLK), 1)
    inner = (step > 0).astype(F32).astype(BF16)
    per_piece = heads // COLS
    q = [every(q_ref, nf, heads, h) for h in range(heads)]
    inside = [
        lax.dot_general(q[h], every(k_ref, tf, heads, h), (((1,), (1,)), ((), ())), preferred_element_type=F32)
        for h in range(heads)
    ]
    for h in range(heads):
        weight = jnp.where(col <= row, inside[h], 0.0) * (gain_ref[h, 0] * gain_factor(0, width))
        left = jnp.concatenate([weight.astype(BF16), q[h], q[h]], axis=1)
        right = jnp.concatenate(
            [every(v_ref, sf, heads, h), cs[h], piece_refs[h // per_piece][0, h % per_piece] * inner], axis=0
        )
        of[pl.ds(h, BLK, stride=heads), :] = jnp.dot(left, right, preferred_element_type=F32)
    full = window_block(wq_ref, kh, vh, base, groups, bias) + of[...]
    out_ref[...] = full
    square_ref[0] = square_sums(full, heads)


def trunk_attention(where, gain, q, k, v, wq, pk, pv, ck, cv, cross, pieces, heads, groups):
    width = q.shape[1]
    blocks = q.shape[0] // (BLK * heads)
    at_block = pl.BlockSpec((BLK * heads, width), lambda i: (i, 0))
    whole = pl.BlockSpec((WIN * groups, width), lambda i: (0, 0))
    own = pl.BlockSpec((cross.shape[0], 1, *cross.shape[2:]), lambda i: (0, 0, 0, 0))
    piece = pl.BlockSpec((1, heads // COLS, width, width), lambda i: (jnp.maximum(i - 1, 0), 0, 0, 0))
    wide = pltpu.VMEM((BLK * heads, width), F32)
    return pl.pallas_call(
        functools.partial(trunk_kernel, heads, groups),
        grid=(blocks,),
        in_specs=[smem(), smem()] + [at_block] * 4 + [whole] * 4 + [own] + [piece] * COLS,
        out_specs=[at_block, pl.BlockSpec((1, 8, BLK), lambda i: (i, 0, 0))],
        out_shape=[
            jax.ShapeDtypeStruct(q.shape, F32),
            jax.ShapeDtypeStruct((blocks, 8, BLK), F32),
        ],
        scratch_shapes=[
            wide,
            wide,
            wide,
            pltpu.VMEM((WIN * groups, width), F32),
            pltpu.VMEM((groups, 2 * WIN, width), BF16),
            pltpu.VMEM((groups, 2 * WIN, 2 * width), BF16),
            wide,
            pltpu.VMEM((heads, width, width), BF16),
        ],
        compiler_params=params(),
        cost_estimate=attention_cost(blocks * BLK, heads, width, 2 * blocks * BLK * BLK * heads * 4 * width),
        name="trunk_attention",
    )(where, gain, q, k, v, wq, pk, pv, ck, cv, cross, *pieces)


def branch_kernel(heads, groups, where_ref, fork_ref, q_ref, wq_ref, far_ref, ck_ref, cv_ref, cross_ref, *rest):
    kv_refs, piece_refs = rest[:COLS], rest[COLS : 2 * COLS]
    out_ref, square_ref = rest[2 * COLS : 2 * COLS + 2]
    nf, kf, kh, vh, kt, of, es = rest[2 * COLS + 2 :]
    step = pl.program_id(0)
    near = WIN // BLK
    width = q_ref.shape[1]
    fork = fork_ref[0]
    column = where_ref[0] & (COLS - 1)
    start = pl.multiple_of(fork * BLK, BLK)

    @pl.when(step == 0)
    def _():
        for i in range(COLS):
            kt[column ^ i] = kv_refs[i][...]
        vh[:, :, width:] = jnp.ones((groups, vh.shape[1], width), BF16)
        place(kt.at[0], kf, vh, 0, groups)
        place(kt.at[1], kf, vh, WIN, groups)
        place(kt.at[2], kf, kh, 0, groups)
        place(kt.at[3], kf, kh, WIN, groups)
        place(ck_ref, kf, kh, pl.multiple_of(start + WIN, BLK), groups)
        place(cv_ref, kf, vh, pl.multiple_of(start + WIN, BLK), groups)
        es[:, :width, :] = cross_ref[:, 0].reshape(heads, width, width)
        inner = (fork > 0).astype(F32).astype(BF16)
        chosen = jnp.maximum(fork - 1, 0)
        per_piece = heads // COLS
        for i in range(COLS):
            mine = (column ^ i) * per_piece
            for j in range(per_piece):
                es[mine + j, width:, :] = piece_refs[i][chosen, j] * inner

    nf[...] = q_ref[...].astype(F32)
    for h in range(heads):
        q = every(q_ref, nf, heads, h)
        both = jnp.concatenate([q, q], axis=1)
        of[pl.ds(h, BLK, stride=heads), :] = jnp.dot(both, es[h], preferred_element_type=F32)

    @pl.when(step < near)
    def _():
        base = pl.multiple_of(start + step * BLK, BLK)
        full = window_block(wq_ref, kh, vh, base, groups) + of[...]
        out_ref[...] = full
        square_ref[0] = square_sums(full, heads)

    @pl.when(step >= near)
    def _():
        full = far_ref[...] + of[...]
        out_ref[...] = full
        square_ref[0] = square_sums(full, heads)


def branch_attention(where, fork, q, wq, far, ck, cv, cross, kvs, pieces, heads, groups):
    width = q.shape[1]
    blocks = q.shape[0] // (BLK * heads)
    near = WIN // BLK
    at_block = pl.BlockSpec((BLK * heads, width), lambda i: (i, 0))
    at_near = pl.BlockSpec((BLK * heads, width), lambda i: (jnp.minimum(i, near - 1), 0))
    at_far = pl.BlockSpec((BLK * heads, width), lambda i: (jnp.maximum(i - near, 0), 0))
    whole = pl.BlockSpec((WIN * groups, width), lambda i: (0, 0))
    end = pl.BlockSpec((cross.shape[0], 1, *cross.shape[2:]), lambda i: (0, 1, 0, 0))
    piece = pl.BlockSpec(pieces[0].shape, lambda i: (0, 0, 0, 0))
    wide = pltpu.VMEM((BLK * heads, width), F32)
    return pl.pallas_call(
        functools.partial(branch_kernel, heads, groups),
        grid=(blocks,),
        in_specs=[smem(), smem(), at_block, at_near, at_far, whole, whole, end] + [whole] * COLS + [piece] * COLS,
        out_specs=[at_block, pl.BlockSpec((1, 8, BLK), lambda i: (i, 0, 0))],
        out_shape=[
            jax.ShapeDtypeStruct(q.shape, F32),
            jax.ShapeDtypeStruct((blocks, 8, BLK), F32),
        ],
        scratch_shapes=[
            wide,
            pltpu.VMEM((WIN * groups, width), F32),
            pltpu.VMEM((groups, 3 * WIN, width), BF16),
            pltpu.VMEM((groups, 3 * WIN, 2 * width), BF16),
            pltpu.VMEM((COLS, WIN * groups, width), BF16),
            wide,
            pltpu.VMEM((heads, 2 * width, width), BF16),
        ],
        compiler_params=params(),
        cost_estimate=attention_cost(near * BLK, heads, width, 4 * blocks * BLK * heads * width * width),
        name="branch_attention",
    )(where, fork, q, wq, far, ck, cv, cross, *kvs, *pieces)


def norm_kernel(heads, features, full_ref, square_ref, out_ref):
    width = full_ref.shape[1]
    scale = lax.rsqrt(square_ref[0, 0:1, :] / features + 1e-06)
    scale = jnp.broadcast_to(scale, (width, BLK)).T
    full = full_ref[...].reshape(BLK, heads, width)
    out_ref[...] = (full * scale[:, None, :]).astype(BF16).reshape(BLK * heads, width)


def normalize(full, squares, heads, features, name):
    width = full.shape[1]
    blocks = full.shape[0] // (BLK * heads)
    at_block = pl.BlockSpec((BLK * heads, width), lambda i: (i, 0))
    return pl.pallas_call(
        functools.partial(norm_kernel, heads, features),
        grid=(blocks,),
        in_specs=[at_block, pl.BlockSpec((1, 8, BLK), lambda i: (i, 0, 0))],
        out_specs=at_block,
        out_shape=jax.ShapeDtypeStruct(full.shape, BF16),
        compiler_params=params(),
        cost_estimate=pl.CostEstimate(flops=2 * full.size, bytes_accessed=6 * full.size, transcendentals=0),
        name=name,
    )(full, squares)


def shards(
    trunk_query,
    trunk_key,
    trunk_value,
    trunk_wquery,
    trunk_wkey,
    trunk_wvalue,
    branch_query,
    branch_wquery,
    branch_wkey,
    branch_wvalue,
    level_gain,
    fork_block,
):
    tokens, heads, width = trunk_query.shape
    groups = trunk_wkey.shape[1]
    depth = (tokens // BLK).bit_length() - 1
    count = lax.axis_size("seq")
    planes = count // COLS
    features = heads * lax.axis_size("head") * width
    me = lax.axis_index("seq")
    column, plane = me % COLS, me // COLS
    where = me.astype(jnp.int32).reshape(1)
    root = count - 1
    top = planes - 1

    def flat(x):
        return x.reshape(x.shape[0] * x.shape[1], x.shape[2])

    tq, tk, tv, twq = flat(trunk_query), flat(trunk_key), flat(trunk_value), flat(trunk_wquery)
    twk, twv = flat(trunk_wkey), flat(trunk_wvalue)
    bq, bwq, bwk, bwv = flat(branch_query), flat(branch_wquery), flat(branch_wkey), flat(branch_wvalue)

    def send(x, pairs):
        return lax.ppermute(x, "seq", pairs)

    def down(x):
        step = planes // 2
        while step:
            starts = [p for p in range(planes) if (top - p) % (2 * step) == 0 and p >= step]
            pairs = [(p * COLS + c, (p - step) * COLS + c) for p in starts for c in range(COLS)]
            got = send(x, pairs)
            hit = functools.reduce(jnp.logical_or, [plane == p - step for p in starts])
            x = jnp.where(hit, got, x)
            step //= 2
        return x

    def around(x):
        return [x] + [send(x, [(i, i ^ d) for i in range(count)]) for d in range(1, COLS)]

    half = COLS // 2
    got = send(twv, [(root - i, root - i - half) for i in range(half)])
    kvs = around(down(jnp.where(column >= half, twk, got)))
    shift = [(i, i + 1) for i in range(count - 1)]
    pk, pv = send(twk, shift), send(twv, shift)

    *pieces, shard_sum = block_sums(level_gain, tk, tv, heads, depth)
    chosen = pieces[COLS - 1]
    for c in range(COLS - 1):
        got = send(pieces[c], [(root, root - (COLS - 1) + c)])
        chosen = jnp.where(column == c, got, chosen)
    ends = around(down(chosen))

    slices = shard_sum.reshape(count, heads * width // count, width)
    slices = lax.all_to_all(slices, "seq", 0, 0, tiled=True)
    cross = cross_sums(where, level_gain, slices, depth, width)
    cross = lax.all_to_all(cross, "seq", 0, 0, tiled=True)

    far = far_attention(bwq, bwk, bwv, heads, groups)
    trunk_full, trunk_square = trunk_attention(
        where, level_gain, tq, tk, tv, twq, pk, pv, twk, twv, cross, pieces, heads, groups
    )
    trunk_square = lax.psum(trunk_square, "head")
    trunk_out = normalize(trunk_full, trunk_square, heads, features, "trunk_norm")
    branch_full, branch_square = branch_attention(
        where, fork_block, bq, bwq, far, bwk, bwv, cross, kvs, ends, heads, groups
    )
    branch_square = lax.psum(branch_square, "head")
    branch_out = normalize(branch_full, branch_square, heads, features, "branch_norm")
    return trunk_out.reshape(trunk_query.shape), branch_out.reshape(branch_query.shape)


def solution(mesh):
    rows = P("seq", "head", None)
    return jax.shard_map(
        shards,
        mesh=mesh,
        in_specs=(rows,) * 10 + (P("head", None), P("seq")),
        out_specs=(rows, rows),
        check_vma=False,
    )
```

```python
import functools
import math

import jax
import jax.numpy as jnp
from jax import lax
from jax.experimental import pallas as pl
from jax.experimental.pallas import tpu as pltpu
from jax.sharding import PartitionSpec as P

BLK = 128
WIN = 512
COLS = 4
MASKED = -1e30
F32 = jnp.float32
BF16 = jnp.bfloat16
VMEM_BYTES = 60 * 1024 * 1024
SMALL_BYTES = 28 * 1024 * 1024


def params(limit=VMEM_BYTES):
    return pltpu.CompilerParams(vmem_limit_bytes=limit)


def hbm():
    return pl.BlockSpec(memory_space=pltpu.HBM)


def vmem():
    return pl.BlockSpec(memory_space=pltpu.VMEM)


def block_copy(src, dst, sems, block, rows, src_block=None):
    src_block = block if src_block is None else src_block
    return pltpu.make_async_copy(
        src.at[pl.ds(src_block * rows, rows)], dst.at[pl.ds(block * rows, rows)], sems.at[block]
    )


def smem():
    return pl.BlockSpec(memory_space=pltpu.SMEM)


def gain_factor(level, width):
    return 1.0 / math.sqrt(width * BLK * 2 ** max(level - 1, 0))


def every(rows_ref, wide, count, each):
    return wide[pl.ds(each, rows_ref.shape[0] // count, stride=count), :].astype(BF16)


def state_kernel(depth, heads, gain_ref, k_hbm, v_hbm, *rest):
    piece_refs, sum_ref = rest[:COLS], rest[COLS]
    keys, values, kf, vf, levels, key_sems, value_sems = rest[COLS + 1 :]
    rows, width = kf.shape
    per_piece = heads // COLS
    copies = [
        (block_copy(k_hbm, keys, key_sems, b, rows), block_copy(v_hbm, values, value_sems, b, rows))
        for b in range(1 << depth)
    ]
    for pair in copies:
        for copy in pair:
            copy.start()
    for b, pair in enumerate(copies):
        for copy in pair:
            copy.wait()
        kf[...] = keys[b * rows : (b + 1) * rows].astype(F32)
        vf[...] = values[b * rows : (b + 1) * rows].astype(F32)
        for h in range(heads):
            k = kf[pl.ds(h, BLK, stride=heads), :].astype(BF16)
            v = vf[pl.ds(h, BLK, stride=heads), :].astype(BF16)
            merged = lax.dot_general(k, v, (((0,), (0,)), ((), ())), preferred_element_type=F32)
            before = None
            for bit in range(depth):
                if b >> bit & 1:
                    part = levels[bit, h] * (gain_ref[h, bit + 1] * gain_factor(bit + 1, width))
                    before = part if before is None else before + part
            carry = 0
            while b >> carry & 1:
                merged = merged + levels[carry, h]
                carry += 1
            if before is not None:
                piece_refs[h // per_piece][b - 1, h % per_piece] = before.astype(BF16)
            if carry < depth:
                levels[carry, h] = merged
            else:
                sum_ref[h // per_piece, h % per_piece] = merged.astype(BF16)


def block_sums(gain, keys, values, heads, depth):
    blocks = 1 << depth
    rows, width = keys.shape[0] // blocks, keys.shape[1]
    piece = jax.ShapeDtypeStruct((blocks - 1, heads // COLS, width, width), BF16)
    return pl.pallas_call(
        functools.partial(state_kernel, depth, heads),
        in_specs=[smem(), hbm(), hbm()],
        out_specs=[vmem()] * (COLS + 1),
        out_shape=[piece] * COLS + [jax.ShapeDtypeStruct((COLS, heads // COLS, width, width), BF16)],
        scratch_shapes=[
            pltpu.VMEM(keys.shape, BF16),
            pltpu.VMEM(values.shape, BF16),
            pltpu.VMEM((rows, width), F32),
            pltpu.VMEM((rows, width), F32),
            pltpu.VMEM((depth, heads, width, width), F32),
            pltpu.SemaphoreType.DMA((blocks,)),
            pltpu.SemaphoreType.DMA((blocks,)),
        ],
        compiler_params=params(),
        cost_estimate=pl.CostEstimate(
            flops=2 * keys.size * width, bytes_accessed=4 * keys.size + 2 * heads * width * width * blocks, transcendentals=0
        ),
        name="block_sums",
    )(gain, keys, values)


def in_plane(sums, column, weight):
    total = None
    for bit in range(COLS.bit_length() - 1):
        if column >> bit & 1:
            first = ((column >> bit) ^ 1) << bit
            part = functools.reduce(jnp.add, sums[first : first + (1 << bit)]) * weight(bit)
            total = part if total is None else total + part
    return total


def level_weight(gain_ref, head, depth, width, bit):
    return gain_ref[head, depth + bit + 1] * gain_factor(depth + bit + 1, width)


def plane_kernel(depth, where_ref, gain_ref, sums_ref, local_ref, plane_ref, ends_ref):
    each, width = sums_ref.shape[1], sums_ref.shape[2]
    first = (where_ref[0] & (COLS - 1)) * each
    for j in range(each):
        sums = [sums_ref[c, j].astype(F32) for c in range(COLS)]
        whole = functools.reduce(jnp.add, sums).astype(BF16)
        for p in range(plane_ref.shape[0]):
            plane_ref[p, j] = whole
        before = in_plane(sums, COLS - 1, lambda bit: level_weight(gain_ref, first + j, depth, width, bit))
        ends_ref[0, j] = before.astype(BF16)
        for f in range(local_ref.shape[0]):
            ends_ref[f + 1, j] = (before + local_ref[f, j].astype(F32)).astype(BF16)


def plane_sums(where, gain, sums, local, planes, depth):
    quarter = sums.shape[1:]
    return pl.pallas_call(
        functools.partial(plane_kernel, depth),
        in_specs=[smem(), smem(), vmem(), vmem()],
        out_specs=[vmem(), vmem()],
        out_shape=[
            jax.ShapeDtypeStruct((planes, *quarter), BF16),
            jax.ShapeDtypeStruct((local.shape[0] + 1, *quarter), BF16),
        ],
        compiler_params=params(),
        cost_estimate=pl.CostEstimate(flops=4 * sums.size, bytes_accessed=8 * sums.size, transcendentals=0),
        name="plane_sums",
    )(where, gain, sums, local)


def cross_kernel(depth, where_ref, gain_ref, sums_ref, planes_ref, out_ref, top_ref):
    each, width = sums_ref.shape[1], sums_ref.shape[2]
    planes = planes_ref.shape[0]
    col_bits = COLS.bit_length() - 1
    plane = where_ref[0] >> col_bits
    first = (where_ref[0] & (COLS - 1)) * each
    for j in range(each):
        sums = [sums_ref[c, j].astype(F32) for c in range(COLS)]
        above = jnp.zeros((width, width), F32)
        top = jnp.zeros((width, width), F32)
        for s in range(planes - 1):
            state = planes_ref[s, j].astype(F32)
            share = jnp.float32(0.0)
            for bit in range(planes.bit_length() - 1):
                weight = level_weight(gain_ref, first + j, depth, width, col_bits + bit)
                held = jnp.logical_and((plane >> bit) & 1 == 1, (plane >> bit) ^ 1 == s >> bit)
                share = share + jnp.where(held, weight, 0.0)
                if ((planes - 1) >> bit) ^ 1 == s >> bit:
                    top = top + state * weight
            above = above + state * share
        top_ref[j] = top
        for c in range(COLS):
            before = in_plane(sums, c, lambda bit: level_weight(gain_ref, first + j, depth, width, bit))
            out_ref[c, j] = (above if before is None else above + before).astype(BF16)


def cross_sums(where, gain, sums, planes, depth):
    return pl.pallas_call(
        functools.partial(cross_kernel, depth),
        in_specs=[smem(), smem(), vmem(), vmem()],
        out_specs=[vmem(), vmem()],
        out_shape=[jax.ShapeDtypeStruct(sums.shape, BF16), jax.ShapeDtypeStruct(sums.shape[1:], F32)],
        compiler_params=params(),
        cost_estimate=pl.CostEstimate(flops=20 * sums.size, bytes_accessed=8 * sums.size, transcendentals=0),
        name="cross_sums",
    )(where, gain, sums, planes)


def place(src_ref, wide, dst, start, groups):
    tokens = src_ref.shape[0] // groups
    wide[...] = src_ref[...].astype(F32)
    for g in range(groups):
        part = wide[pl.ds(g, tokens, stride=groups), :].astype(BF16)
        dst[g, pl.ds(start, tokens), : src_ref.shape[1]] = part


def split_groups(wide):
    rows, width = wide.shape
    pairs = wide.reshape(rows // 16, 16, width)
    low, high = pairs[:, :8], pairs[:, 8:]
    upper = lax.broadcasted_iota(jnp.int32, low.shape, 1) < 4
    first = jnp.where(upper, low, pltpu.roll(high, 4, 1))
    second = jnp.where(upper, pltpu.roll(low, 4, 1), high)
    return [part.reshape(rows // 2, width) for part in (first, second)]


def join_groups(first, second):
    rows, width = first.shape
    first, second = (part.reshape(rows // 8, 8, width) for part in (first, second))
    upper = lax.broadcasted_iota(jnp.int32, first.shape, 1) < 4
    low = jnp.where(upper, first, pltpu.roll(second, 4, 1))
    high = jnp.where(upper, pltpu.roll(first, 4, 1), second)
    return jnp.concatenate([low, high], axis=1).reshape(2 * rows, width)


def window_logits(queries, keys, token, share, bias):
    rows = queries.shape[0]
    logits = lax.dot_general(queries, keys, (((1,), (1,)), ((), ())), preferred_element_type=F32)
    row = token + lax.broadcasted_iota(jnp.int32, (rows, BLK), 0) // share
    col = lax.broadcasted_iota(jnp.int32, (rows, BLK), 1)
    late = col > row
    first = jnp.where(late, logits[:, :BLK], MASKED)
    last = jnp.where(late, MASKED, logits[:, -BLK:])
    logits = jnp.concatenate([first, logits[:, BLK:-BLK], last], axis=1)
    return logits if bias is None else logits + bias


def window_outputs(logits, values, width):
    top = jnp.max(logits, axis=1, keepdims=True)
    weights = jnp.exp2((logits - top) * (math.log2(math.e) / math.sqrt(width))).astype(BF16)
    both = jnp.dot(weights, values, preferred_element_type=F32)
    return both[:, :width] / both[:, width:]


def window_block(q_ref, kh, vh, base, groups, bias=None):
    width = q_ref.shape[1]
    span = WIN + BLK
    share = q_ref.shape[0] // BLK // groups
    parts = [part.astype(BF16) for part in split_groups(q_ref[...].astype(F32))]
    chunks = [(g, c) for g in range(groups) for c in range(0, BLK * share, BLK)]

    def logits_of(chunk):
        g, c = chunk
        return window_logits(parts[g][c : c + BLK], kh[g, pl.ds(base, span), :], c // share, share, bias)

    outs = []
    ahead = logits_of(chunks[0])
    for i, (g, c) in enumerate(chunks):
        now = ahead
        if i + 1 < len(chunks):
            ahead = logits_of(chunks[i + 1])
        outs.append(window_outputs(now, vh[g, pl.ds(base, span), :], width))
    half = len(outs) // 2
    return join_groups(jnp.concatenate(outs[:half], axis=0), jnp.concatenate(outs[half:], axis=0))


def square_sums(full, heads):
    tokens = full.shape[0] // heads
    row = lax.broadcasted_iota(jnp.int32, (tokens, full.shape[0]), 1) // heads
    mine = row == lax.broadcasted_iota(jnp.int32, (tokens, full.shape[0]), 0)
    sums = jnp.dot(mine.astype(BF16), (full * full).astype(BF16), preferred_element_type=F32)
    ones = jnp.ones((8, full.shape[1]), F32)
    return lax.dot_general(
        ones, sums, (((1,), (1,)), ((), ())), precision=lax.Precision.HIGHEST, preferred_element_type=F32
    )


def far_kernel(heads, groups, q_ref, pk_ref, pv_ref, ck_ref, cv_ref, out_ref, kf, kh, vh):
    step = pl.program_id(0)
    width = q_ref.shape[1]

    @pl.when(step == 0)
    def _():
        vh[:, :, width:] = jnp.ones((groups, vh.shape[1], width), BF16)
        place(pk_ref, kf, kh, 0, groups)
        place(ck_ref, kf, kh, WIN, groups)
        place(pv_ref, kf, vh, 0, groups)
        place(cv_ref, kf, vh, WIN, groups)

    out_ref[...] = window_block(q_ref, kh, vh, pl.multiple_of(step * BLK, BLK), groups).astype(BF16)


def attention_cost(tokens, heads, width, extra=0):
    span = WIN + BLK
    return pl.CostEstimate(
        flops=6 * tokens * heads * span * width + extra,
        bytes_accessed=12 * tokens * heads * width,
        transcendentals=tokens * heads * span,
    )


def far_attention(queries, keys, values, heads, groups):
    width = queries.shape[1]
    steps = queries.shape[0] // (BLK * heads) - WIN // BLK
    skip = WIN // BLK
    at_first = pl.BlockSpec((WIN * groups, width), lambda i: (0, 0))
    at_next = pl.BlockSpec((WIN * groups, width), lambda i: (1, 0))
    return pl.pallas_call(
        functools.partial(far_kernel, heads, groups),
        grid=(steps,),
        in_specs=[
            pl.BlockSpec((BLK * heads, width), lambda i: (i + skip, 0)),
            at_first,
            at_first,
            at_next,
            at_next,
        ],
        out_specs=pl.BlockSpec((BLK * heads, width), lambda i: (i, 0)),
        out_shape=jax.ShapeDtypeStruct((steps * BLK * heads, width), BF16),
        scratch_shapes=[
            pltpu.VMEM((WIN * groups, width), F32),
            pltpu.VMEM((groups, 2 * WIN, width), BF16),
            pltpu.VMEM((groups, 2 * WIN, 2 * width), BF16),
        ],
        compiler_params=params(),
        cost_estimate=attention_cost(steps * BLK, heads, width),
        name="far_attention",
    )(queries, keys, values, keys, values)


def trunk_kernel(heads, groups, where_ref, gain_ref, q_ref, k_ref, v_ref, wq_ref, pk_ref, pv_ref, ck_ref, cv_ref, cross_ref, *rest):
    piece_refs, out_ref, square_ref = rest[:COLS], rest[COLS], rest[COLS + 1]
    nf, tf, sf, kf, kh, vh, of = rest[COLS + 2 :]
    step = pl.program_id(0)
    width = q_ref.shape[1]

    @pl.when(step == 0)
    def _():
        vh[:, :, width:] = jnp.ones((groups, vh.shape[1], width), BF16)
        place(pk_ref, kf, kh, 0, groups)
        place(ck_ref, kf, kh, WIN, groups)
        place(pv_ref, kf, vh, 0, groups)
        place(cv_ref, kf, vh, WIN, groups)

    nf[...] = q_ref[...].astype(F32)
    tf[...] = k_ref[...].astype(F32)
    sf[...] = v_ref[...].astype(F32)
    base = pl.multiple_of(step * BLK, BLK)
    span = WIN + BLK
    reach = jnp.where(where_ref[0] == 0, WIN - step * BLK, 0)
    bias = jnp.where(lax.broadcasted_iota(jnp.int32, (1, span), 1) < reach, MASKED, 0.0).astype(F32)
    row = lax.broadcasted_iota(jnp.int32, (BLK, BLK), 0)
    col = lax.broadcasted_iota(jnp.int32, (BLK, BLK), 1)
    inner = (step > 0).astype(F32).astype(BF16)
    per_piece = heads // COLS
    q = [every(q_ref, nf, heads, h) for h in range(heads)]
    inside = [
        lax.dot_general(q[h], every(k_ref, tf, heads, h), (((1,), (1,)), ((), ())), preferred_element_type=F32)
        for h in range(heads)
    ]
    for h in range(heads):
        weight = jnp.where(col <= row, inside[h], 0.0) * (gain_ref[h, 0] * gain_factor(0, width))
        left = jnp.concatenate([weight.astype(BF16), q[h], q[h]], axis=1)
        right = jnp.concatenate(
            [every(v_ref, sf, heads, h), cross_ref[h // per_piece, h % per_piece], piece_refs[h // per_piece][0, h % per_piece] * inner], axis=0
        )
        of[pl.ds(h, BLK, stride=heads), :] = jnp.dot(left, right, preferred_element_type=F32)
    full = window_block(wq_ref, kh, vh, base, groups, bias) + of[...]
    out_ref[...] = full
    square_ref[0] = square_sums(full, heads)


def trunk_attention(where, gain, q, k, v, wq, pk, pv, ck, cv, cross, pieces, heads, groups):
    width = q.shape[1]
    blocks = q.shape[0] // (BLK * heads)
    at_block = pl.BlockSpec((BLK * heads, width), lambda i: (i, 0))
    whole = pl.BlockSpec((WIN * groups, width), lambda i: (0, 0))
    own = pl.BlockSpec(cross.shape, lambda i: (0, 0, 0, 0))
    piece = pl.BlockSpec((1, heads // COLS, width, width), lambda i: (jnp.maximum(i - 1, 0), 0, 0, 0))
    wide = pltpu.VMEM((BLK * heads, width), F32)
    return pl.pallas_call(
        functools.partial(trunk_kernel, heads, groups),
        grid=(blocks,),
        in_specs=[smem(), smem()] + [at_block] * 4 + [whole] * 4 + [own] + [piece] * COLS,
        out_specs=[at_block, pl.BlockSpec((1, 8, BLK), lambda i: (i, 0, 0))],
        out_shape=[
            jax.ShapeDtypeStruct(q.shape, F32),
            jax.ShapeDtypeStruct((blocks, 8, BLK), F32),
        ],
        scratch_shapes=[
            wide,
            wide,
            wide,
            pltpu.VMEM((WIN * groups, width), F32),
            pltpu.VMEM((groups, 2 * WIN, width), BF16),
            pltpu.VMEM((groups, 2 * WIN, 2 * width), BF16),
            wide,
        ],
        compiler_params=params(),
        cost_estimate=attention_cost(blocks * BLK, heads, width, 2 * blocks * BLK * BLK * heads * 4 * width),
        name="trunk_attention",
    )(where, gain, q, k, v, wq, pk, pv, ck, cv, cross, *pieces)


def near_kernel(groups, where_ref, fork_ref, q_ref, ck_ref, cv_ref, *rest):
    kv_refs, out_ref = rest[:COLS], rest[COLS]
    kf, kh, vh, kt = rest[COLS + 1 :]
    step = pl.program_id(0)
    width = q_ref.shape[1]
    column = where_ref[0] & (COLS - 1)
    start = pl.multiple_of(fork_ref[0] * BLK, BLK)

    @pl.when(step == 0)
    def _():
        for i in range(COLS):
            kt[column ^ i] = kv_refs[i][...]
        vh[:, :, width:] = jnp.ones((groups, vh.shape[1], width), BF16)
        place(kt.at[0], kf, vh, 0, groups)
        place(kt.at[1], kf, vh, WIN, groups)
        place(kt.at[2], kf, kh, 0, groups)
        place(kt.at[3], kf, kh, WIN, groups)
        place(ck_ref, kf, kh, pl.multiple_of(start + WIN, BLK), groups)
        place(cv_ref, kf, vh, pl.multiple_of(start + WIN, BLK), groups)

    base = pl.multiple_of(start + step * BLK, BLK)
    out_ref[...] = window_block(q_ref, kh, vh, base, groups).astype(BF16)


def near_attention(where, fork, wq, ck, cv, kvs, heads, groups):
    width = wq.shape[1]
    steps = WIN // BLK
    at_block = pl.BlockSpec((BLK * heads, width), lambda i: (i, 0))
    whole = pl.BlockSpec((WIN * groups, width), lambda i: (0, 0))
    return pl.pallas_call(
        functools.partial(near_kernel, groups),
        grid=(steps,),
        in_specs=[smem(), smem(), at_block, whole, whole] + [whole] * COLS,
        out_specs=at_block,
        out_shape=jax.ShapeDtypeStruct((steps * BLK * heads, width), BF16),
        scratch_shapes=[
            pltpu.VMEM((WIN * groups, width), F32),
            pltpu.VMEM((groups, 3 * WIN, width), BF16),
            pltpu.VMEM((groups, 3 * WIN, 2 * width), BF16),
            pltpu.VMEM((COLS, WIN * groups, width), BF16),
        ],
        compiler_params=params(),
        cost_estimate=attention_cost(steps * BLK, heads, width),
        name="near_attention",
    )(where, fork, wq, ck, cv, *kvs)


def branch_kernel(heads, where_ref, fork_ref, q_hbm, near_hbm, far_hbm, *rest):
    piece_refs = rest[:COLS]
    full_ref, square_ref, qs, ws, nf, of, es, q_sems, w_sems = rest[COLS:]
    rows = nf.shape[0]
    blocks = qs.shape[0] // rows
    skip = WIN // BLK
    per_piece = heads // COLS
    column = where_ref[0] & (COLS - 1)
    for b in range(blocks):
        block_copy(q_hbm, qs, q_sems, b, rows).start()
        if b < skip:
            block_copy(near_hbm, ws, w_sems, b, rows).start()
        else:
            block_copy(far_hbm, ws, w_sems, b, rows, b - skip).start()
    for i in range(COLS):
        for j in range(per_piece):
            es[(column ^ i) * per_piece + j] = piece_refs[i][fork_ref[0], j]

    def one_block(b, carry):
        block_copy(q_hbm, qs, q_sems, b, rows).wait()
        block_copy(near_hbm, ws, w_sems, b, rows, 0).wait()
        at = pl.ds(pl.multiple_of(b * rows, rows), rows)
        nf[...] = qs[at, :].astype(F32)
        for h in range(heads):
            q = nf[pl.ds(h, BLK, stride=heads), :].astype(BF16)
            of[pl.ds(h, BLK, stride=heads), :] = jnp.dot(q, es[h], preferred_element_type=F32)
        full = ws[at, :].astype(F32) + of[...]
        full_ref[at, :] = full
        square_ref[b] = square_sums(full, heads)
        return carry

    lax.fori_loop(0, blocks, one_block, 0)


def branch_linear(where, fork, q, near, far, pieces, heads):
    width = q.shape[1]
    rows = BLK * heads
    blocks = q.shape[0] // rows
    wide = pltpu.VMEM((rows, width), F32)
    return pl.pallas_call(
        functools.partial(branch_kernel, heads),
        in_specs=[smem(), smem(), hbm(), hbm(), hbm()] + [vmem()] * COLS,
        out_specs=[vmem(), vmem()],
        out_shape=[
            jax.ShapeDtypeStruct(q.shape, F32),
            jax.ShapeDtypeStruct((blocks, 8, BLK), F32),
        ],
        scratch_shapes=[
            pltpu.VMEM(q.shape, BF16),
            pltpu.VMEM(q.shape, BF16),
            wide,
            wide,
            pltpu.VMEM((heads, width, width), BF16),
            pltpu.SemaphoreType.DMA((blocks,)),
            pltpu.SemaphoreType.DMA((blocks,)),
        ],
        compiler_params=params(SMALL_BYTES),
        cost_estimate=pl.CostEstimate(
            flops=4 * blocks * BLK * heads * width * width, bytes_accessed=8 * q.size, transcendentals=0
        ),
        name="branch_linear",
    )(where, fork, q, near, far, *pieces)


def norm_kernel(heads, features, trunk_hbm, trunk_square, branch_ref, branch_square, trunk_out, branch_out, held, done, in_sems, out_sems):
    rows, width = BLK * heads, branch_ref.shape[1]
    trunk_blocks = trunk_hbm.shape[0] // rows
    branch_blocks = branch_ref.shape[0] // rows
    for b in range(trunk_blocks):
        block_copy(trunk_hbm, held, in_sems, b, rows).start()

    def scaled(full, square):
        scale = lax.rsqrt(square[0:1, :] / features + 1e-06)
        scale = jnp.broadcast_to(scale, (width, BLK)).T
        return (full.reshape(BLK, heads, width) * scale[:, None, :]).astype(BF16).reshape(rows, width)

    def leave(out_hbm, block, slot):
        return pltpu.make_async_copy(
            done.at[pl.ds(slot * rows, rows)], out_hbm.at[pl.ds(block * rows, rows)], out_sems.at[slot]
        )

    def branch_block(b, carry):
        at = pl.ds(pl.multiple_of(b * rows, rows), rows)
        done[at, :] = scaled(branch_ref[at, :], branch_square[b])
        leave(branch_out, b, b).start()
        return carry

    def trunk_block(b, carry):
        block_copy(trunk_hbm, held, in_sems, b, rows).wait()
        slot = branch_blocks + b
        full = held[pl.ds(pl.multiple_of(b * rows, rows), rows), :]
        done[pl.ds(pl.multiple_of(slot * rows, rows), rows), :] = scaled(full, trunk_square[b])
        leave(trunk_out, b, slot).start()
        return carry

    lax.fori_loop(0, branch_blocks, branch_block, 0)
    lax.fori_loop(0, trunk_blocks, trunk_block, 0)
    for b in range(branch_blocks):
        leave(branch_out, b, b).wait()
    for b in range(trunk_blocks):
        leave(trunk_out, b, branch_blocks + b).wait()


def normalize(trunk, trunk_square, branch, branch_square, heads, features):
    width = trunk.shape[1]
    rows = BLK * heads
    trunk_blocks, branch_blocks = trunk.shape[0] // rows, branch.shape[0] // rows
    total = trunk_blocks + branch_blocks
    return pl.pallas_call(
        functools.partial(norm_kernel, heads, features),
        in_specs=[hbm(), vmem(), vmem(), vmem()],
        out_specs=[hbm(), hbm()],
        out_shape=[jax.ShapeDtypeStruct(trunk.shape, BF16), jax.ShapeDtypeStruct(branch.shape, BF16)],
        scratch_shapes=[
            pltpu.VMEM(trunk.shape, F32),
            pltpu.VMEM((total * rows, width), BF16),
            pltpu.SemaphoreType.DMA((trunk_blocks,)),
            pltpu.SemaphoreType.DMA((total,)),
        ],
        compiler_params=params(SMALL_BYTES),
        cost_estimate=pl.CostEstimate(
            flops=2 * (trunk.size + branch.size), bytes_accessed=6 * (trunk.size + branch.size), transcendentals=0
        ),
        name="normalize",
    )(trunk, trunk_square, branch, branch_square)


def shards(
    trunk_query,
    trunk_key,
    trunk_value,
    trunk_wquery,
    trunk_wkey,
    trunk_wvalue,
    branch_query,
    branch_wquery,
    branch_wkey,
    branch_wvalue,
    level_gain,
    fork_block,
):
    tokens, heads, width = trunk_query.shape
    groups = trunk_wkey.shape[1]
    depth = (tokens // BLK).bit_length() - 1
    count = lax.axis_size("seq")
    planes = count // COLS
    features = heads * lax.axis_size("head") * width
    me = lax.axis_index("seq")
    column, plane = me % COLS, me // COLS
    where = me.astype(jnp.int32).reshape(1)
    root = count - 1
    top = planes - 1

    def flat(x):
        return x.reshape(x.shape[0] * x.shape[1], x.shape[2])

    tq, tk, tv, twq = flat(trunk_query), flat(trunk_key), flat(trunk_value), flat(trunk_wquery)
    twk, twv = flat(trunk_wkey), flat(trunk_wvalue)
    bq, bwq, bwk, bwv = flat(branch_query), flat(branch_wquery), flat(branch_wkey), flat(branch_wvalue)

    def send(x, pairs):
        return lax.ppermute(x, "seq", pairs)

    def down(x):
        step = planes // 2
        while step:
            starts = [p for p in range(planes) if (top - p) % (2 * step) == 0 and p >= step]
            pairs = [(p * COLS + c, (p - step) * COLS + c) for p in starts for c in range(COLS)]
            got = send(x, pairs)
            hit = functools.reduce(jnp.logical_or, [plane == p - step for p in starts])
            x = jnp.where(hit, got, x)
            step //= 2
        return x

    def around(x):
        return [x] + [send(x, [(i, i ^ d) for i in range(count)]) for d in range(1, COLS)]

    def in_groups(x, groups_of):
        return lax.all_to_all(x, "seq", 0, 0, tiled=True, axis_index_groups=groups_of)

    in_one_plane = [[p * COLS + c for c in range(COLS)] for p in range(planes)]
    in_one_column = [[p * COLS + c for p in range(planes)] for c in range(COLS)]

    half = COLS // 2
    got = send(twv, [(root - i, root - i - half) for i in range(half)])
    kv = down(jnp.where(column >= half, twk, got))
    shift = [(i, i + 1) for i in range(count - 1)]
    pk, pv = send(twk, shift), send(twv, shift)

    *pieces, shard_sum = block_sums(level_gain, tk, tv, heads, depth)
    local = pieces[COLS - 1]
    for c in range(COLS - 1):
        got = send(pieces[c], [(root, root - (COLS - 1) + c)])
        local = jnp.where(column == c, got, local)
    sums = in_groups(shard_sum, in_one_plane)
    plane_sum, ends = plane_sums(where, level_gain, sums, local, planes, depth)
    plane_sum = in_groups(plane_sum, in_one_column)
    ends = down(ends)
    cross, above = cross_sums(where, level_gain, sums, plane_sum, depth)
    cross = in_groups(cross, in_one_plane)

    far = far_attention(bwq, bwk, bwv, heads, groups)
    kv, far = lax.optimization_barrier((kv, far))
    kvs = around(kv)
    ends = around((ends.astype(F32) + above).astype(BF16))

    trunk_full, trunk_square = trunk_attention(
        where, level_gain, tq, tk, tv, twq, pk, pv, twk, twv, cross, pieces, heads, groups
    )
    near = near_attention(where, fork_block, bwq, bwk, bwv, kvs, heads, groups)
    branch_full, branch_square = branch_linear(where, fork_block, bq, near, far, ends, heads)
    trunk_square, branch_square = lax.psum((trunk_square, branch_square), "head")
    trunk_out, branch_out = normalize(trunk_full, trunk_square, branch_full, branch_square, heads, features)
    return trunk_out.reshape(trunk_query.shape), branch_out.reshape(branch_query.shape)


def solution(mesh):
    rows = P("seq", "head", None)
    return jax.shard_map(
        shards,
        mesh=mesh,
        in_specs=(rows,) * 10 + (P("head", None), P("seq")),
        out_specs=(rows, rows),
        check_vma=False,
    )
```

```python
import functools
import math

import jax
import jax.numpy as jnp
from jax import lax
from jax.experimental import pallas as pl
from jax.experimental.pallas import tpu as pltpu
from jax.sharding import PartitionSpec as P

BLK = 128
WIN = 512
COLS = 4
MASKED = -1e30
F32 = jnp.float32
BF16 = jnp.bfloat16
VMEM_BYTES = 60 * 1024 * 1024
SMALL_BYTES = 28 * 1024 * 1024


def params(limit=VMEM_BYTES):
    return pltpu.CompilerParams(vmem_limit_bytes=limit)


def hbm():
    return pl.BlockSpec(memory_space=pltpu.HBM)


def vmem():
    return pl.BlockSpec(memory_space=pltpu.VMEM)


def block_copy(src, dst, sems, block, rows, src_block=None):
    src_block = block if src_block is None else src_block
    return pltpu.make_async_copy(
        src.at[pl.ds(src_block * rows, rows)], dst.at[pl.ds(block * rows, rows)], sems.at[block]
    )


def smem():
    return pl.BlockSpec(memory_space=pltpu.SMEM)


def gain_factor(level, width):
    return 1.0 / math.sqrt(width * BLK * 2 ** max(level - 1, 0))


def exchange(parts):
    parts = list(parts)
    rows = lax.broadcasted_iota(jnp.int32, parts[0].shape, 1)
    for step in (4, 2, 1):
        upper = (rows & step) == 0
        for i in range(8):
            if i & step == 0:
                low, high = parts[i], parts[i + step]
                parts[i] = jnp.where(upper, low, pltpu.roll(high, step, 1))
                parts[i + step] = jnp.where(upper, pltpu.roll(low, 8 - step, 1), high)
    return parts


def split_heads(wide):
    rows, width = wide.shape
    octets = wide.reshape(rows // 64, 8, 8, width)
    return [part.reshape(rows // 8, width) for part in exchange([octets[:, t] for t in range(8)])]


def join_heads(heads):
    rows, width = heads[0].shape
    tokens = exchange([head.reshape(rows // 8, 8, width) for head in heads])
    return jnp.stack(tokens, axis=1).reshape(rows * 8, width)


def state_kernel(depth, heads, where_ref, gain_ref, k_hbm, v_hbm, *rest):
    piece_refs, sum_refs = rest[:COLS], rest[COLS : 2 * COLS]
    keys, values, levels, sums, key_sems, value_sems = rest[2 * COLS :]
    width = keys.shape[1]
    rows = keys.shape[0] >> depth
    per_piece = heads // COLS
    column = where_ref[0] & (COLS - 1)
    copies = [
        (block_copy(k_hbm, keys, key_sems, b, rows), block_copy(v_hbm, values, value_sems, b, rows))
        for b in range(1 << depth)
    ]
    for pair in copies:
        for copy in pair:
            copy.start()
    for b, pair in enumerate(copies):
        for copy in pair:
            copy.wait()
        key_heads = split_heads(keys[b * rows : (b + 1) * rows].astype(F32))
        value_heads = split_heads(values[b * rows : (b + 1) * rows].astype(F32))
        for h in range(heads):
            k, v = key_heads[h].astype(BF16), value_heads[h].astype(BF16)
            merged = lax.dot_general(k, v, (((0,), (0,)), ((), ())), preferred_element_type=F32)
            before = None
            for bit in range(depth):
                if b >> bit & 1:
                    part = levels[bit, h] * (gain_ref[h, bit + 1] * gain_factor(bit + 1, width))
                    before = part if before is None else before + part
            carry = 0
            while b >> carry & 1:
                merged = merged + levels[carry, h]
                carry += 1
            if before is not None:
                piece_refs[h // per_piece][b - 1, h % per_piece] = before.astype(BF16)
            if carry < depth:
                levels[carry, h] = merged
            else:
                sums[column ^ (h // per_piece), h % per_piece] = merged.astype(BF16)
    for d in range(COLS):
        sum_refs[d][...] = sums[d]


def block_sums(where, gain, keys, values, heads, depth):
    blocks = 1 << depth
    width = keys.shape[1]
    each = heads // COLS
    piece = jax.ShapeDtypeStruct((blocks - 1, each, width, width), BF16)
    return pl.pallas_call(
        functools.partial(state_kernel, depth, heads),
        in_specs=[smem(), smem(), hbm(), hbm()],
        out_specs=[vmem()] * (2 * COLS),
        out_shape=[piece] * COLS + [jax.ShapeDtypeStruct((each, width, width), BF16)] * COLS,
        scratch_shapes=[
            pltpu.VMEM(keys.shape, BF16),
            pltpu.VMEM(values.shape, BF16),
            pltpu.VMEM((depth, heads, width, width), F32),
            pltpu.VMEM((COLS, each, width, width), BF16),
            pltpu.SemaphoreType.DMA((blocks,)),
            pltpu.SemaphoreType.DMA((blocks,)),
        ],
        compiler_params=params(),
        cost_estimate=pl.CostEstimate(
            flops=2 * keys.size * width, bytes_accessed=4 * keys.size + 2 * heads * width * width * blocks, transcendentals=0
        ),
        name="block_sums",
    )(where, gain, keys, values)


def in_plane(sums, column, weight):
    total = None
    for bit in range(COLS.bit_length() - 1):
        if column >> bit & 1:
            first = ((column >> bit) ^ 1) << bit
            part = functools.reduce(jnp.add, sums[first : first + (1 << bit)]) * weight(bit)
            total = part if total is None else total + part
    return total


def level_weight(gain_ref, head, depth, width, bit):
    return gain_ref[head, depth + bit + 1] * gain_factor(depth + bit + 1, width)


def in_order(where_ref, refs, held):
    for d, ref in enumerate(refs):
        held[(where_ref[0] & (COLS - 1)) ^ d] = ref[...]


def plane_kernel(depth, where_ref, gain_ref, *rest):
    sum_refs, (plane_ref, before_ref, held) = rest[:COLS], rest[COLS:]
    each, width = plane_ref.shape[:2]
    first = (where_ref[0] & (COLS - 1)) * each
    in_order(where_ref, sum_refs, held)
    for j in range(each):
        sums = [held[c, j].astype(F32) for c in range(COLS)]
        plane_ref[j] = functools.reduce(jnp.add, sums).astype(BF16)
        before_ref[j] = in_plane(sums, COLS - 1, lambda bit: level_weight(gain_ref, first + j, depth, width, bit))


def plane_sums(where, gain, sums, depth):
    quarter = sums[0].shape
    return pl.pallas_call(
        functools.partial(plane_kernel, depth),
        in_specs=[smem(), smem()] + [vmem()] * COLS,
        out_specs=[vmem(), vmem()],
        out_shape=[jax.ShapeDtypeStruct(quarter, BF16), jax.ShapeDtypeStruct(quarter, F32)],
        scratch_shapes=[pltpu.VMEM((COLS, *quarter), BF16)],
        compiler_params=params(SMALL_BYTES),
        cost_estimate=pl.CostEstimate(flops=16 * sums[0].size, bytes_accessed=16 * sums[0].size, transcendentals=0),
        name="plane_sums",
    )(where, gain, *sums)


def cross_kernel(depth, planes, where_ref, gain_ref, *rest):
    sum_refs, plane_refs = rest[:COLS], rest[COLS : COLS + planes]
    out_refs, (top_ref, held, states, outs) = rest[COLS + planes : 2 * COLS + planes], rest[2 * COLS + planes :]
    each, width = top_ref.shape[:2]
    col_bits = COLS.bit_length() - 1
    plane = where_ref[0] >> col_bits
    column = where_ref[0] & (COLS - 1)
    in_order(where_ref, sum_refs, held)
    for d, ref in enumerate(plane_refs):
        states[plane ^ d] = ref[...]
    for j in range(each):
        head = column * each + j
        sums = [held[c, j].astype(F32) for c in range(COLS)]
        above = jnp.zeros((width, width), F32)
        top = jnp.zeros((width, width), F32)
        for s in range(planes - 1):
            state = states[s, j].astype(F32)
            share = jnp.float32(0.0)
            for bit in range(planes.bit_length() - 1):
                weight = level_weight(gain_ref, head, depth, width, col_bits + bit)
                inside = jnp.logical_and((plane >> bit) & 1 == 1, (plane >> bit) ^ 1 == s >> bit)
                share = share + jnp.where(inside, weight, 0.0)
                if ((planes - 1) >> bit) ^ 1 == s >> bit:
                    top = top + state * weight
            above = above + state * share
        top_ref[j] = top
        for c in range(COLS):
            before = in_plane(sums, c, lambda bit: level_weight(gain_ref, head, depth, width, bit))
            outs[column ^ c, j] = (above if before is None else above + before).astype(BF16)
    for d in range(COLS):
        out_refs[d][...] = outs[d]


def cross_sums(where, gain, sums, planes, depth):
    quarter = sums[0].shape
    return pl.pallas_call(
        functools.partial(cross_kernel, depth, len(planes)),
        in_specs=[smem(), smem()] + [vmem()] * (COLS + len(planes)),
        out_specs=[vmem()] * (COLS + 1),
        out_shape=[jax.ShapeDtypeStruct(quarter, BF16)] * COLS + [jax.ShapeDtypeStruct(quarter, F32)],
        scratch_shapes=[
            pltpu.VMEM((COLS, *quarter), BF16),
            pltpu.VMEM((len(planes), *quarter), BF16),
            pltpu.VMEM((COLS, *quarter), BF16),
        ],
        compiler_params=params(SMALL_BYTES),
        cost_estimate=pl.CostEstimate(flops=60 * sums[0].size, bytes_accessed=30 * sums[0].size, transcendentals=0),
        name="cross_sums",
    )(where, gain, *sums, *planes)


def place(src_ref, dst, start):
    rows, width = src_ref.shape
    pairs = src_ref[...].astype(F32).reshape(rows // 16, 16, width)
    low, high = pairs[:, :8], pairs[:, 8:]
    even = (lax.broadcasted_iota(jnp.int32, low.shape, 1) & 1) == 0
    first = jnp.where(even, low, pltpu.roll(high, 1, 1))
    second = jnp.where(even, pltpu.roll(low, 7, 1), high)
    for g, part in enumerate((first, second)):
        dst[g, pl.ds(start, rows // 2), :width] = part.reshape(rows // 2, width).astype(BF16)


def token_at(place_of):
    return (place_of & -8) | ((place_of & 1) << 2) | ((place_of & 7) >> 1)


def split_groups(wide):
    rows, width = wide.shape
    pairs = wide.reshape(rows // 16, 16, width)
    low, high = pairs[:, :8], pairs[:, 8:]
    upper = lax.broadcasted_iota(jnp.int32, low.shape, 1) < 4
    first = jnp.where(upper, low, pltpu.roll(high, 4, 1))
    second = jnp.where(upper, pltpu.roll(low, 4, 1), high)
    return [part.reshape(rows // 2, width) for part in (first, second)]


def join_groups(first, second):
    rows, width = first.shape
    first, second = (part.reshape(rows // 8, 8, width) for part in (first, second))
    upper = lax.broadcasted_iota(jnp.int32, first.shape, 1) < 4
    low = jnp.where(upper, first, pltpu.roll(second, 4, 1))
    high = jnp.where(upper, pltpu.roll(first, 4, 1), second)
    return jnp.concatenate([low, high], axis=1).reshape(2 * rows, width)


def window_logits(queries, keys, token, share, bias):
    rows = queries.shape[0]
    logits = lax.dot_general(queries, keys, (((1,), (1,)), ((), ())), preferred_element_type=F32)
    row = token + lax.broadcasted_iota(jnp.int32, (rows, BLK), 0) // share
    col = token_at(lax.broadcasted_iota(jnp.int32, (rows, BLK), 1))
    late = col > row
    first = jnp.where(late, logits[:, :BLK], MASKED)
    last = jnp.where(late, MASKED, logits[:, -BLK:])
    logits = jnp.concatenate([first, logits[:, BLK:-BLK], last], axis=1)
    return logits if bias is None else logits + bias


def window_outputs(logits, values, width):
    top = jnp.max(logits, axis=1, keepdims=True)
    weights = jnp.exp2((logits - top) * (math.log2(math.e) / math.sqrt(width))).astype(BF16)
    both = jnp.dot(weights, values, preferred_element_type=F32)
    return both[:, :width] / both[:, width:]


def window_block(q_ref, kh, vh, base, groups, bias=None):
    width = q_ref.shape[1]
    span = WIN + BLK
    share = q_ref.shape[0] // BLK // groups
    parts = [part.astype(BF16) for part in split_groups(q_ref[...].astype(F32))]
    chunks = [(g, c) for g in range(groups) for c in range(0, BLK * share, BLK)]

    def logits_of(chunk):
        g, c = chunk
        return window_logits(parts[g][c : c + BLK], kh[g, pl.ds(base, span), :], c // share, share, bias)

    outs = []
    ahead = logits_of(chunks[0])
    for i, (g, c) in enumerate(chunks):
        now = ahead
        if i + 1 < len(chunks):
            ahead = logits_of(chunks[i + 1])
        outs.append(window_outputs(now, vh[g, pl.ds(base, span), :], width))
    half = len(outs) // 2
    return join_groups(jnp.concatenate(outs[:half], axis=0), jnp.concatenate(outs[half:], axis=0))


def square_sums(full, heads):
    tokens = full.shape[0] // heads
    row = lax.broadcasted_iota(jnp.int32, (tokens, full.shape[0]), 1) // heads
    mine = row == lax.broadcasted_iota(jnp.int32, (tokens, full.shape[0]), 0)
    sums = jnp.dot(mine.astype(BF16), (full * full).astype(BF16), preferred_element_type=F32)
    ones = jnp.ones((8, full.shape[1]), F32)
    return lax.dot_general(
        ones, sums, (((1,), (1,)), ((), ())), precision=lax.Precision.HIGHEST, preferred_element_type=F32
    )


def far_kernel(heads, groups, q_ref, pk_ref, pv_ref, ck_ref, cv_ref, out_ref, kh, vh):
    step = pl.program_id(0)
    width = q_ref.shape[1]

    @pl.when(step == 0)
    def _():
        vh[:, :, width:] = jnp.ones((groups, vh.shape[1], width), BF16)
        place(pk_ref, kh, 0)
        place(ck_ref, kh, WIN)
        place(pv_ref, vh, 0)
        place(cv_ref, vh, WIN)

    out_ref[...] = window_block(q_ref, kh, vh, pl.multiple_of(step * BLK, BLK), groups).astype(BF16)


def attention_cost(tokens, heads, width, extra=0):
    span = WIN + BLK
    return pl.CostEstimate(
        flops=6 * tokens * heads * span * width + extra,
        bytes_accessed=12 * tokens * heads * width,
        transcendentals=tokens * heads * span,
    )


def far_attention(queries, keys, values, heads, groups):
    width = queries.shape[1]
    steps = queries.shape[0] // (BLK * heads) - WIN // BLK
    skip = WIN // BLK
    at_first = pl.BlockSpec((WIN * groups, width), lambda i: (0, 0))
    at_next = pl.BlockSpec((WIN * groups, width), lambda i: (1, 0))
    return pl.pallas_call(
        functools.partial(far_kernel, heads, groups),
        grid=(steps,),
        in_specs=[
            pl.BlockSpec((BLK * heads, width), lambda i: (i + skip, 0)),
            at_first,
            at_first,
            at_next,
            at_next,
        ],
        out_specs=pl.BlockSpec((BLK * heads, width), lambda i: (i, 0)),
        out_shape=jax.ShapeDtypeStruct((steps * BLK * heads, width), BF16),
        scratch_shapes=[
            pltpu.VMEM((groups, 2 * WIN, width), BF16),
            pltpu.VMEM((groups, 2 * WIN, 2 * width), BF16),
        ],
        compiler_params=params(),
        cost_estimate=attention_cost(steps * BLK, heads, width),
        name="far_attention",
    )(queries, keys, values, keys, values)


def trunk_kernel(heads, groups, where_ref, gain_ref, q_ref, k_ref, v_ref, wq_ref, pk_ref, pv_ref, ck_ref, cv_ref, *rest):
    cross_refs, piece_refs = rest[:COLS], rest[COLS : 2 * COLS]
    out_ref, square_ref, kh, vh, cs = rest[2 * COLS :]
    step = pl.program_id(0)
    width = q_ref.shape[1]

    @pl.when(step == 0)
    def _():
        vh[:, :, width:] = jnp.ones((groups, vh.shape[1], width), BF16)
        place(pk_ref, kh, 0)
        place(ck_ref, kh, WIN)
        place(pv_ref, vh, 0)
        place(cv_ref, vh, WIN)
        in_order(where_ref, cross_refs, cs)

    base = pl.multiple_of(step * BLK, BLK)
    span = WIN + BLK
    reach = jnp.where(where_ref[0] == 0, WIN - step * BLK, 0)
    bias = jnp.where(lax.broadcasted_iota(jnp.int32, (1, span), 1) < reach, MASKED, 0.0).astype(F32)
    row = lax.broadcasted_iota(jnp.int32, (BLK, BLK), 0)
    col = lax.broadcasted_iota(jnp.int32, (BLK, BLK), 1)
    inner = (step > 0).astype(F32).astype(BF16)
    per_piece = heads // COLS
    q, k, v = (
        [part.astype(BF16) for part in split_heads(ref[...].astype(F32))] for ref in (q_ref, k_ref, v_ref)
    )
    inside = [
        lax.dot_general(q[h], k[h], (((1,), (1,)), ((), ())), preferred_element_type=F32) for h in range(heads)
    ]
    outs = []
    for h in range(heads):
        weight = jnp.where(col <= row, inside[h], 0.0) * (gain_ref[h, 0] * gain_factor(0, width))
        left = jnp.concatenate([weight.astype(BF16), q[h], q[h]], axis=1)
        j, i = h // per_piece, h % per_piece
        right = jnp.concatenate([v[h], cs[j, i], piece_refs[j][0, i] * inner], axis=0)
        outs.append(jnp.dot(left, right, preferred_element_type=F32))
    full = window_block(wq_ref, kh, vh, base, groups, bias) + join_heads(outs)
    out_ref[...] = full
    square_ref[0] = square_sums(full, heads)


def trunk_attention(where, gain, q, k, v, wq, pk, pv, ck, cv, cross, pieces, heads, groups):
    width = q.shape[1]
    blocks = q.shape[0] // (BLK * heads)
    at_block = pl.BlockSpec((BLK * heads, width), lambda i: (i, 0))
    whole = pl.BlockSpec((WIN * groups, width), lambda i: (0, 0))
    own = pl.BlockSpec(cross[0].shape, lambda i: (0, 0, 0))
    piece = pl.BlockSpec((1, heads // COLS, width, width), lambda i: (jnp.maximum(i - 1, 0), 0, 0, 0))
    return pl.pallas_call(
        functools.partial(trunk_kernel, heads, groups),
        grid=(blocks,),
        in_specs=[smem(), smem()] + [at_block] * 4 + [whole] * 4 + [own] * COLS + [piece] * COLS,
        out_specs=[at_block, pl.BlockSpec((1, 8, BLK), lambda i: (i, 0, 0))],
        out_shape=[
            jax.ShapeDtypeStruct(q.shape, F32),
            jax.ShapeDtypeStruct((blocks, 8, BLK), F32),
        ],
        scratch_shapes=[
            pltpu.VMEM((groups, 2 * WIN, width), BF16),
            pltpu.VMEM((groups, 2 * WIN, 2 * width), BF16),
            pltpu.VMEM((COLS, *cross[0].shape), BF16),
        ],
        compiler_params=params(),
        cost_estimate=attention_cost(blocks * BLK, heads, width, 2 * blocks * BLK * BLK * heads * 4 * width),
        name="trunk_attention",
    )(where, gain, q, k, v, wq, pk, pv, ck, cv, *cross, *pieces)


def near_kernel(groups, where_ref, fork_ref, q_ref, ck_ref, cv_ref, *rest):
    kv_refs, out_ref = rest[:COLS], rest[COLS]
    kh, vh, kt = rest[COLS + 1 :]
    step = pl.program_id(0)
    width = q_ref.shape[1]
    column = where_ref[0] & (COLS - 1)
    start = pl.multiple_of(fork_ref[0] * BLK, BLK)

    @pl.when(step == 0)
    def _():
        for i in range(COLS):
            kt[column ^ i] = kv_refs[i][...]
        vh[:, :, width:] = jnp.ones((groups, vh.shape[1], width), BF16)
        place(kt.at[0], vh, 0)
        place(kt.at[1], vh, WIN)
        place(kt.at[2], kh, 0)
        place(kt.at[3], kh, WIN)
        place(ck_ref, kh, pl.multiple_of(start + WIN, BLK))
        place(cv_ref, vh, pl.multiple_of(start + WIN, BLK))

    base = pl.multiple_of(start + step * BLK, BLK)
    out_ref[...] = window_block(q_ref, kh, vh, base, groups).astype(BF16)


def near_attention(where, fork, wq, ck, cv, kvs, heads, groups):
    width = wq.shape[1]
    steps = WIN // BLK
    at_block = pl.BlockSpec((BLK * heads, width), lambda i: (i, 0))
    whole = pl.BlockSpec((WIN * groups, width), lambda i: (0, 0))
    return pl.pallas_call(
        functools.partial(near_kernel, groups),
        grid=(steps,),
        in_specs=[smem(), smem(), at_block, whole, whole] + [whole] * COLS,
        out_specs=at_block,
        out_shape=jax.ShapeDtypeStruct((steps * BLK * heads, width), BF16),
        scratch_shapes=[
            pltpu.VMEM((groups, 3 * WIN, width), BF16),
            pltpu.VMEM((groups, 3 * WIN, 2 * width), BF16),
            pltpu.VMEM((COLS, WIN * groups, width), BF16),
        ],
        compiler_params=params(),
        cost_estimate=attention_cost(steps * BLK, heads, width),
        name="near_attention",
    )(where, fork, wq, ck, cv, *kvs)


def branch_kernel(heads, where_ref, fork_ref, q_hbm, near_hbm, far_hbm, *rest):
    piece_hbms = rest[:COLS]
    full_hbm, square_ref, qs, ws, fs, es, q_sems, w_sems, f_sems, e_sems = rest[COLS:]
    rows = BLK * heads
    blocks = qs.shape[0] // rows
    skip = WIN // BLK
    per_piece = heads // COLS
    column = where_ref[0] & (COLS - 1)
    ends = [
        pltpu.make_async_copy(piece_hbms[i].at[fork_ref[0]], es.at[column ^ i], e_sems.at[i]) for i in range(COLS)
    ]
    for copy in ends:
        copy.start()
    for b in range(blocks):
        block_copy(q_hbm, qs, q_sems, b, rows).start()
        if b < skip:
            block_copy(near_hbm, ws, w_sems, b, rows).start()
        else:
            block_copy(far_hbm, ws, w_sems, b, rows, b - skip).start()
    for copy in ends:
        copy.wait()

    def one_block(b, carry):
        block_copy(q_hbm, qs, q_sems, b, rows).wait()
        block_copy(near_hbm, ws, w_sems, b, rows, 0).wait()
        at = pl.ds(pl.multiple_of(b * rows, rows), rows)
        q = split_heads(qs[at, :].astype(F32))
        outs = [
            jnp.dot(q[h].astype(BF16), es[h // per_piece, h % per_piece], preferred_element_type=F32)
            for h in range(heads)
        ]
        full = ws[at, :].astype(F32) + join_heads(outs)
        fs[at, :] = full
        block_copy(fs, full_hbm, f_sems, b, rows).start()
        square_ref[b] = square_sums(full, heads)
        return carry

    lax.fori_loop(0, blocks, one_block, 0)
    for b in range(blocks):
        block_copy(fs, full_hbm, f_sems, b, rows).wait()


def branch_linear(where, fork, q, near, far, pieces, heads):
    width = q.shape[1]
    blocks = q.shape[0] // (BLK * heads)
    return pl.pallas_call(
        functools.partial(branch_kernel, heads),
        in_specs=[smem(), smem()] + [hbm()] * (3 + COLS),
        out_specs=[hbm(), vmem()],
        out_shape=[
            jax.ShapeDtypeStruct(q.shape, F32),
            jax.ShapeDtypeStruct((blocks, 8, BLK), F32),
        ],
        scratch_shapes=[
            pltpu.VMEM(q.shape, BF16),
            pltpu.VMEM(q.shape, BF16),
            pltpu.VMEM(q.shape, F32),
            pltpu.VMEM((COLS, *pieces[0].shape[1:]), BF16),
            pltpu.SemaphoreType.DMA((blocks,)),
            pltpu.SemaphoreType.DMA((blocks,)),
            pltpu.SemaphoreType.DMA((blocks,)),
            pltpu.SemaphoreType.DMA((COLS,)),
        ],
        compiler_params=params(),
        cost_estimate=pl.CostEstimate(
            flops=4 * blocks * BLK * heads * width * width, bytes_accessed=8 * q.size, transcendentals=0
        ),
        name="branch_linear",
    )(where, fork, q, near, far, *pieces)


def norm_kernel(heads, features, trunk_hbm, trunk_square, branch_hbm, branch_square, trunk_out, branch_out, held, done, in_sems, out_sems):
    rows = BLK * heads
    width = held.shape[1]
    trunk_blocks = trunk_hbm.shape[0] // rows
    branch_blocks = branch_hbm.shape[0] // rows

    def arrive(src, block, slot):
        return pltpu.make_async_copy(
            src.at[pl.ds(block * rows, rows)], held.at[pl.ds(slot * rows, rows)], in_sems.at[slot]
        )

    def leave(dst, block, slot):
        return pltpu.make_async_copy(
            done.at[pl.ds(slot * rows, rows)], dst.at[pl.ds(block * rows, rows)], out_sems.at[slot]
        )

    parts = ((branch_hbm, branch_square, branch_out, 0, branch_blocks), (trunk_hbm, trunk_square, trunk_out, branch_blocks, trunk_blocks))
    for src, _, _, first, blocks in parts:
        for b in range(blocks):
            arrive(src, b, first + b).start()
    for src, squares, dst, first, blocks in parts:

        def one_block(b, carry):
            slot = first + b
            arrive(src, b, slot).wait()
            at = pl.ds(pl.multiple_of(slot * rows, rows), rows)
            scale = lax.rsqrt(squares[b, 0:1, :] / features + 1e-06)
            scale = jnp.broadcast_to(scale, (width, BLK)).T
            full = held[at, :].reshape(BLK, heads, width)
            done[at, :] = (full * scale[:, None, :]).astype(BF16).reshape(rows, width)
            leave(dst, b, slot).start()
            return carry

        lax.fori_loop(0, blocks, one_block, 0)
    for _, _, dst, first, blocks in parts:
        for b in range(blocks):
            leave(dst, b, first + b).wait()


def normalize(trunk, trunk_square, branch, branch_square, heads, features):
    total = trunk.shape[0] + branch.shape[0]
    slots = total // (BLK * heads)
    return pl.pallas_call(
        functools.partial(norm_kernel, heads, features),
        in_specs=[hbm(), vmem(), hbm(), vmem()],
        out_specs=[hbm(), hbm()],
        out_shape=[jax.ShapeDtypeStruct(trunk.shape, BF16), jax.ShapeDtypeStruct(branch.shape, BF16)],
        scratch_shapes=[
            pltpu.VMEM((total, trunk.shape[1]), F32),
            pltpu.VMEM((total, trunk.shape[1]), BF16),
            pltpu.SemaphoreType.DMA((slots,)),
            pltpu.SemaphoreType.DMA((slots,)),
        ],
        compiler_params=params(),
        cost_estimate=pl.CostEstimate(
            flops=2 * (trunk.size + branch.size), bytes_accessed=6 * (trunk.size + branch.size), transcendentals=0
        ),
        name="normalize",
    )(trunk, trunk_square, branch, branch_square)


def shards(
    trunk_query,
    trunk_key,
    trunk_value,
    trunk_wquery,
    trunk_wkey,
    trunk_wvalue,
    branch_query,
    branch_wquery,
    branch_wkey,
    branch_wvalue,
    level_gain,
    fork_block,
):
    tokens, heads, width = trunk_query.shape
    groups = trunk_wkey.shape[1]
    depth = (tokens // BLK).bit_length() - 1
    count = lax.axis_size("seq")
    planes = count // COLS
    features = heads * lax.axis_size("head") * width
    me = lax.axis_index("seq")
    column, plane = me % COLS, me // COLS
    where = me.astype(jnp.int32).reshape(1)
    root = count - 1
    top = planes - 1

    def flat(x):
        return x.reshape(x.shape[0] * x.shape[1], x.shape[2])

    tq, tk, tv, twq = flat(trunk_query), flat(trunk_key), flat(trunk_value), flat(trunk_wquery)
    twk, twv = flat(trunk_wkey), flat(trunk_wvalue)
    bq, bwq, bwk, bwv = flat(branch_query), flat(branch_wquery), flat(branch_wkey), flat(branch_wvalue)

    def send(x, pairs):
        return lax.ppermute(x, "seq", pairs)

    def down(x):
        step = planes // 2
        while step:
            starts = [p for p in range(planes) if (top - p) % (2 * step) == 0 and p >= step]
            pairs = [(p * COLS + c, (p - step) * COLS + c) for p in starts for c in range(COLS)]
            got = send(x, pairs)
            hit = functools.reduce(jnp.logical_or, [plane == p - step for p in starts])
            x = jnp.where(hit, got, x)
            step //= 2
        return x

    def around(x):
        return [x] + [send(x, [(i, i ^ d) for i in range(count)]) for d in range(1, COLS)]

    def along(x):
        return [x] + [send(x, [(i, i ^ (d * COLS)) for i in range(count)]) for d in range(1, planes)]

    def swap(parts):
        return [parts[0]] + [send(parts[d], [(i, i ^ d) for i in range(count)]) for d in range(1, COLS)]

    half = COLS // 2
    got = send(twv, [(root - i, root - i - half) for i in range(half)])
    kv = down(jnp.where(column >= half, twk, got))
    shift = [(i, i + 1) for i in range(count - 1)]

    outs = block_sums(where, level_gain, tk, tv, heads, depth)
    pieces, shard_sum = outs[:COLS], outs[COLS:]
    sums = swap(shard_sum)
    local = pieces[COLS - 1]
    for c in range(COLS - 1):
        got = send(pieces[c], [(root, root - (COLS - 1) + c)])
        local = jnp.where(column == c, got, local)
    plane_sum, before = plane_sums(where, level_gain, sums, depth)
    plane_list = along(plane_sum)
    ends = jnp.concatenate([jnp.zeros_like(local[:1]), local], axis=0)
    pk, pv = send(twk, shift), send(twv, shift)

    far = far_attention(bwq, bwk, bwv, heads, groups)
    plane_list, far, kv, ends = lax.optimization_barrier((plane_list, far, kv, ends))
    ends = down((before[None] + ends.astype(F32)).astype(BF16))
    *cross, above = cross_sums(where, level_gain, sums, plane_list, depth)
    cross = swap(cross)
    kvs = around(kv)
    ends = around((ends.astype(F32) + above).astype(BF16))

    trunk_full, trunk_square = trunk_attention(
        where, level_gain, tq, tk, tv, twq, pk, pv, twk, twv, cross, pieces, heads, groups
    )
    trunk_full, kvs = lax.optimization_barrier((trunk_full, kvs))
    near = near_attention(where, fork_block, bwq, bwk, bwv, kvs, heads, groups)
    branch_full, branch_square = branch_linear(where, fork_block, bq, near, far, ends, heads)
    trunk_square, branch_square = lax.psum((trunk_square, branch_square), "head")
    trunk_out, branch_out = normalize(trunk_full, trunk_square, branch_full, branch_square, heads, features)
    return trunk_out.reshape(trunk_query.shape), branch_out.reshape(branch_query.shape)


def solution(mesh):
    rows = P("seq", "head", None)
    return jax.shard_map(
        shards,
        mesh=mesh,
        in_specs=(rows,) * 10 + (P("head", None), P("seq")),
        out_specs=(rows, rows),
        check_vma=False,
    )
```

```python
import functools
import math

import jax
import jax.numpy as jnp
from jax import lax
from jax.experimental import pallas as pl
from jax.experimental.pallas import tpu as pltpu
from jax.sharding import PartitionSpec as P

BLK = 128
WIN = 512
COLS = 4
MASKED = -1e30
F32 = jnp.float32
BF16 = jnp.bfloat16
VMEM_BYTES = 60 * 1024 * 1024
SMALL_BYTES = 28 * 1024 * 1024


def params(limit=VMEM_BYTES):
    return pltpu.CompilerParams(vmem_limit_bytes=limit)


def hbm():
    return pl.BlockSpec(memory_space=pltpu.HBM)


def vmem():
    return pl.BlockSpec(memory_space=pltpu.VMEM)


def block_copy(src, dst, sems, block, rows, src_block=None):
    src_block = block if src_block is None else src_block
    return pltpu.make_async_copy(
        src.at[pl.ds(src_block * rows, rows)], dst.at[pl.ds(block * rows, rows)], sems.at[block]
    )


def smem():
    return pl.BlockSpec(memory_space=pltpu.SMEM)


def gain_factor(level, width):
    return 1.0 / math.sqrt(width * BLK * 2 ** max(level - 1, 0))


def every(rows_ref, wide, count, each):
    return wide[pl.ds(each, rows_ref.shape[0] // count, stride=count), :].astype(BF16)


def state_kernel(depth, heads, where_ref, gain_ref, k_hbm, v_hbm, *rest):
    out_refs = rest[:COLS]
    local_ref, keys, values, kf, vf, levels, outs, key_sems, value_sems = rest[COLS:]
    rows, width = kf.shape
    each = heads // COLS
    column = where_ref[0] & (COLS - 1)
    copies = [
        (block_copy(k_hbm, keys, key_sems, b, rows), block_copy(v_hbm, values, value_sems, b, rows))
        for b in range(1 << depth)
    ]
    for pair in copies:
        for copy in pair:
            copy.start()
    for b, pair in enumerate(copies):
        for copy in pair:
            copy.wait()
        kf[...] = keys[b * rows : (b + 1) * rows].astype(F32)
        vf[...] = values[b * rows : (b + 1) * rows].astype(F32)
        for h in range(heads):
            k = kf[pl.ds(h, BLK, stride=heads), :].astype(BF16)
            v = vf[pl.ds(h, BLK, stride=heads), :].astype(BF16)
            merged = lax.dot_general(k, v, (((0,), (0,)), ((), ())), preferred_element_type=F32)
            before = None
            for bit in range(depth):
                if b >> bit & 1:
                    part = levels[bit, h] * (gain_ref[h, bit + 1] * gain_factor(bit + 1, width))
                    before = part if before is None else before + part
            carry = 0
            while b >> carry & 1:
                merged = merged + levels[carry, h]
                carry += 1
            if before is not None:
                before = before.astype(BF16)
                local_ref[b - 1, h] = before
                outs[column ^ (h // each), b, h % each] = before
            if carry < depth:
                levels[carry, h] = merged
            else:
                outs[column ^ (h // each), 0, h % each] = merged.astype(BF16)
    for d in range(COLS):
        out_refs[d][...] = outs[d]


def block_sums(where, gain, keys, values, heads, depth):
    blocks = 1 << depth
    rows, width = keys.shape[0] // blocks, keys.shape[1]
    quarter = (blocks, heads // COLS, width, width)
    return pl.pallas_call(
        functools.partial(state_kernel, depth, heads),
        in_specs=[smem(), smem(), hbm(), hbm()],
        out_specs=[vmem()] * (COLS + 1),
        out_shape=[jax.ShapeDtypeStruct(quarter, BF16)] * COLS
        + [jax.ShapeDtypeStruct((blocks - 1, heads, width, width), BF16)],
        scratch_shapes=[
            pltpu.VMEM(keys.shape, BF16),
            pltpu.VMEM(values.shape, BF16),
            pltpu.VMEM((rows, width), F32),
            pltpu.VMEM((rows, width), F32),
            pltpu.VMEM((depth, heads, width, width), F32),
            pltpu.VMEM((COLS, *quarter), BF16),
            pltpu.SemaphoreType.DMA((blocks,)),
            pltpu.SemaphoreType.DMA((blocks,)),
        ],
        compiler_params=params(),
        cost_estimate=pl.CostEstimate(
            flops=2 * keys.size * width, bytes_accessed=4 * keys.size + 2 * heads * width * width * blocks, transcendentals=0
        ),
        name="block_sums",
    )(where, gain, keys, values)


def in_plane(sums, column, weight):
    total = None
    for bit in range(COLS.bit_length() - 1):
        if column >> bit & 1:
            first = ((column >> bit) ^ 1) << bit
            part = functools.reduce(jnp.add, sums[first : first + (1 << bit)]) * weight(bit)
            total = part if total is None else total + part
    return total


def level_weight(gain_ref, head, depth, width, bit):
    return gain_ref[head, depth + bit + 1] * gain_factor(depth + bit + 1, width)


def in_order(where_ref, refs, held):
    for d, ref in enumerate(refs):
        held[(where_ref[0] & (COLS - 1)) ^ d] = ref[...]


def plane_kernel(depth, where_ref, gain_ref, *rest):
    part_refs, (plane_ref, ends_ref, sums_ref, held) = rest[:COLS], rest[COLS:]
    blocks, each, width = held.shape[1:4]
    first = (where_ref[0] & (COLS - 1)) * each
    in_order(where_ref, part_refs, held)
    for j in range(each):
        sums = [held[c, 0, j].astype(F32) for c in range(COLS)]
        plane_ref[j] = functools.reduce(jnp.add, sums).astype(BF16)
        before = in_plane(sums, COLS - 1, lambda bit: level_weight(gain_ref, first + j, depth, width, bit))
        ends_ref[0, j] = before.astype(BF16)
        for b in range(1, blocks):
            ends_ref[b, j] = (before + held[COLS - 1, b, j].astype(F32)).astype(BF16)
        for c in range(COLS):
            sums_ref[c, j] = held[c, 0, j]


def plane_sums(where, gain, parts, depth):
    blocks, *quarter = parts[0].shape
    return pl.pallas_call(
        functools.partial(plane_kernel, depth),
        in_specs=[smem(), smem()] + [vmem()] * COLS,
        out_specs=[vmem()] * 3,
        out_shape=[
            jax.ShapeDtypeStruct(tuple(quarter), BF16),
            jax.ShapeDtypeStruct((blocks, *quarter), BF16),
            jax.ShapeDtypeStruct((COLS, *quarter), BF16),
        ],
        scratch_shapes=[pltpu.VMEM((COLS, blocks, *quarter), BF16)],
        compiler_params=params(SMALL_BYTES),
        cost_estimate=pl.CostEstimate(flops=16 * parts[0].size, bytes_accessed=16 * parts[0].size, transcendentals=0),
        name="plane_sums",
    )(where, gain, *parts)


def cross_kernel(depth, planes, where_ref, gain_ref, *rest):
    held, plane_refs = rest[0], rest[1 : 1 + planes]
    out_refs, (top_ref, states, outs) = rest[1 + planes : 1 + COLS + planes], rest[1 + COLS + planes :]
    each, width = top_ref.shape[:2]
    col_bits = COLS.bit_length() - 1
    plane = where_ref[0] >> col_bits
    column = where_ref[0] & (COLS - 1)
    for d, ref in enumerate(plane_refs):
        states[plane ^ d] = ref[...]
    for j in range(each):
        head = column * each + j
        sums = [held[c, j].astype(F32) for c in range(COLS)]
        above = jnp.zeros((width, width), F32)
        top = jnp.zeros((width, width), F32)
        for s in range(planes - 1):
            state = states[s, j].astype(F32)
            share = jnp.float32(0.0)
            for bit in range(planes.bit_length() - 1):
                weight = level_weight(gain_ref, head, depth, width, col_bits + bit)
                inside = jnp.logical_and((plane >> bit) & 1 == 1, (plane >> bit) ^ 1 == s >> bit)
                share = share + jnp.where(inside, weight, 0.0)
                if ((planes - 1) >> bit) ^ 1 == s >> bit:
                    top = top + state * weight
            above = above + state * share
        top_ref[j] = top
        for c in range(COLS):
            before = in_plane(sums, c, lambda bit: level_weight(gain_ref, head, depth, width, bit))
            outs[column ^ c, j] = (above if before is None else above + before).astype(BF16)
    for d in range(COLS):
        out_refs[d][...] = outs[d]


def cross_sums(where, gain, sums, planes, depth):
    quarter = sums.shape[1:]
    return pl.pallas_call(
        functools.partial(cross_kernel, depth, len(planes)),
        in_specs=[smem(), smem()] + [vmem()] * (1 + len(planes)),
        out_specs=[vmem()] * (COLS + 1),
        out_shape=[jax.ShapeDtypeStruct(quarter, BF16)] * COLS + [jax.ShapeDtypeStruct(quarter, F32)],
        scratch_shapes=[
            pltpu.VMEM((len(planes), *quarter), BF16),
            pltpu.VMEM((COLS, *quarter), BF16),
        ],
        compiler_params=params(SMALL_BYTES),
        cost_estimate=pl.CostEstimate(flops=15 * sums.size, bytes_accessed=8 * sums.size, transcendentals=0),
        name="cross_sums",
    )(where, gain, sums, *planes)


def place(src_ref, wide, dst, start, groups):
    tokens = src_ref.shape[0] // groups
    wide[...] = src_ref[...].astype(F32)
    for g in range(groups):
        part = wide[pl.ds(g, tokens, stride=groups), :].astype(BF16)
        dst[g, pl.ds(start, tokens), : src_ref.shape[1]] = part


def split_groups(wide):
    rows, width = wide.shape
    pairs = wide.reshape(rows // 16, 16, width)
    low, high = pairs[:, :8], pairs[:, 8:]
    upper = lax.broadcasted_iota(jnp.int32, low.shape, 1) < 4
    first = jnp.where(upper, low, pltpu.roll(high, 4, 1))
    second = jnp.where(upper, pltpu.roll(low, 4, 1), high)
    return [part.reshape(rows // 2, width) for part in (first, second)]


def join_groups(first, second):
    rows, width = first.shape
    first, second = (part.reshape(rows // 8, 8, width) for part in (first, second))
    upper = lax.broadcasted_iota(jnp.int32, first.shape, 1) < 4
    low = jnp.where(upper, first, pltpu.roll(second, 4, 1))
    high = jnp.where(upper, pltpu.roll(first, 4, 1), second)
    return jnp.concatenate([low, high], axis=1).reshape(2 * rows, width)


def window_logits(queries, keys, token, share, bias):
    rows = queries.shape[0]
    logits = lax.dot_general(queries, keys, (((1,), (1,)), ((), ())), preferred_element_type=F32)
    row = token + lax.broadcasted_iota(jnp.int32, (rows, BLK), 0) // share
    col = lax.broadcasted_iota(jnp.int32, (rows, BLK), 1)
    late = col > row
    first = jnp.where(late, logits[:, :BLK], MASKED)
    last = jnp.where(late, MASKED, logits[:, -BLK:])
    logits = jnp.concatenate([first, logits[:, BLK:-BLK], last], axis=1)
    return logits if bias is None else logits + bias


def window_outputs(logits, values, width):
    top = jnp.max(logits, axis=1, keepdims=True)
    weights = jnp.exp2((logits - top) * (math.log2(math.e) / math.sqrt(width))).astype(BF16)
    both = jnp.dot(weights, values, preferred_element_type=F32)
    return both[:, :width] / both[:, width:]


def window_block(q_ref, kh, vh, base, groups, bias=None):
    width = q_ref.shape[1]
    span = WIN + BLK
    share = q_ref.shape[0] // BLK // groups
    parts = [part.astype(BF16) for part in split_groups(q_ref[...].astype(F32))]
    chunks = [(g, c) for g in range(groups) for c in range(0, BLK * share, BLK)]

    def logits_of(chunk):
        g, c = chunk
        return window_logits(parts[g][c : c + BLK], kh[g, pl.ds(base, span), :], c // share, share, bias)

    outs = []
    ahead = logits_of(chunks[0])
    for i, (g, c) in enumerate(chunks):
        now = ahead
        if i + 1 < len(chunks):
            ahead = logits_of(chunks[i + 1])
        outs.append(window_outputs(now, vh[g, pl.ds(base, span), :], width))
    half = len(outs) // 2
    return join_groups(jnp.concatenate(outs[:half], axis=0), jnp.concatenate(outs[half:], axis=0))


def square_sums(full, heads):
    tokens = full.shape[0] // heads
    row = lax.broadcasted_iota(jnp.int32, (tokens, full.shape[0]), 1) // heads
    mine = row == lax.broadcasted_iota(jnp.int32, (tokens, full.shape[0]), 0)
    sums = jnp.dot(mine.astype(BF16), (full * full).astype(BF16), preferred_element_type=F32)
    ones = jnp.ones((8, full.shape[1]), F32)
    return lax.dot_general(
        ones, sums, (((1,), (1,)), ((), ())), precision=lax.Precision.HIGHEST, preferred_element_type=F32
    )


def far_kernel(heads, groups, q_ref, pk_ref, pv_ref, ck_ref, cv_ref, out_ref, kf, kh, vh):
    step = pl.program_id(0)
    width = q_ref.shape[1]

    @pl.when(step == 0)
    def _():
        vh[:, :, width:] = jnp.ones((groups, vh.shape[1], width), BF16)
        place(pk_ref, kf, kh, 0, groups)
        place(ck_ref, kf, kh, WIN, groups)
        place(pv_ref, kf, vh, 0, groups)
        place(cv_ref, kf, vh, WIN, groups)

    out_ref[...] = window_block(q_ref, kh, vh, pl.multiple_of(step * BLK, BLK), groups).astype(BF16)


def attention_cost(tokens, heads, width, extra=0):
    span = WIN + BLK
    return pl.CostEstimate(
        flops=6 * tokens * heads * span * width + extra,
        bytes_accessed=12 * tokens * heads * width,
        transcendentals=tokens * heads * span,
    )


def far_attention(queries, keys, values, heads, groups):
    width = queries.shape[1]
    steps = queries.shape[0] // (BLK * heads) - WIN // BLK
    skip = WIN // BLK
    at_first = pl.BlockSpec((WIN * groups, width), lambda i: (0, 0))
    at_next = pl.BlockSpec((WIN * groups, width), lambda i: (1, 0))
    return pl.pallas_call(
        functools.partial(far_kernel, heads, groups),
        grid=(steps,),
        in_specs=[
            pl.BlockSpec((BLK * heads, width), lambda i: (i + skip, 0)),
            at_first,
            at_first,
            at_next,
            at_next,
        ],
        out_specs=pl.BlockSpec((BLK * heads, width), lambda i: (i, 0)),
        out_shape=jax.ShapeDtypeStruct((steps * BLK * heads, width), BF16),
        scratch_shapes=[
            pltpu.VMEM((WIN * groups, width), F32),
            pltpu.VMEM((groups, 2 * WIN, width), BF16),
            pltpu.VMEM((groups, 2 * WIN, 2 * width), BF16),
        ],
        compiler_params=params(),
        cost_estimate=attention_cost(steps * BLK, heads, width),
        name="far_attention",
    )(queries, keys, values, keys, values)


def trunk_kernel(heads, groups, first, where_ref, gain_ref, q_ref, k_ref, v_ref, wq_ref, pk_ref, pv_ref, ck_ref, cv_ref, local_ref, out_ref, nf, tf, sf, kf, kh, vh, of):
    block = pl.program_id(0) + first
    width = q_ref.shape[1]

    @pl.when(pl.program_id(0) == 0)
    def _():
        vh[:, :, width:] = jnp.ones((groups, vh.shape[1], width), BF16)
        place(pk_ref, kf, kh, 0, groups)
        place(ck_ref, kf, kh, WIN, groups)
        place(pv_ref, kf, vh, 0, groups)
        place(cv_ref, kf, vh, WIN, groups)

    nf[...] = q_ref[...].astype(F32)
    tf[...] = k_ref[...].astype(F32)
    sf[...] = v_ref[...].astype(F32)
    base = pl.multiple_of(block * BLK, BLK)
    reach = jnp.where(where_ref[0] == 0, WIN - block * BLK, 0)
    bias = jnp.where(lax.broadcasted_iota(jnp.int32, (1, WIN + BLK), 1) < reach, MASKED, 0.0).astype(F32)
    row = lax.broadcasted_iota(jnp.int32, (BLK, BLK), 0)
    col = lax.broadcasted_iota(jnp.int32, (BLK, BLK), 1)
    inner = (block > 0).astype(F32).astype(BF16)
    q = [every(q_ref, nf, heads, h) for h in range(heads)]
    inside = [
        lax.dot_general(q[h], every(k_ref, tf, heads, h), (((1,), (1,)), ((), ())), preferred_element_type=F32)
        for h in range(heads)
    ]
    for h in range(heads):
        weight = jnp.where(col <= row, inside[h], 0.0) * (gain_ref[h, 0] * gain_factor(0, width))
        left = jnp.concatenate([weight.astype(BF16), q[h]], axis=1)
        right = jnp.concatenate([every(v_ref, sf, heads, h), local_ref[0, h] * inner], axis=0)
        of[pl.ds(h, BLK, stride=heads), :] = jnp.dot(left, right, preferred_element_type=F32)
    out_ref[...] = window_block(wq_ref, kh, vh, base, groups, bias) + of[...]


def trunk_attention(where, gain, q, k, v, wq, pk, pv, ck, cv, local, heads, groups, first, steps):
    width = q.shape[1]
    rows = BLK * heads
    at_block = pl.BlockSpec((rows, width), lambda i: (i + first, 0))
    whole = pl.BlockSpec((WIN * groups, width), lambda i: (0, 0))
    before = pl.BlockSpec((1, heads, width, width), lambda i: (jnp.maximum(i + first - 1, 0), 0, 0, 0))
    wide = pltpu.VMEM((rows, width), F32)
    return pl.pallas_call(
        functools.partial(trunk_kernel, heads, groups, first),
        grid=(steps,),
        in_specs=[smem(), smem()] + [at_block] * 4 + [whole] * 4 + [before],
        out_specs=pl.BlockSpec((rows, width), lambda i: (i, 0)),
        out_shape=jax.ShapeDtypeStruct((steps * rows, width), F32),
        scratch_shapes=[
            wide,
            wide,
            wide,
            pltpu.VMEM((WIN * groups, width), F32),
            pltpu.VMEM((groups, 2 * WIN, width), BF16),
            pltpu.VMEM((groups, 2 * WIN, 2 * width), BF16),
            wide,
        ],
        compiler_params=params(),
        cost_estimate=attention_cost(steps * BLK, heads, width, 2 * steps * BLK * BLK * heads * 3 * width),
        name=f"trunk_attention_{first}",
    )(where, gain, q, k, v, wq, pk, pv, ck, cv, local)


def near_kernel(groups, where_ref, fork_ref, q_ref, ck_ref, cv_ref, *rest):
    kv_refs, out_ref = rest[:COLS], rest[COLS]
    kf, kh, vh, kt = rest[COLS + 1 :]
    step = pl.program_id(0)
    width = q_ref.shape[1]
    column = where_ref[0] & (COLS - 1)
    start = pl.multiple_of(fork_ref[0] * BLK, BLK)

    @pl.when(step == 0)
    def _():
        for i in range(COLS):
            kt[column ^ i] = kv_refs[i][...]
        vh[:, :, width:] = jnp.ones((groups, vh.shape[1], width), BF16)
        place(kt.at[0], kf, vh, 0, groups)
        place(kt.at[1], kf, vh, WIN, groups)
        place(kt.at[2], kf, kh, 0, groups)
        place(kt.at[3], kf, kh, WIN, groups)
        place(ck_ref, kf, kh, pl.multiple_of(start + WIN, BLK), groups)
        place(cv_ref, kf, vh, pl.multiple_of(start + WIN, BLK), groups)

    base = pl.multiple_of(start + step * BLK, BLK)
    out_ref[...] = window_block(q_ref, kh, vh, base, groups).astype(BF16)


def near_attention(where, fork, wq, ck, cv, kvs, heads, groups):
    width = wq.shape[1]
    steps = WIN // BLK
    at_block = pl.BlockSpec((BLK * heads, width), lambda i: (i, 0))
    whole = pl.BlockSpec((WIN * groups, width), lambda i: (0, 0))
    return pl.pallas_call(
        functools.partial(near_kernel, groups),
        grid=(steps,),
        in_specs=[smem(), smem(), at_block, whole, whole] + [whole] * COLS,
        out_specs=at_block,
        out_shape=jax.ShapeDtypeStruct((steps * BLK * heads, width), BF16),
        scratch_shapes=[
            pltpu.VMEM((WIN * groups, width), F32),
            pltpu.VMEM((groups, 3 * WIN, width), BF16),
            pltpu.VMEM((groups, 3 * WIN, 2 * width), BF16),
            pltpu.VMEM((COLS, WIN * groups, width), BF16),
        ],
        compiler_params=params(),
        cost_estimate=attention_cost(steps * BLK, heads, width),
        name="near_attention",
    )(where, fork, wq, ck, cv, *kvs)


def final_kernel(heads, parts, where_ref, fork_ref, bq_hbm, tq_hbm, *rest):
    window_hbms, trunk_hbms = rest[:2], rest[2 : 2 + parts]
    end_hbms, cross_hbms = rest[2 + parts : 2 + parts + COLS], rest[2 + parts + COLS : 2 + parts + 2 * COLS]
    branch_full, trunk_full, square_ref, qs, ws, ts, nf, of, fs, es, cs = rest[2 + parts + 2 * COLS :][:11]
    q_sems, w_sems, f_sems, e_sems, c_sems = rest[2 + parts + 2 * COLS :][11:]
    rows = BLK * heads
    branch_blocks, trunk_blocks = ws.shape[0] // rows, ts.shape[0] // rows
    each = heads // COLS
    column = where_ref[0] & (COLS - 1)
    states = [
        pltpu.make_async_copy(end_hbms[i].at[fork_ref[0]], es.at[column ^ i], e_sems.at[i]) for i in range(COLS)
    ] + [pltpu.make_async_copy(cross_hbms[i], cs.at[column ^ i], c_sems.at[i]) for i in range(COLS)]

    def query_copy(src, b, slot):
        return pltpu.make_async_copy(src.at[pl.ds(b * rows, rows)], qs.at[pl.ds(slot * rows, rows)], q_sems.at[slot])

    def other_copy(src, b, dst, place_of, slot):
        return pltpu.make_async_copy(
            src.at[pl.ds(b * rows, rows)], dst.at[pl.ds(place_of * rows, rows)], w_sems.at[slot]
        )

    def result_copy(b, dst, slot):
        return pltpu.make_async_copy(fs.at[pl.ds(slot * rows, rows)], dst.at[pl.ds(b * rows, rows)], f_sems.at[slot])

    for copy in states:
        copy.start()
    per_window = branch_blocks // 2
    per_trunk = trunk_blocks // parts
    for b in range(branch_blocks):
        query_copy(bq_hbm, b, b).start()
        other_copy(window_hbms[b // per_window], b % per_window, ws, b, b).start()
    for b in range(trunk_blocks):
        query_copy(tq_hbm, b, branch_blocks + b).start()
        other_copy(trunk_hbms[b // per_trunk], b % per_trunk, ts, b, branch_blocks + b).start()
    for copy in states:
        copy.wait()

    def rest_of(slot, window, states_ref):
        at = pl.ds(pl.multiple_of(slot * rows, rows), rows)
        nf[...] = qs[at, :].astype(F32)
        for h in range(heads):
            q = nf[pl.ds(h, BLK, stride=heads), :].astype(BF16)
            of[pl.ds(h, BLK, stride=heads), :] = jnp.dot(
                q, states_ref[h // each, h % each], preferred_element_type=F32
            )
        full = window.astype(F32) + of[...]
        fs[at, :] = full
        square_ref[slot] = square_sums(full, heads)

    def branch_block(b, carry):
        query_copy(bq_hbm, b, b).wait()
        other_copy(window_hbms[0], 0, ws, b, b).wait()
        rest_of(b, ws[pl.ds(pl.multiple_of(b * rows, rows), rows), :], es)
        result_copy(b, branch_full, b).start()
        return carry

    def trunk_block(b, carry):
        slot = branch_blocks + b
        query_copy(tq_hbm, b, slot).wait()
        other_copy(trunk_hbms[0], 0, ts, b, slot).wait()
        rest_of(slot, ts[pl.ds(pl.multiple_of(b * rows, rows), rows), :], cs)
        result_copy(b, trunk_full, slot).start()
        return carry

    lax.fori_loop(0, branch_blocks, branch_block, 0)
    lax.fori_loop(0, trunk_blocks, trunk_block, 0)
    for b in range(branch_blocks):
        result_copy(b, branch_full, b).wait()
    for b in range(trunk_blocks):
        result_copy(b, trunk_full, branch_blocks + b).wait()


def final_linear(where, fork, bq, tq, windows, trunks, ends, cross, heads):
    width = bq.shape[1]
    rows = BLK * heads
    total = bq.shape[0] + tq.shape[0]
    blocks = total // rows
    wide = pltpu.VMEM((rows, width), F32)
    quarter = cross[0].shape
    return pl.pallas_call(
        functools.partial(final_kernel, heads, len(trunks)),
        in_specs=[smem(), smem()] + [hbm()] * (4 + len(trunks) + 2 * COLS),
        out_specs=[hbm(), hbm(), vmem()],
        out_shape=[
            jax.ShapeDtypeStruct(bq.shape, F32),
            jax.ShapeDtypeStruct(tq.shape, F32),
            jax.ShapeDtypeStruct((blocks, 8, BLK), F32),
        ],
        scratch_shapes=[
            pltpu.VMEM((total, width), BF16),
            pltpu.VMEM(bq.shape, BF16),
            pltpu.VMEM(tq.shape, F32),
            wide,
            wide,
            pltpu.VMEM((total, width), F32),
            pltpu.VMEM((COLS, *quarter), BF16),
            pltpu.VMEM((COLS, *quarter), BF16),
            pltpu.SemaphoreType.DMA((blocks,)),
            pltpu.SemaphoreType.DMA((blocks,)),
            pltpu.SemaphoreType.DMA((blocks,)),
            pltpu.SemaphoreType.DMA((COLS,)),
            pltpu.SemaphoreType.DMA((COLS,)),
        ],
        compiler_params=params(),
        cost_estimate=pl.CostEstimate(flops=4 * total * width * width, bytes_accessed=8 * total * width, transcendentals=0),
        name="final_linear",
    )(where, fork, bq, tq, *windows, *trunks, *ends, *cross)


def norm_kernel(heads, features, trunk_hbm, branch_hbm, square_ref, other_ref, trunk_out, branch_out, held, done, in_sems, out_sems):
    rows = BLK * heads
    width = held.shape[1]
    trunk_blocks = trunk_hbm.shape[0] // rows
    branch_blocks = branch_hbm.shape[0] // rows

    def arrive(src, block, slot):
        return pltpu.make_async_copy(
            src.at[pl.ds(block * rows, rows)], held.at[pl.ds(slot * rows, rows)], in_sems.at[slot]
        )

    def leave(dst, block, slot):
        return pltpu.make_async_copy(
            done.at[pl.ds(slot * rows, rows)], dst.at[pl.ds(block * rows, rows)], out_sems.at[slot]
        )

    parts = ((branch_hbm, branch_out, 0, branch_blocks), (trunk_hbm, trunk_out, branch_blocks, trunk_blocks))
    for src, _, first, blocks in parts:
        for b in range(blocks):
            arrive(src, b, first + b).start()
    for src, dst, first, blocks in parts:

        def one_block(b, carry):
            slot = first + b
            arrive(src, b, slot).wait()
            at = pl.ds(pl.multiple_of(slot * rows, rows), rows)
            square = square_ref[slot, 0:1, :] + other_ref[slot, 0:1, :]
            scale = lax.rsqrt(square / features + 1e-06)
            scale = jnp.broadcast_to(scale, (width, BLK)).T
            full = held[at, :].reshape(BLK, heads, width)
            done[at, :] = (full * scale[:, None, :]).astype(BF16).reshape(rows, width)
            leave(dst, b, slot).start()
            return carry

        lax.fori_loop(0, blocks, one_block, 0)
    for _, dst, first, blocks in parts:
        for b in range(blocks):
            leave(dst, b, first + b).wait()


def normalize(trunk, branch, square, other, heads, features):
    total = trunk.shape[0] + branch.shape[0]
    slots = total // (BLK * heads)
    return pl.pallas_call(
        functools.partial(norm_kernel, heads, features),
        in_specs=[hbm(), hbm(), vmem(), vmem()],
        out_specs=[hbm(), hbm()],
        out_shape=[jax.ShapeDtypeStruct(trunk.shape, BF16), jax.ShapeDtypeStruct(branch.shape, BF16)],
        scratch_shapes=[
            pltpu.VMEM((total, trunk.shape[1]), F32),
            pltpu.VMEM((total, trunk.shape[1]), BF16),
            pltpu.SemaphoreType.DMA((slots,)),
            pltpu.SemaphoreType.DMA((slots,)),
        ],
        compiler_params=params(),
        cost_estimate=pl.CostEstimate(
            flops=2 * (trunk.size + branch.size), bytes_accessed=6 * (trunk.size + branch.size), transcendentals=0
        ),
        name="normalize",
    )(trunk, branch, square, other)


def shards(
    trunk_query,
    trunk_key,
    trunk_value,
    trunk_wquery,
    trunk_wkey,
    trunk_wvalue,
    branch_query,
    branch_wquery,
    branch_wkey,
    branch_wvalue,
    level_gain,
    fork_block,
):
    tokens, heads, width = trunk_query.shape
    groups = trunk_wkey.shape[1]
    depth = (tokens // BLK).bit_length() - 1
    count = lax.axis_size("seq")
    planes = count // COLS
    features = heads * lax.axis_size("head") * width
    me = lax.axis_index("seq")
    column, plane = me % COLS, me // COLS
    where = me.astype(jnp.int32).reshape(1)
    root = count - 1
    top = planes - 1

    def flat(x):
        return x.reshape(x.shape[0] * x.shape[1], x.shape[2])

    tq, tk, tv, twq = flat(trunk_query), flat(trunk_key), flat(trunk_value), flat(trunk_wquery)
    twk, twv = flat(trunk_wkey), flat(trunk_wvalue)
    bq, bwq, bwk, bwv = flat(branch_query), flat(branch_wquery), flat(branch_wkey), flat(branch_wvalue)

    def send(x, pairs):
        return lax.ppermute(x, "seq", pairs)

    def down_step(x, step):
        starts = [p for p in range(planes) if (top - p) % (2 * step) == 0 and p >= step]
        pairs = [(p * COLS + c, (p - step) * COLS + c) for p in starts for c in range(COLS)]
        got = send(x, pairs)
        hit = functools.reduce(jnp.logical_or, [plane == p - step for p in starts])
        return jnp.where(hit, got, x)

    def down_first(x):
        return down_step(x, planes // 2)

    def down_rest(x):
        step = planes // 4
        while step:
            x = down_step(x, step)
            step //= 2
        return x

    def around(x):
        return [x] + [send(x, [(i, i ^ d) for i in range(count)]) for d in range(1, COLS)]

    def along(x):
        return [x] + [send(x, [(i, i ^ (d * COLS)) for i in range(count)]) for d in range(1, planes)]

    def swap(parts):
        return [parts[0]] + [send(parts[d], [(i, i ^ d) for i in range(count)]) for d in range(1, COLS)]

    tie = lax.optimization_barrier

    half = COLS // 2
    got = send(twv, [(root - i, root - i - half) for i in range(half)])
    shift = [(i, i + 1) for i in range(count - 1)]
    pk, pv = send(twk, shift), send(twv, shift)
    *parts, local = block_sums(where, level_gain, tk, tv, heads, depth)

    bwq, parts, got = tie((bwq, parts, got))
    kv = jnp.where(column >= half, twk, got)
    far = far_attention(bwq, bwk, bwv, heads, groups)
    parts = swap(parts)
    kv = down_first(kv)
    parts, kv, far, pk, pv = tie((parts, kv, far, pk, pv))
    plane_sum, ends, sums = plane_sums(where, level_gain, parts, depth)

    blocks = tokens // BLK
    first = blocks // 2

    def trunk_part(start, steps):
        return trunk_attention(
            where, level_gain, tq, tk, tv, twq, pk, pv, twk, twv, local, heads, groups, start, steps
        )

    twq, plane_sum, ends = tie((twq, plane_sum, ends))
    trunk_a = trunk_part(0, first)
    plane_list = along(plane_sum)
    kv = down_rest(kv)
    ends = down_first(ends)
    plane_list, kv, ends, trunk_a, twq = tie((plane_list, kv, ends, trunk_a, twq))
    *cross, above = cross_sums(where, level_gain, sums, plane_list, depth)

    twq, cross = tie((twq, cross))
    trunk_b = trunk_part(first, blocks - first)
    kvs = around(kv)
    ends = down_rest(ends)
    kvs, ends, trunk_b, bwq = tie((kvs, ends, trunk_b, bwq))
    ends = (ends.astype(F32) + above).astype(BF16)

    bwq, ends = tie((bwq, ends))
    near = near_attention(where, fork_block, bwq, bwk, bwv, kvs, heads, groups)
    ends = around(ends)
    cross = swap(cross)
    branch_full, trunk_full, square = final_linear(
        where, fork_block, bq, tq, (near, far), (trunk_a, trunk_b), ends, cross, heads
    )
    other = lax.ppermute(square, "head", [(0, 1), (1, 0)])
    trunk_out, branch_out = normalize(trunk_full, branch_full, square, other, heads, features)
    return trunk_out.reshape(trunk_query.shape), branch_out.reshape(branch_query.shape)


def solution(mesh):
    rows = P("seq", "head", None)
    return jax.shard_map(
        shards,
        mesh=mesh,
        in_specs=(rows,) * 10 + (P("head", None), P("seq")),
        out_specs=(rows, rows),
        check_vma=False,
    )
```

```python
import functools
import math

import jax
import jax.numpy as jnp
from jax import lax
from jax.experimental import pallas as pl
from jax.experimental.pallas import tpu as pltpu
from jax.sharding import PartitionSpec as P

BLK = 128
WIN = 512
COLS = 4
MASKED = -1e30
F32 = jnp.float32
BF16 = jnp.bfloat16
VMEM_BYTES = 60 * 1024 * 1024
SMALL_BYTES = 28 * 1024 * 1024


def params(limit=VMEM_BYTES):
    return pltpu.CompilerParams(vmem_limit_bytes=limit)


def hbm():
    return pl.BlockSpec(memory_space=pltpu.HBM)


def vmem():
    return pl.BlockSpec(memory_space=pltpu.VMEM)


def block_copy(src, dst, sems, block, rows, src_block=None):
    src_block = block if src_block is None else src_block
    return pltpu.make_async_copy(
        src.at[pl.ds(src_block * rows, rows)], dst.at[pl.ds(block * rows, rows)], sems.at[block]
    )


def smem():
    return pl.BlockSpec(memory_space=pltpu.SMEM)


def gain_factor(level, width):
    return 1.0 / math.sqrt(width * BLK * 2 ** max(level - 1, 0))


def every(rows_ref, wide, count, each):
    return wide[pl.ds(each, rows_ref.shape[0] // count, stride=count), :].astype(BF16)


def masked_copies(x, count):
    rows, width = x.shape
    tiles = x.reshape(rows // 16, 16, width)
    row = lax.broadcasted_iota(jnp.int32, (16, width), 0) & (count - 1)
    kept = [tiles * jnp.where(row == m, 1.0, 0.0).astype(BF16)[None] for m in range(count)]
    return jnp.concatenate([part.reshape(rows, width) for part in kept], axis=1)


def state_kernel(depth, heads, gain_ref, k_hbm, v_hbm, *rest):
    piece_refs = rest[:COLS]
    local_ref, sum_ref, keys, values, levels, key_sems, value_sems = rest[COLS:]
    width = keys.shape[1]
    rows = keys.shape[0] >> depth
    each = heads // COLS
    copies = [
        (block_copy(k_hbm, keys, key_sems, b, rows), block_copy(v_hbm, values, value_sems, b, rows))
        for b in range(1 << depth)
    ]
    for pair in copies:
        for copy in pair:
            copy.start()
    for b, pair in enumerate(copies):
        for copy in pair:
            copy.wait()
        states = lax.dot_general(
            keys[b * rows : (b + 1) * rows],
            masked_copies(values[b * rows : (b + 1) * rows], heads),
            (((0,), (0,)), ((), ())),
            preferred_element_type=F32,
        )
        for h in range(heads):
            merged = states[:, h * width : (h + 1) * width]
            before = None
            for bit in range(depth):
                if b >> bit & 1:
                    part = levels[bit, h] * (gain_ref[h, bit + 1] * gain_factor(bit + 1, width))
                    before = part if before is None else before + part
            carry = 0
            while b >> carry & 1:
                merged = merged + levels[carry, h]
                carry += 1
            if before is not None:
                before = before.astype(BF16)
                local_ref[b - 1, h] = before
                piece_refs[h // each][b - 1, h % each] = before
            if carry < depth:
                levels[carry, h] = merged
            else:
                sum_ref[h // each, h % each] = merged.astype(BF16)


def block_sums(gain, keys, values, heads, depth):
    blocks = 1 << depth
    width = keys.shape[1]
    each = heads // COLS
    return pl.pallas_call(
        functools.partial(state_kernel, depth, heads),
        in_specs=[smem(), hbm(), hbm()],
        out_specs=[vmem()] * (COLS + 2),
        out_shape=[jax.ShapeDtypeStruct((blocks - 1, each, width, width), BF16)] * COLS
        + [
            jax.ShapeDtypeStruct((blocks - 1, heads, width, width), BF16),
            jax.ShapeDtypeStruct((COLS, each, width, width), BF16),
        ],
        scratch_shapes=[
            pltpu.VMEM(keys.shape, BF16),
            pltpu.VMEM(values.shape, BF16),
            pltpu.VMEM((depth, heads, width, width), F32),
            pltpu.SemaphoreType.DMA((blocks,)),
            pltpu.SemaphoreType.DMA((blocks,)),
        ],
        compiler_params=params(),
        cost_estimate=pl.CostEstimate(
            flops=2 * keys.size * width, bytes_accessed=4 * keys.size + 2 * heads * width * width * blocks, transcendentals=0
        ),
        name="block_sums",
    )(gain, keys, values)


def in_plane(sums, column, weight):
    total = None
    for bit in range(COLS.bit_length() - 1):
        if column >> bit & 1:
            first = ((column >> bit) ^ 1) << bit
            part = functools.reduce(jnp.add, sums[first : first + (1 << bit)]) * weight(bit)
            total = part if total is None else total + part
    return total


def level_weight(gain_ref, head, depth, width, bit):
    return gain_ref[head, depth + bit + 1] * gain_factor(depth + bit + 1, width)


def plane_kernel(depth, where_ref, gain_ref, sums_ref, local_ref, plane_ref, ends_ref):
    each, width = sums_ref.shape[1], sums_ref.shape[2]
    first = (where_ref[0] & (COLS - 1)) * each
    for j in range(each):
        sums = [sums_ref[c, j].astype(F32) for c in range(COLS)]
        whole = functools.reduce(jnp.add, sums).astype(BF16)
        for p in range(plane_ref.shape[0]):
            plane_ref[p, j] = whole
        before = in_plane(sums, COLS - 1, lambda bit: level_weight(gain_ref, first + j, depth, width, bit))
        ends_ref[0, j] = before.astype(BF16)
        for f in range(local_ref.shape[0]):
            ends_ref[f + 1, j] = (before + local_ref[f, j].astype(F32)).astype(BF16)


def plane_sums(where, gain, sums, local, planes, depth):
    quarter = sums.shape[1:]
    return pl.pallas_call(
        functools.partial(plane_kernel, depth),
        in_specs=[smem(), smem(), vmem(), vmem()],
        out_specs=[vmem(), vmem()],
        out_shape=[
            jax.ShapeDtypeStruct((planes, *quarter), BF16),
            jax.ShapeDtypeStruct((local.shape[0] + 1, *quarter), BF16),
        ],
        compiler_params=params(SMALL_BYTES),
        cost_estimate=pl.CostEstimate(flops=4 * sums.size, bytes_accessed=8 * sums.size, transcendentals=0),
        name="plane_sums",
    )(where, gain, sums, local)


def cross_kernel(depth, where_ref, gain_ref, sums_ref, planes_ref, out_ref, top_ref):
    each, width = sums_ref.shape[1], sums_ref.shape[2]
    planes = planes_ref.shape[0]
    col_bits = COLS.bit_length() - 1
    plane = where_ref[0] >> col_bits
    first = (where_ref[0] & (COLS - 1)) * each
    for j in range(each):
        sums = [sums_ref[c, j].astype(F32) for c in range(COLS)]
        above = jnp.zeros((width, width), F32)
        top = jnp.zeros((width, width), F32)
        for s in range(planes - 1):
            state = planes_ref[s, j].astype(F32)
            share = jnp.float32(0.0)
            for bit in range(planes.bit_length() - 1):
                weight = level_weight(gain_ref, first + j, depth, width, col_bits + bit)
                held = jnp.logical_and((plane >> bit) & 1 == 1, (plane >> bit) ^ 1 == s >> bit)
                share = share + jnp.where(held, weight, 0.0)
                if ((planes - 1) >> bit) ^ 1 == s >> bit:
                    top = top + state * weight
            above = above + state * share
        top_ref[j] = top
        for c in range(COLS):
            before = in_plane(sums, c, lambda bit: level_weight(gain_ref, first + j, depth, width, bit))
            out_ref[c, j] = (above if before is None else above + before).astype(BF16)


def cross_sums(where, gain, sums, planes, depth):
    return pl.pallas_call(
        functools.partial(cross_kernel, depth),
        in_specs=[smem(), smem(), vmem(), vmem()],
        out_specs=[vmem(), vmem()],
        out_shape=[jax.ShapeDtypeStruct(sums.shape, BF16), jax.ShapeDtypeStruct(sums.shape[1:], F32)],
        compiler_params=params(SMALL_BYTES),
        cost_estimate=pl.CostEstimate(flops=20 * sums.size, bytes_accessed=8 * sums.size, transcendentals=0),
        name="cross_sums",
    )(where, gain, sums, planes)


def place(src_ref, wide, dst, start, groups):
    tokens = src_ref.shape[0] // groups
    wide[...] = src_ref[...].astype(F32)
    for g in range(groups):
        part = wide[pl.ds(g, tokens, stride=groups), :].astype(BF16)
        dst[g, pl.ds(start, tokens), : src_ref.shape[1]] = part


def split_groups(wide):
    rows, width = wide.shape
    pairs = wide.reshape(rows // 16, 16, width)
    low, high = pairs[:, :8], pairs[:, 8:]
    upper = lax.broadcasted_iota(jnp.int32, low.shape, 1) < 4
    first = jnp.where(upper, low, pltpu.roll(high, 4, 1))
    second = jnp.where(upper, pltpu.roll(low, 4, 1), high)
    return [part.reshape(rows // 2, width) for part in (first, second)]


def join_groups(first, second):
    rows, width = first.shape
    first, second = (part.reshape(rows // 8, 8, width) for part in (first, second))
    upper = lax.broadcasted_iota(jnp.int32, first.shape, 1) < 4
    low = jnp.where(upper, first, pltpu.roll(second, 4, 1))
    high = jnp.where(upper, pltpu.roll(first, 4, 1), second)
    return jnp.concatenate([low, high], axis=1).reshape(2 * rows, width)


def window_logits(queries, keys, token, share, bias):
    rows = queries.shape[0]
    logits = lax.dot_general(queries, keys, (((1,), (1,)), ((), ())), preferred_element_type=F32)
    row = token + lax.broadcasted_iota(jnp.int32, (rows, BLK), 0) // share
    col = lax.broadcasted_iota(jnp.int32, (rows, BLK), 1)
    late = col > row
    first = jnp.where(late, logits[:, :BLK], MASKED)
    last = jnp.where(late, MASKED, logits[:, -BLK:])
    logits = jnp.concatenate([first, logits[:, BLK:-BLK], last], axis=1)
    return logits if bias is None else logits + bias


def window_outputs(logits, values, width):
    top = jnp.max(logits, axis=1, keepdims=True)
    weights = jnp.exp2((logits - top) * (math.log2(math.e) / math.sqrt(width))).astype(BF16)
    both = jnp.dot(weights, values, preferred_element_type=F32)
    return both[:, :width] / both[:, width:]


def window_block(q_ref, kh, vh, base, groups, bias=None):
    width = q_ref.shape[1]
    span = WIN + BLK
    share = q_ref.shape[0] // BLK // groups
    parts = [part.astype(BF16) for part in split_groups(q_ref[...].astype(F32))]
    chunks = [(g, c) for g in range(groups) for c in range(0, BLK * share, BLK)]

    def logits_of(chunk):
        g, c = chunk
        return window_logits(parts[g][c : c + BLK], kh[g, pl.ds(base, span), :], c // share, share, bias)

    outs = []
    ahead = logits_of(chunks[0])
    for i, (g, c) in enumerate(chunks):
        now = ahead
        if i + 1 < len(chunks):
            ahead = logits_of(chunks[i + 1])
        outs.append(window_outputs(now, vh[g, pl.ds(base, span), :], width))
    half = len(outs) // 2
    return join_groups(jnp.concatenate(outs[:half], axis=0), jnp.concatenate(outs[half:], axis=0))


def token_rows(tokens, heads):
    row = lax.broadcasted_iota(jnp.int32, (tokens, tokens * heads), 1) // heads
    return (row == lax.broadcasted_iota(jnp.int32, (tokens, tokens * heads), 0)).astype(F32).astype(BF16)


def square_sums(full, mine):
    sums = jnp.dot(mine, (full * full).astype(BF16), preferred_element_type=F32)
    ones = jnp.ones((8, full.shape[1]), F32)
    return lax.dot_general(
        ones, sums, (((1,), (1,)), ((), ())), precision=lax.Precision.HIGHEST, preferred_element_type=F32
    )


def far_kernel(heads, groups, q_ref, pk_ref, pv_ref, ck_ref, cv_ref, out_ref, kf, kh, vh):
    step = pl.program_id(0)
    width = q_ref.shape[1]

    @pl.when(step == 0)
    def _():
        vh[:, :, width:] = jnp.ones((groups, vh.shape[1], width), BF16)
        place(pk_ref, kf, kh, 0, groups)
        place(ck_ref, kf, kh, WIN, groups)
        place(pv_ref, kf, vh, 0, groups)
        place(cv_ref, kf, vh, WIN, groups)

    out_ref[...] = window_block(q_ref, kh, vh, pl.multiple_of(step * BLK, BLK), groups).astype(BF16)


def attention_cost(tokens, heads, width, extra=0):
    span = WIN + BLK
    return pl.CostEstimate(
        flops=6 * tokens * heads * span * width + extra,
        bytes_accessed=12 * tokens * heads * width,
        transcendentals=tokens * heads * span,
    )


def far_attention(queries, keys, values, heads, groups):
    width = queries.shape[1]
    steps = queries.shape[0] // (BLK * heads) - WIN // BLK
    skip = WIN // BLK
    at_first = pl.BlockSpec((WIN * groups, width), lambda i: (0, 0))
    at_next = pl.BlockSpec((WIN * groups, width), lambda i: (1, 0))
    return pl.pallas_call(
        functools.partial(far_kernel, heads, groups),
        grid=(steps,),
        in_specs=[
            pl.BlockSpec((BLK * heads, width), lambda i: (i + skip, 0)),
            at_first,
            at_first,
            at_next,
            at_next,
        ],
        out_specs=pl.BlockSpec((BLK * heads, width), lambda i: (i, 0)),
        out_shape=jax.ShapeDtypeStruct((steps * BLK * heads, width), BF16),
        scratch_shapes=[
            pltpu.VMEM((WIN * groups, width), F32),
            pltpu.VMEM((groups, 2 * WIN, width), BF16),
            pltpu.VMEM((groups, 2 * WIN, 2 * width), BF16),
        ],
        compiler_params=params(),
        cost_estimate=attention_cost(steps * BLK, heads, width),
        name="far_attention",
    )(queries, keys, values, keys, values)


def trunk_kernel(heads, groups, first, where_ref, gain_ref, q_ref, k_ref, v_ref, wq_ref, pk_ref, pv_ref, ck_ref, cv_ref, local_ref, out_ref, nf, tf, sf, kf, kh, vh, of):
    block = pl.program_id(0) + first
    width = q_ref.shape[1]

    @pl.when(pl.program_id(0) == 0)
    def _():
        vh[:, :, width:] = jnp.ones((groups, vh.shape[1], width), BF16)
        place(pk_ref, kf, kh, 0, groups)
        place(ck_ref, kf, kh, WIN, groups)
        place(pv_ref, kf, vh, 0, groups)
        place(cv_ref, kf, vh, WIN, groups)

    nf[...] = q_ref[...].astype(F32)
    tf[...] = k_ref[...].astype(F32)
    sf[...] = v_ref[...].astype(F32)
    base = pl.multiple_of(block * BLK, BLK)
    reach = jnp.where(where_ref[0] == 0, WIN - block * BLK, 0)
    bias = jnp.where(lax.broadcasted_iota(jnp.int32, (1, WIN + BLK), 1) < reach, MASKED, 0.0).astype(F32)
    row = lax.broadcasted_iota(jnp.int32, (BLK, BLK), 0)
    col = lax.broadcasted_iota(jnp.int32, (BLK, BLK), 1)
    inner = (block > 0).astype(F32).astype(BF16)
    q = [every(q_ref, nf, heads, h) for h in range(heads)]
    inside = [
        lax.dot_general(q[h], every(k_ref, tf, heads, h), (((1,), (1,)), ((), ())), preferred_element_type=F32)
        for h in range(heads)
    ]
    for h in range(heads):
        weight = jnp.where(col <= row, inside[h], 0.0) * (gain_ref[h, 0] * gain_factor(0, width))
        left = jnp.concatenate([weight.astype(BF16), q[h]], axis=1)
        right = jnp.concatenate([every(v_ref, sf, heads, h), local_ref[0, h] * inner], axis=0)
        of[pl.ds(h, BLK, stride=heads), :] = jnp.dot(left, right, preferred_element_type=F32)
    out_ref[...] = window_block(wq_ref, kh, vh, base, groups, bias) + of[...]


def trunk_attention(where, gain, q, k, v, wq, pk, pv, ck, cv, local, heads, groups, first, steps):
    width = q.shape[1]
    rows = BLK * heads
    at_block = pl.BlockSpec((rows, width), lambda i: (i + first, 0))
    whole = pl.BlockSpec((WIN * groups, width), lambda i: (0, 0))
    before = pl.BlockSpec((1, heads, width, width), lambda i: (jnp.maximum(i + first - 1, 0), 0, 0, 0))
    wide = pltpu.VMEM((rows, width), F32)
    return pl.pallas_call(
        functools.partial(trunk_kernel, heads, groups, first),
        grid=(steps,),
        in_specs=[smem(), smem()] + [at_block] * 4 + [whole] * 4 + [before],
        out_specs=pl.BlockSpec((rows, width), lambda i: (i, 0)),
        out_shape=jax.ShapeDtypeStruct((steps * rows, width), F32),
        scratch_shapes=[
            wide,
            wide,
            wide,
            pltpu.VMEM((WIN * groups, width), F32),
            pltpu.VMEM((groups, 2 * WIN, width), BF16),
            pltpu.VMEM((groups, 2 * WIN, 2 * width), BF16),
            wide,
        ],
        compiler_params=params(),
        cost_estimate=attention_cost(steps * BLK, heads, width, 2 * steps * BLK * BLK * heads * 3 * width),
        name=f"trunk_attention_{first}",
    )(where, gain, q, k, v, wq, pk, pv, ck, cv, local)


def near_kernel(groups, where_ref, fork_ref, q_ref, ck_ref, cv_ref, *rest):
    kv_refs, out_ref = rest[:COLS], rest[COLS]
    kf, kh, vh, kt = rest[COLS + 1 :]
    step = pl.program_id(0)
    width = q_ref.shape[1]
    column = where_ref[0] & (COLS - 1)
    start = pl.multiple_of(fork_ref[0] * BLK, BLK)

    @pl.when(step == 0)
    def _():
        for i in range(COLS):
            kt[column ^ i] = kv_refs[i][...]
        vh[:, :, width:] = jnp.ones((groups, vh.shape[1], width), BF16)
        place(kt.at[0], kf, vh, 0, groups)
        place(kt.at[1], kf, vh, WIN, groups)
        place(kt.at[2], kf, kh, 0, groups)
        place(kt.at[3], kf, kh, WIN, groups)
        place(ck_ref, kf, kh, pl.multiple_of(start + WIN, BLK), groups)
        place(cv_ref, kf, vh, pl.multiple_of(start + WIN, BLK), groups)

    base = pl.multiple_of(start + step * BLK, BLK)
    out_ref[...] = window_block(q_ref, kh, vh, base, groups).astype(BF16)


def near_attention(where, fork, wq, ck, cv, kvs, heads, groups):
    width = wq.shape[1]
    steps = WIN // BLK
    at_block = pl.BlockSpec((BLK * heads, width), lambda i: (i, 0))
    whole = pl.BlockSpec((WIN * groups, width), lambda i: (0, 0))
    return pl.pallas_call(
        functools.partial(near_kernel, groups),
        grid=(steps,),
        in_specs=[smem(), smem(), at_block, whole, whole] + [whole] * COLS,
        out_specs=at_block,
        out_shape=jax.ShapeDtypeStruct((steps * BLK * heads, width), BF16),
        scratch_shapes=[
            pltpu.VMEM((WIN * groups, width), F32),
            pltpu.VMEM((groups, 3 * WIN, width), BF16),
            pltpu.VMEM((groups, 3 * WIN, 2 * width), BF16),
            pltpu.VMEM((COLS, WIN * groups, width), BF16),
        ],
        compiler_params=params(),
        cost_estimate=attention_cost(steps * BLK, heads, width),
        name="near_attention",
    )(where, fork, wq, ck, cv, *kvs)


def final_kernel(heads, where_ref, fork_ref, bq_hbm, tq_hbm, near_hbm, far_hbm, trunk_hbm, cross_hbm, *rest):
    end_hbms, (branch_full, trunk_full, square_ref, qs, ws, ts, fs, es, cs, stacked, mine) = rest[:COLS], rest[COLS : COLS + 11]
    q_sems, w_sems, f_sems, e_sems = rest[COLS + 11 :]
    window_hbms = (near_hbm, far_hbm)
    rows = BLK * heads
    branch_blocks, trunk_blocks = ws.shape[0] // rows, ts.shape[0] // rows
    each = heads // COLS
    column = where_ref[0] & (COLS - 1)
    states = [
        pltpu.make_async_copy(end_hbms[i].at[fork_ref[0]], es.at[column ^ i], e_sems.at[i]) for i in range(COLS)
    ] + [pltpu.make_async_copy(cross_hbm, cs, e_sems.at[COLS])]

    def query_copy(src, b, slot):
        return pltpu.make_async_copy(src.at[pl.ds(b * rows, rows)], qs.at[pl.ds(slot * rows, rows)], q_sems.at[slot])

    def other_copy(src, b, dst, place_of, slot):
        return pltpu.make_async_copy(
            src.at[pl.ds(b * rows, rows)], dst.at[pl.ds(place_of * rows, rows)], w_sems.at[slot]
        )

    def result_copy(b, dst, slot):
        return pltpu.make_async_copy(fs.at[pl.ds(slot * rows, rows)], dst.at[pl.ds(b * rows, rows)], f_sems.at[slot])

    for copy in states:
        copy.start()
    per_window = branch_blocks // 2
    for b in range(branch_blocks):
        query_copy(bq_hbm, b, b).start()
        other_copy(window_hbms[b // per_window], b % per_window, ws, b, b).start()
    for b in range(trunk_blocks):
        query_copy(tq_hbm, b, branch_blocks + b).start()
        other_copy(trunk_hbm, b, ts, b, branch_blocks + b).start()
    mine[...] = token_rows(BLK, heads)
    for copy in states:
        copy.wait()
    width = qs.shape[1]
    for i, held in enumerate((es, cs)):
        for h in range(heads):
            m, n = h % COLS, h // COLS
            stacked[i, m * width : (m + 1) * width, n * width : (n + 1) * width] = held[h // each, h % each]

    def rest_of(slot, window, which):
        at = pl.ds(pl.multiple_of(slot * rows, rows), rows)
        both = jnp.dot(masked_copies(qs[at, :], COLS), stacked[which], preferred_element_type=F32)
        upper = (lax.broadcasted_iota(jnp.int32, (rows, width), 0) & (heads - 1)) < COLS
        full = window.astype(F32) + jnp.where(upper, both[:, :width], both[:, width:])
        fs[at, :] = full
        square_ref[slot] = square_sums(full, mine[...])

    def branch_block(b, carry):
        query_copy(bq_hbm, b, b).wait()
        other_copy(window_hbms[0], 0, ws, b, b).wait()
        rest_of(b, ws[pl.ds(pl.multiple_of(b * rows, rows), rows), :], 0)
        result_copy(b, branch_full, b).start()
        return carry

    def trunk_block(b, carry):
        slot = branch_blocks + b
        query_copy(tq_hbm, b, slot).wait()
        other_copy(trunk_hbm, 0, ts, b, slot).wait()
        rest_of(slot, ts[pl.ds(pl.multiple_of(b * rows, rows), rows), :], 1)
        result_copy(b, trunk_full, slot).start()
        return carry

    lax.fori_loop(0, branch_blocks, branch_block, 0)
    lax.fori_loop(0, trunk_blocks, trunk_block, 0)
    for b in range(branch_blocks):
        result_copy(b, branch_full, b).wait()
    for b in range(trunk_blocks):
        result_copy(b, trunk_full, branch_blocks + b).wait()


def final_linear(where, fork, bq, tq, near, far, trunk, cross, ends, heads):
    width = bq.shape[1]
    rows = BLK * heads
    total = bq.shape[0] + tq.shape[0]
    blocks = total // rows
    return pl.pallas_call(
        functools.partial(final_kernel, heads),
        in_specs=[smem(), smem()] + [hbm()] * (6 + COLS),
        out_specs=[hbm(), hbm(), vmem()],
        out_shape=[
            jax.ShapeDtypeStruct(bq.shape, F32),
            jax.ShapeDtypeStruct(tq.shape, F32),
            jax.ShapeDtypeStruct((blocks, 8, BLK), F32),
        ],
        scratch_shapes=[
            pltpu.VMEM((total, width), BF16),
            pltpu.VMEM(bq.shape, BF16),
            pltpu.VMEM(tq.shape, F32),
            pltpu.VMEM((total, width), F32),
            pltpu.VMEM(cross.shape, BF16),
            pltpu.VMEM(cross.shape, BF16),
            pltpu.VMEM((2, COLS * width, heads // COLS * width), BF16),
            pltpu.VMEM((BLK, rows), BF16),
            pltpu.SemaphoreType.DMA((blocks,)),
            pltpu.SemaphoreType.DMA((blocks,)),
            pltpu.SemaphoreType.DMA((blocks,)),
            pltpu.SemaphoreType.DMA((COLS + 1,)),
        ],
        compiler_params=params(),
        cost_estimate=pl.CostEstimate(flops=4 * total * width * width, bytes_accessed=8 * total * width, transcendentals=0),
        name="final_linear",
    )(where, fork, bq, tq, near, far, trunk, cross, *ends)


def norm_kernel(heads, features, trunk_hbm, branch_hbm, square_ref, other_ref, trunk_out, branch_out, held, done, in_sems, out_sems):
    rows = BLK * heads
    width = held.shape[1]
    trunk_blocks = trunk_hbm.shape[0] // rows
    branch_blocks = branch_hbm.shape[0] // rows

    def arrive(src, block, slot):
        return pltpu.make_async_copy(
            src.at[pl.ds(block * rows, rows)], held.at[pl.ds(slot * rows, rows)], in_sems.at[slot]
        )

    def leave(dst, block, slot):
        return pltpu.make_async_copy(
            done.at[pl.ds(slot * rows, rows)], dst.at[pl.ds(block * rows, rows)], out_sems.at[slot]
        )

    parts = ((branch_hbm, branch_out, 0, branch_blocks), (trunk_hbm, trunk_out, branch_blocks, trunk_blocks))
    for src, _, first, blocks in parts:
        for b in range(blocks):
            arrive(src, b, first + b).start()
    for src, dst, first, blocks in parts:

        def one_block(b, carry):
            slot = first + b
            arrive(src, b, slot).wait()
            at = pl.ds(pl.multiple_of(slot * rows, rows), rows)
            square = square_ref[slot, 0:1, :] + other_ref[slot, 0:1, :]
            scale = lax.rsqrt(square / features + 1e-06)
            scale = jnp.broadcast_to(scale, (width, BLK)).T
            full = held[at, :].reshape(BLK, heads, width)
            done[at, :] = (full * scale[:, None, :]).astype(BF16).reshape(rows, width)
            leave(dst, b, slot).start()
            return carry

        lax.fori_loop(0, blocks, one_block, 0)
    for _, dst, first, blocks in parts:
        for b in range(blocks):
            leave(dst, b, first + b).wait()


def normalize(trunk, branch, square, other, heads, features):
    total = trunk.shape[0] + branch.shape[0]
    slots = total // (BLK * heads)
    return pl.pallas_call(
        functools.partial(norm_kernel, heads, features),
        in_specs=[hbm(), hbm(), vmem(), vmem()],
        out_specs=[hbm(), hbm()],
        out_shape=[jax.ShapeDtypeStruct(trunk.shape, BF16), jax.ShapeDtypeStruct(branch.shape, BF16)],
        scratch_shapes=[
            pltpu.VMEM((total, trunk.shape[1]), F32),
            pltpu.VMEM((total, trunk.shape[1]), BF16),
            pltpu.SemaphoreType.DMA((slots,)),
            pltpu.SemaphoreType.DMA((slots,)),
        ],
        compiler_params=params(),
        cost_estimate=pl.CostEstimate(
            flops=2 * (trunk.size + branch.size), bytes_accessed=6 * (trunk.size + branch.size), transcendentals=0
        ),
        name="normalize",
    )(trunk, branch, square, other)


def shards(
    trunk_query,
    trunk_key,
    trunk_value,
    trunk_wquery,
    trunk_wkey,
    trunk_wvalue,
    branch_query,
    branch_wquery,
    branch_wkey,
    branch_wvalue,
    level_gain,
    fork_block,
):
    tokens, heads, width = trunk_query.shape
    groups = trunk_wkey.shape[1]
    depth = (tokens // BLK).bit_length() - 1
    count = lax.axis_size("seq")
    planes = count // COLS
    features = heads * lax.axis_size("head") * width
    me = lax.axis_index("seq")
    column, plane = me % COLS, me // COLS
    where = me.astype(jnp.int32).reshape(1)
    root = count - 1
    top = planes - 1

    def flat(x):
        return x.reshape(x.shape[0] * x.shape[1], x.shape[2])

    tq, tk, tv, twq = flat(trunk_query), flat(trunk_key), flat(trunk_value), flat(trunk_wquery)
    twk, twv = flat(trunk_wkey), flat(trunk_wvalue)
    bq, bwq, bwk, bwv = flat(branch_query), flat(branch_wquery), flat(branch_wkey), flat(branch_wvalue)

    def send(x, pairs):
        return lax.ppermute(x, "seq", pairs)

    def down_step(x, step):
        starts = [p for p in range(planes) if (top - p) % (2 * step) == 0 and p >= step]
        pairs = [(p * COLS + c, (p - step) * COLS + c) for p in starts for c in range(COLS)]
        got = send(x, pairs)
        hit = functools.reduce(jnp.logical_or, [plane == p - step for p in starts])
        return jnp.where(hit, got, x)

    def down_first(x):
        return down_step(x, planes // 2)

    def down_rest(x):
        step = planes // 4
        while step:
            x = down_step(x, step)
            step //= 2
        return x

    def around(x):
        return [x] + [send(x, [(i, i ^ d) for i in range(count)]) for d in range(1, COLS)]

    def in_groups(x, groups_of):
        return lax.all_to_all(x, "seq", 0, 0, tiled=True, axis_index_groups=groups_of)

    in_one_plane = [[p * COLS + c for c in range(COLS)] for p in range(planes)]
    in_one_column = [[p * COLS + c for p in range(planes)] for c in range(COLS)]
    tie = lax.optimization_barrier

    half = COLS // 2
    got = send(twv, [(root - i, root - i - half) for i in range(half)])
    *pieces, local, shard_sum = block_sums(level_gain, tk, tv, heads, depth)
    mine = pieces[COLS - 1]
    for c in range(COLS - 1):
        mine = jnp.where(column == c, send(pieces[c], [(root, root - (COLS - 1) + c)]), mine)
    sums = in_groups(shard_sum, in_one_plane)
    got, sums = tie((got, sums))
    kv = down_first(jnp.where(column >= half, twk, got))
    plane_sum, ends = plane_sums(where, level_gain, sums, mine, planes, depth)
    plane_sum = in_groups(plane_sum, in_one_column)

    plane_sum, kv, ends, bwq, twk, twv = tie((plane_sum, kv, ends, bwq, twk, twv))
    shift = [(i, i + 1) for i in range(count - 1)]
    pk, pv = send(twk, shift), send(twv, shift)
    kv, ends = down_rest(kv), down_first(ends)
    far = far_attention(bwq, bwk, bwv, heads, groups)
    kv, ends, far, pk, pv, plane_sum = tie((kv, ends, far, pk, pv, plane_sum))

    cross, above = cross_sums(where, level_gain, sums, plane_sum, depth)
    cross = in_groups(cross, in_one_plane)
    cross, twq, kv = tie((cross, twq, kv))
    kvs = around(kv)
    ends = down_rest(ends)
    trunk = trunk_attention(
        where, level_gain, tq, tk, tv, twq, pk, pv, twk, twv, local, heads, groups, 0, tokens // BLK
    )
    kvs, ends, trunk, bwq = tie((kvs, ends, trunk, bwq))
    ends = (ends.astype(F32) + above).astype(BF16)
    bwq, ends = tie((bwq, ends))
    near = near_attention(where, fork_block, bwq, bwk, bwv, kvs, heads, groups)
    ends = around(ends)
    branch_full, trunk_full, square = final_linear(
        where, fork_block, bq, tq, near, far, trunk, cross, ends, heads
    )
    other = lax.ppermute(square, "head", [(0, 1), (1, 0)])
    trunk_out, branch_out = normalize(trunk_full, branch_full, square, other, heads, features)
    return trunk_out.reshape(trunk_query.shape), branch_out.reshape(branch_query.shape)


def solution(mesh):
    rows = P("seq", "head", None)
    return jax.shard_map(
        shards,
        mesh=mesh,
        in_specs=(rows,) * 10 + (P("head", None), P("seq")),
        out_specs=(rows, rows),
        check_vma=False,
    )
```

```python
import functools
import math

import jax
import jax.numpy as jnp
from jax import lax
from jax.experimental import pallas as pl
from jax.experimental.pallas import tpu as pltpu
from jax.sharding import PartitionSpec as P

BLK = 128
WIN = 512
COLS = 4
MASKED = -1e30
F32 = jnp.float32
BF16 = jnp.bfloat16
VMEM_BYTES = 60 * 1024 * 1024
SMALL_BYTES = 28 * 1024 * 1024


def params(limit=VMEM_BYTES):
    return pltpu.CompilerParams(vmem_limit_bytes=limit)


def hbm():
    return pl.BlockSpec(memory_space=pltpu.HBM)


def vmem():
    return pl.BlockSpec(memory_space=pltpu.VMEM)


def block_copy(src, dst, sems, block, rows, src_block=None):
    src_block = block if src_block is None else src_block
    return pltpu.make_async_copy(
        src.at[pl.ds(src_block * rows, rows)], dst.at[pl.ds(block * rows, rows)], sems.at[block]
    )


def smem():
    return pl.BlockSpec(memory_space=pltpu.SMEM)


def gain_factor(level, width):
    return 1.0 / math.sqrt(width * BLK * 2 ** max(level - 1, 0))


def every(rows_ref, wide, count, each):
    return wide[pl.ds(each, rows_ref.shape[0] // count, stride=count), :].astype(BF16)


def state_kernel(depth, heads, gain_ref, k_hbm, v_hbm, *rest):
    piece_refs = rest[:COLS]
    local_ref, sum_ref, keys, values, kf, vf, levels, key_sems, value_sems = rest[COLS:]
    rows, width = kf.shape
    each = heads // COLS
    copies = [
        (block_copy(k_hbm, keys, key_sems, b, rows), block_copy(v_hbm, values, value_sems, b, rows))
        for b in range(1 << depth)
    ]
    for pair in copies:
        for copy in pair:
            copy.start()
    for b, pair in enumerate(copies):
        for copy in pair:
            copy.wait()
        kf[...] = keys[b * rows : (b + 1) * rows].astype(F32)
        vf[...] = values[b * rows : (b + 1) * rows].astype(F32)
        for h in range(heads):
            k = kf[pl.ds(h, BLK, stride=heads), :].astype(BF16)
            v = vf[pl.ds(h, BLK, stride=heads), :].astype(BF16)
            merged = lax.dot_general(k, v, (((0,), (0,)), ((), ())), preferred_element_type=F32)
            before = None
            for bit in range(depth):
                if b >> bit & 1:
                    part = levels[bit, h] * (gain_ref[h, bit + 1] * gain_factor(bit + 1, width))
                    before = part if before is None else before + part
            carry = 0
            while b >> carry & 1:
                merged = merged + levels[carry, h]
                carry += 1
            if before is not None:
                before = before.astype(BF16)
                local_ref[b - 1, h] = before
                piece_refs[h // each][b - 1, h % each] = before
            if carry < depth:
                levels[carry, h] = merged
            else:
                sum_ref[h // each, h % each] = merged.astype(BF16)


def block_sums(gain, keys, values, heads, depth):
    blocks = 1 << depth
    width = keys.shape[1]
    each = heads // COLS
    return pl.pallas_call(
        functools.partial(state_kernel, depth, heads),
        in_specs=[smem(), hbm(), hbm()],
        out_specs=[vmem()] * (COLS + 2),
        out_shape=[jax.ShapeDtypeStruct((blocks - 1, each, width, width), BF16)] * COLS
        + [
            jax.ShapeDtypeStruct((blocks - 1, heads, width, width), BF16),
            jax.ShapeDtypeStruct((COLS, each, width, width), BF16),
        ],
        scratch_shapes=[
            pltpu.VMEM(keys.shape, BF16),
            pltpu.VMEM(values.shape, BF16),
            pltpu.VMEM((keys.shape[0] // blocks, width), F32),
            pltpu.VMEM((keys.shape[0] // blocks, width), F32),
            pltpu.VMEM((depth, heads, width, width), F32),
            pltpu.SemaphoreType.DMA((blocks,)),
            pltpu.SemaphoreType.DMA((blocks,)),
        ],
        compiler_params=params(),
        cost_estimate=pl.CostEstimate(
            flops=2 * keys.size * width, bytes_accessed=4 * keys.size + 2 * heads * width * width * blocks, transcendentals=0
        ),
        name="block_sums",
    )(gain, keys, values)


def in_plane(sums, column, weight):
    total = None
    for bit in range(COLS.bit_length() - 1):
        if column >> bit & 1:
            first = ((column >> bit) ^ 1) << bit
            part = functools.reduce(jnp.add, sums[first : first + (1 << bit)]) * weight(bit)
            total = part if total is None else total + part
    return total


def level_weight(gain_ref, head, depth, width, bit):
    return gain_ref[head, depth + bit + 1] * gain_factor(depth + bit + 1, width)


def plane_kernel(depth, where_ref, gain_ref, sums_ref, local_ref, plane_ref, ends_ref):
    each, width = sums_ref.shape[1], sums_ref.shape[2]
    first = (where_ref[0] & (COLS - 1)) * each
    for j in range(each):
        sums = [sums_ref[c, j].astype(F32) for c in range(COLS)]
        whole = functools.reduce(jnp.add, sums).astype(BF16)
        for p in range(plane_ref.shape[0]):
            plane_ref[p, j] = whole
        before = in_plane(sums, COLS - 1, lambda bit: level_weight(gain_ref, first + j, depth, width, bit))
        ends_ref[0, j] = before.astype(BF16)
        for f in range(local_ref.shape[0]):
            ends_ref[f + 1, j] = (before + local_ref[f, j].astype(F32)).astype(BF16)


def plane_sums(where, gain, sums, local, planes, depth):
    quarter = sums.shape[1:]
    return pl.pallas_call(
        functools.partial(plane_kernel, depth),
        in_specs=[smem(), smem(), vmem(), vmem()],
        out_specs=[vmem(), vmem()],
        out_shape=[
            jax.ShapeDtypeStruct((planes, *quarter), BF16),
            jax.ShapeDtypeStruct((local.shape[0] + 1, *quarter), BF16),
        ],
        compiler_params=params(SMALL_BYTES),
        cost_estimate=pl.CostEstimate(flops=4 * sums.size, bytes_accessed=8 * sums.size, transcendentals=0),
        name="plane_sums",
    )(where, gain, sums, local)


def cross_kernel(depth, where_ref, gain_ref, sums_ref, planes_ref, out_ref, top_ref):
    each, width = sums_ref.shape[1], sums_ref.shape[2]
    planes = planes_ref.shape[0]
    col_bits = COLS.bit_length() - 1
    plane = where_ref[0] >> col_bits
    first = (where_ref[0] & (COLS - 1)) * each
    for j in range(each):
        sums = [sums_ref[c, j].astype(F32) for c in range(COLS)]
        above = jnp.zeros((width, width), F32)
        top = jnp.zeros((width, width), F32)
        for s in range(planes - 1):
            state = planes_ref[s, j].astype(F32)
            share = jnp.float32(0.0)
            for bit in range(planes.bit_length() - 1):
                weight = level_weight(gain_ref, first + j, depth, width, col_bits + bit)
                held = jnp.logical_and((plane >> bit) & 1 == 1, (plane >> bit) ^ 1 == s >> bit)
                share = share + jnp.where(held, weight, 0.0)
                if ((planes - 1) >> bit) ^ 1 == s >> bit:
                    top = top + state * weight
            above = above + state * share
        top_ref[j] = top
        for c in range(COLS):
            before = in_plane(sums, c, lambda bit: level_weight(gain_ref, first + j, depth, width, bit))
            out_ref[c, j] = (above if before is None else above + before).astype(BF16)


def cross_sums(where, gain, sums, planes, depth):
    return pl.pallas_call(
        functools.partial(cross_kernel, depth),
        in_specs=[smem(), smem(), vmem(), vmem()],
        out_specs=[vmem(), vmem()],
        out_shape=[jax.ShapeDtypeStruct(sums.shape, BF16), jax.ShapeDtypeStruct(sums.shape[1:], F32)],
        compiler_params=params(SMALL_BYTES),
        cost_estimate=pl.CostEstimate(flops=20 * sums.size, bytes_accessed=8 * sums.size, transcendentals=0),
        name="cross_sums",
    )(where, gain, sums, planes)


def place(src_ref, wide, dst, start, groups):
    tokens = src_ref.shape[0] // groups
    wide[...] = src_ref[...].astype(F32)
    for g in range(groups):
        part = wide[pl.ds(g, tokens, stride=groups), :].astype(BF16)
        dst[g, pl.ds(start, tokens), : src_ref.shape[1]] = part


def split_groups(wide):
    rows, width = wide.shape
    pairs = wide.reshape(rows // 16, 16, width)
    low, high = pairs[:, :8], pairs[:, 8:]
    upper = lax.broadcasted_iota(jnp.int32, low.shape, 1) < 4
    first = jnp.where(upper, low, pltpu.roll(high, 4, 1))
    second = jnp.where(upper, pltpu.roll(low, 4, 1), high)
    return [part.reshape(rows // 2, width) for part in (first, second)]


def join_groups(first, second):
    rows, width = first.shape
    first, second = (part.reshape(rows // 8, 8, width) for part in (first, second))
    upper = lax.broadcasted_iota(jnp.int32, first.shape, 1) < 4
    low = jnp.where(upper, first, pltpu.roll(second, 4, 1))
    high = jnp.where(upper, pltpu.roll(first, 4, 1), second)
    return jnp.concatenate([low, high], axis=1).reshape(2 * rows, width)


def window_logits(queries, keys, token, share, bias):
    rows = queries.shape[0]
    logits = lax.dot_general(queries, keys, (((1,), (1,)), ((), ())), preferred_element_type=F32)
    row = token + lax.broadcasted_iota(jnp.int32, (rows, BLK), 0) // share
    col = lax.broadcasted_iota(jnp.int32, (rows, BLK), 1)
    late = col > row
    first = jnp.where(late, logits[:, :BLK], MASKED)
    last = jnp.where(late, MASKED, logits[:, -BLK:])
    logits = jnp.concatenate([first, logits[:, BLK:-BLK], last], axis=1)
    return logits if bias is None else logits + bias


def window_outputs(logits, values, width):
    top = jnp.max(logits, axis=1, keepdims=True)
    weights = jnp.exp2((logits - top) * (math.log2(math.e) / math.sqrt(width))).astype(BF16)
    both = jnp.dot(weights, values, preferred_element_type=F32)
    return both[:, :width] / both[:, width:]


def window_block(q_ref, kh, vh, base, groups, bias=None):
    width = q_ref.shape[1]
    span = WIN + BLK
    share = q_ref.shape[0] // BLK // groups
    parts = [part.astype(BF16) for part in split_groups(q_ref[...].astype(F32))]
    chunks = [(g, c) for g in range(groups) for c in range(0, BLK * share, BLK)]

    def logits_of(chunk):
        g, c = chunk
        return window_logits(parts[g][c : c + BLK], kh[g, pl.ds(base, span), :], c // share, share, bias)

    outs = []
    ahead = logits_of(chunks[0])
    for i, (g, c) in enumerate(chunks):
        now = ahead
        if i + 1 < len(chunks):
            ahead = logits_of(chunks[i + 1])
        outs.append(window_outputs(now, vh[g, pl.ds(base, span), :], width))
    half = len(outs) // 2
    return join_groups(jnp.concatenate(outs[:half], axis=0), jnp.concatenate(outs[half:], axis=0))


def token_rows(tokens, heads):
    row = lax.broadcasted_iota(jnp.int32, (tokens, tokens * heads), 1) // heads
    return (row == lax.broadcasted_iota(jnp.int32, (tokens, tokens * heads), 0)).astype(F32).astype(BF16)


def square_sums(full, mine):
    sums = jnp.dot(mine, (full * full).astype(BF16), preferred_element_type=F32)
    ones = jnp.ones((8, full.shape[1]), F32)
    return lax.dot_general(
        ones, sums, (((1,), (1,)), ((), ())), precision=lax.Precision.HIGHEST, preferred_element_type=F32
    )


def far_kernel(heads, groups, q_ref, pk_ref, pv_ref, ck_ref, cv_ref, out_ref, kf, kh, vh):
    step = pl.program_id(0)
    width = q_ref.shape[1]

    @pl.when(step == 0)
    def _():
        vh[:, :, width:] = jnp.ones((groups, vh.shape[1], width), BF16)
        place(pk_ref, kf, kh, 0, groups)
        place(ck_ref, kf, kh, WIN, groups)
        place(pv_ref, kf, vh, 0, groups)
        place(cv_ref, kf, vh, WIN, groups)

    out_ref[...] = window_block(q_ref, kh, vh, pl.multiple_of(step * BLK, BLK), groups).astype(BF16)


def attention_cost(tokens, heads, width, extra=0):
    span = WIN + BLK
    return pl.CostEstimate(
        flops=6 * tokens * heads * span * width + extra,
        bytes_accessed=12 * tokens * heads * width,
        transcendentals=tokens * heads * span,
    )


def far_attention(queries, keys, values, heads, groups):
    width = queries.shape[1]
    steps = queries.shape[0] // (BLK * heads) - WIN // BLK
    skip = WIN // BLK
    at_first = pl.BlockSpec((WIN * groups, width), lambda i: (0, 0))
    at_next = pl.BlockSpec((WIN * groups, width), lambda i: (1, 0))
    return pl.pallas_call(
        functools.partial(far_kernel, heads, groups),
        grid=(steps,),
        in_specs=[
            pl.BlockSpec((BLK * heads, width), lambda i: (i + skip, 0)),
            at_first,
            at_first,
            at_next,
            at_next,
        ],
        out_specs=pl.BlockSpec((BLK * heads, width), lambda i: (i, 0)),
        out_shape=jax.ShapeDtypeStruct((steps * BLK * heads, width), BF16),
        scratch_shapes=[
            pltpu.VMEM((WIN * groups, width), F32),
            pltpu.VMEM((groups, 2 * WIN, width), BF16),
            pltpu.VMEM((groups, 2 * WIN, 2 * width), BF16),
        ],
        compiler_params=params(),
        cost_estimate=attention_cost(steps * BLK, heads, width),
        name="far_attention",
    )(queries, keys, values, keys, values)


def trunk_kernel(heads, groups, first, where_ref, gain_ref, q_ref, k_ref, v_ref, wq_ref, pk_ref, pv_ref, ck_ref, cv_ref, local_ref, out_ref, nf, tf, sf, kf, kh, vh, of):
    block = pl.program_id(0) + first
    width = q_ref.shape[1]

    @pl.when(pl.program_id(0) == 0)
    def _():
        vh[:, :, width:] = jnp.ones((groups, vh.shape[1], width), BF16)
        place(pk_ref, kf, kh, 0, groups)
        place(ck_ref, kf, kh, WIN, groups)
        place(pv_ref, kf, vh, 0, groups)
        place(cv_ref, kf, vh, WIN, groups)

    nf[...] = q_ref[...].astype(F32)
    tf[...] = k_ref[...].astype(F32)
    sf[...] = v_ref[...].astype(F32)
    base = pl.multiple_of(block * BLK, BLK)
    reach = jnp.where(where_ref[0] == 0, WIN - block * BLK, 0)
    bias = jnp.where(lax.broadcasted_iota(jnp.int32, (1, WIN + BLK), 1) < reach, MASKED, 0.0).astype(F32)
    row = lax.broadcasted_iota(jnp.int32, (BLK, BLK), 0)
    col = lax.broadcasted_iota(jnp.int32, (BLK, BLK), 1)
    inner = (block > 0).astype(F32).astype(BF16)
    q = [every(q_ref, nf, heads, h) for h in range(heads)]
    inside = [
        lax.dot_general(q[h], every(k_ref, tf, heads, h), (((1,), (1,)), ((), ())), preferred_element_type=F32)
        for h in range(heads)
    ]
    for h in range(heads):
        weight = jnp.where(col <= row, inside[h], 0.0) * (gain_ref[h, 0] * gain_factor(0, width))
        left = jnp.concatenate([weight.astype(BF16), q[h]], axis=1)
        right = jnp.concatenate([every(v_ref, sf, heads, h), local_ref[0, h] * inner], axis=0)
        of[pl.ds(h, BLK, stride=heads), :] = jnp.dot(left, right, preferred_element_type=F32)
    out_ref[...] = window_block(wq_ref, kh, vh, base, groups, bias) + of[...]


def trunk_attention(where, gain, q, k, v, wq, before_kv, ck, cv, local, heads, groups, first, steps):
    width = q.shape[1]
    rows = BLK * heads
    at_block = pl.BlockSpec((rows, width), lambda i: (i + first, 0))
    whole = pl.BlockSpec((WIN * groups, width), lambda i: (0, 0))
    second = pl.BlockSpec((WIN * groups, width), lambda i: (1, 0))
    before = pl.BlockSpec((1, heads, width, width), lambda i: (jnp.maximum(i + first - 1, 0), 0, 0, 0))
    wide = pltpu.VMEM((rows, width), F32)
    return pl.pallas_call(
        functools.partial(trunk_kernel, heads, groups, first),
        grid=(steps,),
        in_specs=[smem(), smem()] + [at_block] * 4 + [whole, second, whole, whole, before],
        out_specs=pl.BlockSpec((rows, width), lambda i: (i, 0)),
        out_shape=jax.ShapeDtypeStruct((steps * rows, width), F32),
        scratch_shapes=[
            wide,
            wide,
            wide,
            pltpu.VMEM((WIN * groups, width), F32),
            pltpu.VMEM((groups, 2 * WIN, width), BF16),
            pltpu.VMEM((groups, 2 * WIN, 2 * width), BF16),
            wide,
        ],
        compiler_params=params(),
        cost_estimate=attention_cost(steps * BLK, heads, width, 2 * steps * BLK * BLK * heads * 3 * width),
        name="trunk_attention",
    )(where, gain, q, k, v, wq, before_kv, before_kv, ck, cv, local)


def near_kernel(groups, where_ref, fork_ref, q_ref, ck_ref, cv_ref, *rest):
    kv_refs, out_ref = rest[:COLS], rest[COLS]
    kf, kh, vh, kt = rest[COLS + 1 :]
    step = pl.program_id(0)
    width = q_ref.shape[1]
    column = where_ref[0] & (COLS - 1)
    start = pl.multiple_of(fork_ref[0] * BLK, BLK)

    @pl.when(step == 0)
    def _():
        for i in range(COLS):
            kt[column ^ i] = kv_refs[i][...]
        vh[:, :, width:] = jnp.ones((groups, vh.shape[1], width), BF16)
        place(kt.at[0], kf, vh, 0, groups)
        place(kt.at[1], kf, vh, WIN, groups)
        place(kt.at[2], kf, kh, 0, groups)
        place(kt.at[3], kf, kh, WIN, groups)
        place(ck_ref, kf, kh, pl.multiple_of(start + WIN, BLK), groups)
        place(cv_ref, kf, vh, pl.multiple_of(start + WIN, BLK), groups)

    base = pl.multiple_of(start + step * BLK, BLK)
    out_ref[...] = window_block(q_ref, kh, vh, base, groups).astype(BF16)


def near_attention(where, fork, wq, ck, cv, kvs, heads, groups):
    width = wq.shape[1]
    steps = WIN // BLK
    at_block = pl.BlockSpec((BLK * heads, width), lambda i: (i, 0))
    whole = pl.BlockSpec((WIN * groups, width), lambda i: (0, 0))
    return pl.pallas_call(
        functools.partial(near_kernel, groups),
        grid=(steps,),
        in_specs=[smem(), smem(), at_block, whole, whole] + [whole] * COLS,
        out_specs=at_block,
        out_shape=jax.ShapeDtypeStruct((steps * BLK * heads, width), BF16),
        scratch_shapes=[
            pltpu.VMEM((WIN * groups, width), F32),
            pltpu.VMEM((groups, 3 * WIN, width), BF16),
            pltpu.VMEM((groups, 3 * WIN, 2 * width), BF16),
            pltpu.VMEM((COLS, WIN * groups, width), BF16),
        ],
        compiler_params=params(),
        cost_estimate=attention_cost(steps * BLK, heads, width),
        name="near_attention",
    )(where, fork, wq, ck, cv, *kvs)


def final_kernel(heads, where_ref, fork_ref, bq_hbm, tq_hbm, near_hbm, far_hbm, trunk_hbm, cross_hbm, *rest):
    end_hbms, (branch_full, trunk_full, square_ref, qs, ws, ts, nf, of, fs, es, cs, mine) = rest[:COLS], rest[COLS : COLS + 12]
    q_sems, w_sems, f_sems, e_sems = rest[COLS + 12 :]
    window_hbms = (near_hbm, far_hbm)
    rows = BLK * heads
    branch_blocks, trunk_blocks = ws.shape[0] // rows, ts.shape[0] // rows
    each = heads // COLS
    column = where_ref[0] & (COLS - 1)
    states = [
        pltpu.make_async_copy(end_hbms[i].at[fork_ref[0]], es.at[column ^ i], e_sems.at[i]) for i in range(COLS)
    ] + [pltpu.make_async_copy(cross_hbm, cs, e_sems.at[COLS])]

    def query_copy(src, b, slot):
        return pltpu.make_async_copy(src.at[pl.ds(b * rows, rows)], qs.at[pl.ds(slot * rows, rows)], q_sems.at[slot])

    def other_copy(src, b, dst, place_of, slot):
        return pltpu.make_async_copy(
            src.at[pl.ds(b * rows, rows)], dst.at[pl.ds(place_of * rows, rows)], w_sems.at[slot]
        )

    def result_copy(b, dst, slot):
        return pltpu.make_async_copy(fs.at[pl.ds(slot * rows, rows)], dst.at[pl.ds(b * rows, rows)], f_sems.at[slot])

    for copy in states:
        copy.start()
    per_window = branch_blocks // 2
    for b in range(branch_blocks):
        query_copy(bq_hbm, b, b).start()
        other_copy(window_hbms[b // per_window], b % per_window, ws, b, b).start()
    for b in range(trunk_blocks):
        query_copy(tq_hbm, b, branch_blocks + b).start()
        other_copy(trunk_hbm, b, ts, b, branch_blocks + b).start()
    mine[...] = token_rows(BLK, heads)
    for copy in states:
        copy.wait()

    def rest_of(slot, window, states_ref):
        at = pl.ds(pl.multiple_of(slot * rows, rows), rows)
        nf[...] = qs[at, :].astype(F32)
        for h in range(heads):
            q = nf[pl.ds(h, BLK, stride=heads), :].astype(BF16)
            of[pl.ds(h, BLK, stride=heads), :] = jnp.dot(
                q, states_ref[h // each, h % each], preferred_element_type=F32
            )
        full = window.astype(F32) + of[...]
        fs[at, :] = full
        square_ref[slot] = square_sums(full, mine[...])

    def branch_block(b, carry):
        query_copy(bq_hbm, b, b).wait()
        other_copy(window_hbms[0], 0, ws, b, b).wait()
        rest_of(b, ws[pl.ds(pl.multiple_of(b * rows, rows), rows), :], es)
        result_copy(b, branch_full, b).start()
        return carry

    def trunk_block(b, carry):
        slot = branch_blocks + b
        query_copy(tq_hbm, b, slot).wait()
        other_copy(trunk_hbm, 0, ts, b, slot).wait()
        rest_of(slot, ts[pl.ds(pl.multiple_of(b * rows, rows), rows), :], cs)
        result_copy(b, trunk_full, slot).start()
        return carry

    lax.fori_loop(0, branch_blocks, branch_block, 0)
    lax.fori_loop(0, trunk_blocks, trunk_block, 0)
    for b in range(branch_blocks):
        result_copy(b, branch_full, b).wait()
    for b in range(trunk_blocks):
        result_copy(b, trunk_full, branch_blocks + b).wait()


def final_linear(where, fork, bq, tq, near, far, trunk, cross, ends, heads):
    width = bq.shape[1]
    rows = BLK * heads
    total = bq.shape[0] + tq.shape[0]
    blocks = total // rows
    return pl.pallas_call(
        functools.partial(final_kernel, heads),
        in_specs=[smem(), smem()] + [hbm()] * (6 + COLS),
        out_specs=[hbm(), hbm(), vmem()],
        out_shape=[
            jax.ShapeDtypeStruct(bq.shape, F32),
            jax.ShapeDtypeStruct(tq.shape, F32),
            jax.ShapeDtypeStruct((blocks, 8, BLK), F32),
        ],
        scratch_shapes=[
            pltpu.VMEM((total, width), BF16),
            pltpu.VMEM(bq.shape, BF16),
            pltpu.VMEM(tq.shape, F32),
            pltpu.VMEM((rows, width), F32),
            pltpu.VMEM((rows, width), F32),
            pltpu.VMEM((total, width), F32),
            pltpu.VMEM(cross.shape, BF16),
            pltpu.VMEM(cross.shape, BF16),
            pltpu.VMEM((BLK, rows), BF16),
            pltpu.SemaphoreType.DMA((blocks,)),
            pltpu.SemaphoreType.DMA((blocks,)),
            pltpu.SemaphoreType.DMA((blocks,)),
            pltpu.SemaphoreType.DMA((COLS + 1,)),
        ],
        compiler_params=params(),
        cost_estimate=pl.CostEstimate(flops=4 * total * width * width, bytes_accessed=8 * total * width, transcendentals=0),
        name="final_linear",
    )(where, fork, bq, tq, near, far, trunk, cross, *ends)


def norm_kernel(heads, features, trunk_hbm, branch_hbm, square_ref, other_ref, trunk_out, branch_out, held, done, in_sems, out_sems):
    rows = BLK * heads
    width = held.shape[1]
    trunk_blocks = trunk_hbm.shape[0] // rows
    branch_blocks = branch_hbm.shape[0] // rows

    def arrive(src, block, slot):
        return pltpu.make_async_copy(
            src.at[pl.ds(block * rows, rows)], held.at[pl.ds(slot * rows, rows)], in_sems.at[slot]
        )

    def leave(dst, block, slot):
        return pltpu.make_async_copy(
            done.at[pl.ds(slot * rows, rows)], dst.at[pl.ds(block * rows, rows)], out_sems.at[slot]
        )

    parts = ((branch_hbm, branch_out, 0, branch_blocks), (trunk_hbm, trunk_out, branch_blocks, trunk_blocks))
    for src, _, first, blocks in parts:
        for b in range(blocks):
            arrive(src, b, first + b).start()
    for src, dst, first, blocks in parts:

        def one_block(b, carry):
            slot = first + b
            arrive(src, b, slot).wait()
            at = pl.ds(pl.multiple_of(slot * rows, rows), rows)
            square = square_ref[slot, 0:1, :] + other_ref[slot, 0:1, :]
            scale = lax.rsqrt(square / features + 1e-06)
            scale = jnp.broadcast_to(scale, (width, BLK)).T
            full = held[at, :].reshape(BLK, heads, width)
            done[at, :] = (full * scale[:, None, :]).astype(BF16).reshape(rows, width)
            leave(dst, b, slot).start()
            return carry

        lax.fori_loop(0, blocks, one_block, 0)
    for _, dst, first, blocks in parts:
        for b in range(blocks):
            leave(dst, b, first + b).wait()


def normalize(trunk, branch, square, other, heads, features):
    total = trunk.shape[0] + branch.shape[0]
    slots = total // (BLK * heads)
    return pl.pallas_call(
        functools.partial(norm_kernel, heads, features),
        in_specs=[hbm(), hbm(), vmem(), vmem()],
        out_specs=[hbm(), hbm()],
        out_shape=[jax.ShapeDtypeStruct(trunk.shape, BF16), jax.ShapeDtypeStruct(branch.shape, BF16)],
        scratch_shapes=[
            pltpu.VMEM((total, trunk.shape[1]), F32),
            pltpu.VMEM((total, trunk.shape[1]), BF16),
            pltpu.SemaphoreType.DMA((slots,)),
            pltpu.SemaphoreType.DMA((slots,)),
        ],
        compiler_params=params(),
        cost_estimate=pl.CostEstimate(
            flops=2 * (trunk.size + branch.size), bytes_accessed=6 * (trunk.size + branch.size), transcendentals=0
        ),
        name="normalize",
    )(trunk, branch, square, other)


def shards(
    trunk_query,
    trunk_key,
    trunk_value,
    trunk_wquery,
    trunk_wkey,
    trunk_wvalue,
    branch_query,
    branch_wquery,
    branch_wkey,
    branch_wvalue,
    level_gain,
    fork_block,
):
    tokens, heads, width = trunk_query.shape
    groups = trunk_wkey.shape[1]
    depth = (tokens // BLK).bit_length() - 1
    count = lax.axis_size("seq")
    planes = count // COLS
    features = heads * lax.axis_size("head") * width
    me = lax.axis_index("seq")
    column, plane = me % COLS, me // COLS
    where = me.astype(jnp.int32).reshape(1)
    root = count - 1
    top = planes - 1

    def flat(x):
        return x.reshape(x.shape[0] * x.shape[1], x.shape[2])

    tq, tk, tv, twq = flat(trunk_query), flat(trunk_key), flat(trunk_value), flat(trunk_wquery)
    twk, twv = flat(trunk_wkey), flat(trunk_wvalue)
    bq, bwq, bwk, bwv = flat(branch_query), flat(branch_wquery), flat(branch_wkey), flat(branch_wvalue)

    def send(x, pairs):
        return lax.ppermute(x, "seq", pairs)

    def down_step(x, step):
        starts = [p for p in range(planes) if (top - p) % (2 * step) == 0 and p >= step]
        pairs = [(p * COLS + c, (p - step) * COLS + c) for p in starts for c in range(COLS)]
        got = send(x, pairs)
        hit = functools.reduce(jnp.logical_or, [plane == p - step for p in starts])
        return jnp.where(hit, got, x)

    def down_first(x):
        return down_step(x, planes // 2)

    def down_rest(x):
        step = planes // 4
        while step:
            x = down_step(x, step)
            step //= 2
        return x

    def around(x):
        return [x] + [send(x, [(i, i ^ d) for i in range(count)]) for d in range(1, COLS)]

    def in_groups(x, groups_of):
        return lax.all_to_all(x, "seq", 0, 0, tiled=True, axis_index_groups=groups_of)

    in_one_plane = [[p * COLS + c for c in range(COLS)] for p in range(planes)]
    in_one_column = [[p * COLS + c for p in range(planes)] for c in range(COLS)]
    tie = lax.optimization_barrier

    def down(x):
        return down_rest(down_first(x))

    half = COLS // 2
    got = send(twv, [(root - i, root - i - half) for i in range(half)])
    kv = down(jnp.where(column >= half, twk, got))
    before_kv = send(jnp.concatenate([twk, twv], axis=0), [(i, i + 1) for i in range(count - 1)])

    *pieces, local, shard_sum = block_sums(level_gain, tk, tv, heads, depth)
    mine = pieces[COLS - 1]
    for c in range(COLS - 1):
        mine = jnp.where(column == c, send(pieces[c], [(root, root - (COLS - 1) + c)]), mine)
    sums = in_groups(shard_sum, in_one_plane)
    plane_sum, ends = plane_sums(where, level_gain, sums, mine, planes, depth)
    plane_sum = in_groups(plane_sum, in_one_column)
    ends = down(ends)
    cross, above = cross_sums(where, level_gain, sums, plane_sum, depth)
    cross = in_groups(cross, in_one_plane)

    far = far_attention(bwq, bwk, bwv, heads, groups)
    kv, far = tie((kv, far))
    kvs = around(kv)
    ends = around((ends.astype(F32) + above).astype(BF16))
    trunk = trunk_attention(
        where, level_gain, tq, tk, tv, twq, before_kv, twk, twv, local, heads, groups, 0, tokens // BLK
    )
    trunk, bwq = tie((trunk, bwq))
    near = near_attention(where, fork_block, bwq, bwk, bwv, kvs, heads, groups)
    branch_full, trunk_full, square = final_linear(
        where, fork_block, bq, tq, near, far, trunk, cross, ends, heads
    )
    other = lax.ppermute(square, "head", [(0, 1), (1, 0)])
    trunk_out, branch_out = normalize(trunk_full, branch_full, square, other, heads, features)
    return trunk_out.reshape(trunk_query.shape), branch_out.reshape(branch_query.shape)


def solution(mesh):
    rows = P("seq", "head", None)
    return jax.shard_map(
        shards,
        mesh=mesh,
        in_specs=(rows,) * 10 + (P("head", None), P("seq")),
        out_specs=(rows, rows),
        check_vma=False,
    )
```

```python
import functools
import math

import jax
import jax.numpy as jnp
from jax import lax
from jax.experimental import pallas as pl
from jax.experimental.pallas import tpu as pltpu
from jax.sharding import PartitionSpec as P

BLK = 128
WIN = 512
COLS = 4
MASKED = -1e30
CHUNK = 32
F32 = jnp.float32
BF16 = jnp.bfloat16
VMEM_BYTES = 60 * 1024 * 1024
SMALL_BYTES = 28 * 1024 * 1024


def params(limit=VMEM_BYTES):
    return pltpu.CompilerParams(vmem_limit_bytes=limit)


def hbm():
    return pl.BlockSpec(memory_space=pltpu.HBM)


def vmem():
    return pl.BlockSpec(memory_space=pltpu.VMEM)


def block_copy(src, dst, sems, block, rows, src_block=None):
    src_block = block if src_block is None else src_block
    return pltpu.make_async_copy(
        src.at[pl.ds(src_block * rows, rows)], dst.at[pl.ds(block * rows, rows)], sems.at[block]
    )


def smem():
    return pl.BlockSpec(memory_space=pltpu.SMEM)


def gain_factor(level, width):
    return 1.0 / math.sqrt(width * BLK * 2 ** max(level - 1, 0))


def every(rows_ref, wide, count, each):
    return wide[pl.ds(each, rows_ref.shape[0] // count, stride=count), :].astype(BF16)


def state_kernel(depth, heads, gain_ref, k_hbm, v_hbm, *rest):
    piece_refs = rest[:COLS]
    local_ref, sum_ref, keys, values, kf, vf, levels, key_sems, value_sems = rest[COLS:]
    rows, width = kf.shape
    each = heads // COLS
    copies = [
        (block_copy(k_hbm, keys, key_sems, b, rows), block_copy(v_hbm, values, value_sems, b, rows))
        for b in range(1 << depth)
    ]
    for pair in copies:
        for copy in pair:
            copy.start()
    for b, pair in enumerate(copies):
        for copy in pair:
            copy.wait()
        kf[...] = keys[b * rows : (b + 1) * rows].astype(F32)
        vf[...] = values[b * rows : (b + 1) * rows].astype(F32)
        for h in range(heads):
            k = kf[pl.ds(h, BLK, stride=heads), :].astype(BF16)
            v = vf[pl.ds(h, BLK, stride=heads), :].astype(BF16)
            merged = lax.dot_general(k, v, (((0,), (0,)), ((), ())), preferred_element_type=F32)
            before = None
            for bit in range(depth):
                if b >> bit & 1:
                    part = levels[bit, h] * (gain_ref[h, bit + 1] * gain_factor(bit + 1, width))
                    before = part if before is None else before + part
            carry = 0
            while b >> carry & 1:
                merged = merged + levels[carry, h]
                carry += 1
            if before is not None:
                before = before.astype(BF16)
                local_ref[b - 1, h] = before
                piece_refs[h // each][b - 1, h % each] = before
            if carry < depth:
                levels[carry, h] = merged
            else:
                sum_ref[h // each, h % each] = merged.astype(BF16)


def block_sums(gain, keys, values, heads, depth):
    blocks = 1 << depth
    width = keys.shape[1]
    each = heads // COLS
    return pl.pallas_call(
        functools.partial(state_kernel, depth, heads),
        in_specs=[smem(), hbm(), hbm()],
        out_specs=[vmem()] * (COLS + 2),
        out_shape=[jax.ShapeDtypeStruct((blocks - 1, each, width, width), BF16)] * COLS
        + [
            jax.ShapeDtypeStruct((blocks - 1, heads, width, width), BF16),
            jax.ShapeDtypeStruct((COLS, each, width, width), BF16),
        ],
        scratch_shapes=[
            pltpu.VMEM(keys.shape, BF16),
            pltpu.VMEM(values.shape, BF16),
            pltpu.VMEM((keys.shape[0] // blocks, width), F32),
            pltpu.VMEM((keys.shape[0] // blocks, width), F32),
            pltpu.VMEM((depth, heads, width, width), F32),
            pltpu.SemaphoreType.DMA((blocks,)),
            pltpu.SemaphoreType.DMA((blocks,)),
        ],
        compiler_params=params(),
        cost_estimate=pl.CostEstimate(
            flops=2 * keys.size * width, bytes_accessed=4 * keys.size + 2 * heads * width * width * blocks, transcendentals=0
        ),
        name="block_sums",
    )(gain, keys, values)


def in_plane(sums, column, weight):
    total = None
    for bit in range(COLS.bit_length() - 1):
        if column >> bit & 1:
            first = ((column >> bit) ^ 1) << bit
            part = functools.reduce(jnp.add, sums[first : first + (1 << bit)]) * weight(bit)
            total = part if total is None else total + part
    return total


def level_weight(gain_ref, head, depth, width, bit):
    return gain_ref[head, depth + bit + 1] * gain_factor(depth + bit + 1, width)


def plane_kernel(depth, where_ref, gain_ref, sums_ref, local_ref, plane_ref, ends_ref):
    each, width = sums_ref.shape[1], sums_ref.shape[2]
    first = (where_ref[0] & (COLS - 1)) * each
    for j in range(each):
        sums = [sums_ref[c, j].astype(F32) for c in range(COLS)]
        whole = functools.reduce(jnp.add, sums).astype(BF16)
        for p in range(plane_ref.shape[0]):
            plane_ref[p, j] = whole
        before = in_plane(sums, COLS - 1, lambda bit: level_weight(gain_ref, first + j, depth, width, bit))
        ends_ref[0, j] = before.astype(BF16)
        for f in range(local_ref.shape[0]):
            ends_ref[f + 1, j] = (before + local_ref[f, j].astype(F32)).astype(BF16)


def plane_sums(where, gain, sums, local, planes, depth):
    quarter = sums.shape[1:]
    return pl.pallas_call(
        functools.partial(plane_kernel, depth),
        in_specs=[smem(), smem(), vmem(), vmem()],
        out_specs=[vmem(), vmem()],
        out_shape=[
            jax.ShapeDtypeStruct((planes, *quarter), BF16),
            jax.ShapeDtypeStruct((local.shape[0] + 1, *quarter), BF16),
        ],
        compiler_params=params(SMALL_BYTES),
        cost_estimate=pl.CostEstimate(flops=4 * sums.size, bytes_accessed=8 * sums.size, transcendentals=0),
        name="plane_sums",
    )(where, gain, sums, local)


def cross_kernel(depth, where_ref, gain_ref, sums_ref, planes_ref, out_ref, top_ref):
    each, width = sums_ref.shape[1], sums_ref.shape[2]
    planes = planes_ref.shape[0]
    col_bits = COLS.bit_length() - 1
    plane = where_ref[0] >> col_bits
    first = (where_ref[0] & (COLS - 1)) * each
    for j in range(each):
        sums = [sums_ref[c, j].astype(F32) for c in range(COLS)]
        above = jnp.zeros((width, width), F32)
        top = jnp.zeros((width, width), F32)
        for s in range(planes - 1):
            state = planes_ref[s, j].astype(F32)
            share = jnp.float32(0.0)
            for bit in range(planes.bit_length() - 1):
                weight = level_weight(gain_ref, first + j, depth, width, col_bits + bit)
                held = jnp.logical_and((plane >> bit) & 1 == 1, (plane >> bit) ^ 1 == s >> bit)
                share = share + jnp.where(held, weight, 0.0)
                if ((planes - 1) >> bit) ^ 1 == s >> bit:
                    top = top + state * weight
            above = above + state * share
        top_ref[j] = top
        for c in range(COLS):
            before = in_plane(sums, c, lambda bit: level_weight(gain_ref, first + j, depth, width, bit))
            out_ref[c, j] = (above if before is None else above + before).astype(BF16)


def cross_sums(where, gain, sums, planes, depth):
    return pl.pallas_call(
        functools.partial(cross_kernel, depth),
        in_specs=[smem(), smem(), vmem(), vmem()],
        out_specs=[vmem(), vmem()],
        out_shape=[jax.ShapeDtypeStruct(sums.shape, BF16), jax.ShapeDtypeStruct(sums.shape[1:], F32)],
        compiler_params=params(SMALL_BYTES),
        cost_estimate=pl.CostEstimate(flops=20 * sums.size, bytes_accessed=8 * sums.size, transcendentals=0),
        name="cross_sums",
    )(where, gain, sums, planes)


def place(src_ref, wide, dst, start, groups):
    tokens = src_ref.shape[0] // groups
    wide[...] = src_ref[...].astype(F32)
    for g in range(groups):
        part = wide[pl.ds(g, tokens, stride=groups), :].astype(BF16)
        dst[g, pl.ds(start, tokens), : src_ref.shape[1]] = part


def split_groups(wide):
    rows, width = wide.shape
    pairs = wide.reshape(rows // 16, 16, width)
    low, high = pairs[:, :8], pairs[:, 8:]
    upper = lax.broadcasted_iota(jnp.int32, low.shape, 1) < 4
    first = jnp.where(upper, low, pltpu.roll(high, 4, 1))
    second = jnp.where(upper, pltpu.roll(low, 4, 1), high)
    return [part.reshape(rows // 2, width) for part in (first, second)]


def join_groups(first, second):
    rows, width = first.shape
    first, second = (part.reshape(rows // 8, 8, width) for part in (first, second))
    upper = lax.broadcasted_iota(jnp.int32, first.shape, 1) < 4
    low = jnp.where(upper, first, pltpu.roll(second, 4, 1))
    high = jnp.where(upper, pltpu.roll(first, 4, 1), second)
    return jnp.concatenate([low, high], axis=1).reshape(2 * rows, width)


def window_block(q_ref, kh, vh, logits, weights, base, groups, bias=None):
    width = q_ref.shape[1]
    span = WIN + BLK
    share = q_ref.shape[0] // BLK // groups
    parts = [part.astype(BF16) for part in split_groups(q_ref[...].astype(F32))]
    scale = math.log2(math.e) / math.sqrt(width)
    for g in range(groups):
        logits[g] = lax.dot_general(
            parts[g], kh[g, pl.ds(base, span), :], (((1,), (1,)), ((), ())), preferred_element_type=F32
        )
    row = lax.broadcasted_iota(jnp.int32, (CHUNK, BLK), 0) // share
    ahead = lax.broadcasted_iota(jnp.int32, (CHUNK, BLK), 1) - row
    outs = []
    for g in range(groups):
        for r in range(0, BLK * share, CHUNK):
            late = ahead > r // share
            first = jnp.where(late, logits[g, r : r + CHUNK, :BLK], MASKED)
            last = jnp.where(late, MASKED, logits[g, r : r + CHUNK, WIN:])
            now = jnp.concatenate([first, logits[g, r : r + CHUNK, BLK:WIN], last], axis=1)
            if bias is not None:
                now = now + bias
            top = jnp.max(now, axis=1, keepdims=True)
            weights[g, r : r + CHUNK, :] = jnp.exp2((now - top) * scale).astype(BF16)
        both = jnp.dot(weights[g], vh[g, pl.ds(base, span), :], preferred_element_type=F32)
        outs.append(both[:, :width] / both[:, width:])
    return join_groups(*outs)


def window_scratch(heads, groups):
    rows = BLK * heads // groups
    return [pltpu.VMEM((groups, rows, WIN + BLK), F32), pltpu.VMEM((groups, rows, WIN + BLK), BF16)]


def token_rows(tokens, heads):
    row = lax.broadcasted_iota(jnp.int32, (tokens, tokens * heads), 1) // heads
    return (row == lax.broadcasted_iota(jnp.int32, (tokens, tokens * heads), 0)).astype(F32).astype(BF16)


def square_sums(full, mine):
    sums = jnp.dot(mine, (full * full).astype(BF16), preferred_element_type=F32)
    ones = jnp.ones((8, full.shape[1]), F32)
    return lax.dot_general(
        ones, sums, (((1,), (1,)), ((), ())), precision=lax.Precision.HIGHEST, preferred_element_type=F32
    )


def far_kernel(heads, groups, q_ref, pk_ref, pv_ref, ck_ref, cv_ref, out_ref, kf, kh, vh, logits, weights):
    step = pl.program_id(0)
    width = q_ref.shape[1]

    @pl.when(step == 0)
    def _():
        vh[:, :, width:] = jnp.ones((groups, vh.shape[1], width), BF16)
        place(pk_ref, kf, kh, 0, groups)
        place(ck_ref, kf, kh, WIN, groups)
        place(pv_ref, kf, vh, 0, groups)
        place(cv_ref, kf, vh, WIN, groups)

    out_ref[...] = window_block(q_ref, kh, vh, logits, weights, pl.multiple_of(step * BLK, BLK), groups).astype(BF16)


def attention_cost(tokens, heads, width, extra=0):
    span = WIN + BLK
    return pl.CostEstimate(
        flops=6 * tokens * heads * span * width + extra,
        bytes_accessed=12 * tokens * heads * width,
        transcendentals=tokens * heads * span,
    )


def far_attention(queries, keys, values, heads, groups):
    width = queries.shape[1]
    steps = queries.shape[0] // (BLK * heads) - WIN // BLK
    skip = WIN // BLK
    at_first = pl.BlockSpec((WIN * groups, width), lambda i: (0, 0))
    at_next = pl.BlockSpec((WIN * groups, width), lambda i: (1, 0))
    return pl.pallas_call(
        functools.partial(far_kernel, heads, groups),
        grid=(steps,),
        in_specs=[
            pl.BlockSpec((BLK * heads, width), lambda i: (i + skip, 0)),
            at_first,
            at_first,
            at_next,
            at_next,
        ],
        out_specs=pl.BlockSpec((BLK * heads, width), lambda i: (i, 0)),
        out_shape=jax.ShapeDtypeStruct((steps * BLK * heads, width), BF16),
        scratch_shapes=[
            pltpu.VMEM((WIN * groups, width), F32),
            pltpu.VMEM((groups, 2 * WIN, width), BF16),
            pltpu.VMEM((groups, 2 * WIN, 2 * width), BF16),
            *window_scratch(heads, groups),
        ],
        compiler_params=params(),
        cost_estimate=attention_cost(steps * BLK, heads, width),
        name="far_attention",
    )(queries, keys, values, keys, values)


def trunk_kernel(heads, groups, first, where_ref, gain_ref, q_ref, k_ref, v_ref, wq_ref, pk_ref, pv_ref, ck_ref, cv_ref, local_ref, cross_ref, out_ref, square_ref, nf, tf, sf, kf, kh, vh, of, mine, logits, weights):
    block = pl.program_id(0) + first
    width = q_ref.shape[1]

    @pl.when(pl.program_id(0) == 0)
    def _():
        vh[:, :, width:] = jnp.ones((groups, vh.shape[1], width), BF16)
        place(pk_ref, kf, kh, 0, groups)
        place(ck_ref, kf, kh, WIN, groups)
        place(pv_ref, kf, vh, 0, groups)
        place(cv_ref, kf, vh, WIN, groups)
        mine[...] = token_rows(BLK, heads)

    nf[...] = q_ref[...].astype(F32)
    tf[...] = k_ref[...].astype(F32)
    sf[...] = v_ref[...].astype(F32)
    base = pl.multiple_of(block * BLK, BLK)
    reach = jnp.where(where_ref[0] == 0, WIN - block * BLK, 0)
    bias = jnp.where(lax.broadcasted_iota(jnp.int32, (1, WIN + BLK), 1) < reach, MASKED, 0.0).astype(F32)
    row = lax.broadcasted_iota(jnp.int32, (BLK, BLK), 0)
    col = lax.broadcasted_iota(jnp.int32, (BLK, BLK), 1)
    inner = (block > 0).astype(F32).astype(BF16)
    each = heads // COLS
    q = [every(q_ref, nf, heads, h) for h in range(heads)]
    inside = [
        lax.dot_general(q[h], every(k_ref, tf, heads, h), (((1,), (1,)), ((), ())), preferred_element_type=F32)
        for h in range(heads)
    ]
    for h in range(heads):
        weight = jnp.where(col <= row, inside[h], 0.0) * (gain_ref[h, 0] * gain_factor(0, width))
        left = jnp.concatenate([weight.astype(BF16), q[h], q[h]], axis=1)
        cross = cross_ref[h // each, h % each]
        right = jnp.concatenate([every(v_ref, sf, heads, h), cross, local_ref[0, h] * inner], axis=0)
        of[pl.ds(h, BLK, stride=heads), :] = jnp.dot(left, right, preferred_element_type=F32)
    full = window_block(wq_ref, kh, vh, logits, weights, base, groups, bias) + of[...]
    out_ref[...] = full
    square_ref[0] = square_sums(full, mine[...])


def trunk_attention(where, gain, q, k, v, wq, before_kv, ck, cv, local, cross, heads, groups, first, steps):
    width = q.shape[1]
    rows = BLK * heads
    at_block = pl.BlockSpec((rows, width), lambda i: (i + first, 0))
    whole = pl.BlockSpec((WIN * groups, width), lambda i: (0, 0))
    second = pl.BlockSpec((WIN * groups, width), lambda i: (1, 0))
    before = pl.BlockSpec((1, heads, width, width), lambda i: (jnp.maximum(i + first - 1, 0), 0, 0, 0))
    wide = pltpu.VMEM((rows, width), F32)
    return pl.pallas_call(
        functools.partial(trunk_kernel, heads, groups, first),
        grid=(steps,),
        in_specs=[smem(), smem()] + [at_block] * 4 + [whole, second, whole, whole, before, pl.BlockSpec(cross.shape, lambda i: (0, 0, 0, 0))],
        out_specs=[pl.BlockSpec((rows, width), lambda i: (i, 0)), pl.BlockSpec((1, 8, BLK), lambda i: (i, 0, 0))],
        out_shape=[
            jax.ShapeDtypeStruct((steps * rows, width), F32),
            jax.ShapeDtypeStruct((steps, 8, BLK), F32),
        ],
        scratch_shapes=[
            wide,
            wide,
            wide,
            pltpu.VMEM((WIN * groups, width), F32),
            pltpu.VMEM((groups, 2 * WIN, width), BF16),
            pltpu.VMEM((groups, 2 * WIN, 2 * width), BF16),
            wide,
            pltpu.VMEM((BLK, rows), BF16),
            *window_scratch(heads, groups),
        ],
        compiler_params=params(),
        cost_estimate=attention_cost(steps * BLK, heads, width, 2 * steps * BLK * BLK * heads * 3 * width),
        name="trunk_attention",
    )(where, gain, q, k, v, wq, before_kv, before_kv, ck, cv, local, cross)


def near_kernel(groups, where_ref, fork_ref, q_ref, ck_ref, cv_ref, *rest):
    kv_refs, out_ref = rest[:COLS], rest[COLS]
    kf, kh, vh, kt, logits, weights = rest[COLS + 1 :]
    step = pl.program_id(0)
    width = q_ref.shape[1]
    column = where_ref[0] & (COLS - 1)
    start = pl.multiple_of(fork_ref[0] * BLK, BLK)

    @pl.when(step == 0)
    def _():
        for i in range(COLS):
            kt[column ^ i] = kv_refs[i][...]
        vh[:, :, width:] = jnp.ones((groups, vh.shape[1], width), BF16)
        place(kt.at[0], kf, vh, 0, groups)
        place(kt.at[1], kf, vh, WIN, groups)
        place(kt.at[2], kf, kh, 0, groups)
        place(kt.at[3], kf, kh, WIN, groups)
        place(ck_ref, kf, kh, pl.multiple_of(start + WIN, BLK), groups)
        place(cv_ref, kf, vh, pl.multiple_of(start + WIN, BLK), groups)

    base = pl.multiple_of(start + step * BLK, BLK)
    out_ref[...] = window_block(q_ref, kh, vh, logits, weights, base, groups).astype(BF16)


def near_attention(where, fork, wq, ck, cv, kvs, heads, groups):
    width = wq.shape[1]
    steps = WIN // BLK
    at_block = pl.BlockSpec((BLK * heads, width), lambda i: (i, 0))
    whole = pl.BlockSpec((WIN * groups, width), lambda i: (0, 0))
    return pl.pallas_call(
        functools.partial(near_kernel, groups),
        grid=(steps,),
        in_specs=[smem(), smem(), at_block, whole, whole] + [whole] * COLS,
        out_specs=at_block,
        out_shape=jax.ShapeDtypeStruct((steps * BLK * heads, width), BF16),
        scratch_shapes=[
            pltpu.VMEM((WIN * groups, width), F32),
            pltpu.VMEM((groups, 3 * WIN, width), BF16),
            pltpu.VMEM((groups, 3 * WIN, 2 * width), BF16),
            pltpu.VMEM((COLS, WIN * groups, width), BF16),
            *window_scratch(heads, groups),
        ],
        compiler_params=params(),
        cost_estimate=attention_cost(steps * BLK, heads, width),
        name="near_attention",
    )(where, fork, wq, ck, cv, *kvs)


def branch_kernel(heads, where_ref, fork_ref, trunk_square, q_hbm, near_hbm, far_hbm, *rest):
    end_hbms, (full_hbm, square_ref, qs, ws, nf, of, fs, es, mine) = rest[:COLS], rest[COLS : COLS + 9]
    q_sems, w_sems, f_sems, e_sems = rest[COLS + 9 :]
    rows = BLK * heads
    blocks = ws.shape[0] // rows
    near = near_hbm.shape[0] // rows
    each = heads // COLS
    column = where_ref[0] & (COLS - 1)
    states = [
        pltpu.make_async_copy(end_hbms[i].at[fork_ref[0]], es.at[column ^ i], e_sems.at[i]) for i in range(COLS)
    ]
    for copy in states:
        copy.start()
    for b in range(blocks):
        block_copy(q_hbm, qs, q_sems, b, rows).start()
        if b < near:
            block_copy(near_hbm, ws, w_sems, b, rows).start()
        else:
            block_copy(far_hbm, ws, w_sems, b, rows, b - near).start()
    mine[...] = token_rows(BLK, heads)
    square_ref[blocks:] = trunk_square[...]
    for copy in states:
        copy.wait()

    def one_block(b, carry):
        block_copy(q_hbm, qs, q_sems, b, rows).wait()
        block_copy(near_hbm, ws, w_sems, b, rows, 0).wait()
        at = pl.ds(pl.multiple_of(b * rows, rows), rows)
        nf[...] = qs[at, :].astype(F32)
        for h in range(heads):
            q = nf[pl.ds(h, BLK, stride=heads), :].astype(BF16)
            of[pl.ds(h, BLK, stride=heads), :] = jnp.dot(q, es[h // each, h % each], preferred_element_type=F32)
        full = ws[at, :].astype(F32) + of[...]
        fs[at, :] = full
        block_copy(fs, full_hbm, f_sems, b, rows).start()
        square_ref[b] = square_sums(full, mine[...])
        return carry

    lax.fori_loop(0, blocks, one_block, 0)
    for b in range(blocks):
        block_copy(fs, full_hbm, f_sems, b, rows).wait()


def branch_linear(where, fork, trunk_square, q, near, far, ends, heads):
    width = q.shape[1]
    rows = BLK * heads
    blocks = q.shape[0] // rows
    return pl.pallas_call(
        functools.partial(branch_kernel, heads),
        in_specs=[smem(), smem(), vmem()] + [hbm()] * (3 + COLS),
        out_specs=[hbm(), vmem()],
        out_shape=[jax.ShapeDtypeStruct(q.shape, F32), jax.ShapeDtypeStruct((blocks + trunk_square.shape[0], 8, BLK), F32)],
        scratch_shapes=[
            pltpu.VMEM(q.shape, BF16),
            pltpu.VMEM(q.shape, BF16),
            pltpu.VMEM((rows, width), F32),
            pltpu.VMEM((rows, width), F32),
            pltpu.VMEM(q.shape, F32),
            pltpu.VMEM((COLS, heads // COLS, width, width), BF16),
            pltpu.VMEM((BLK, rows), BF16),
            pltpu.SemaphoreType.DMA((blocks,)),
            pltpu.SemaphoreType.DMA((blocks,)),
            pltpu.SemaphoreType.DMA((blocks,)),
            pltpu.SemaphoreType.DMA((COLS,)),
        ],
        compiler_params=params(),
        cost_estimate=pl.CostEstimate(flops=4 * q.size * width, bytes_accessed=8 * q.size, transcendentals=0),
        name="branch_linear",
    )(where, fork, trunk_square, q, near, far, *ends)


def norm_kernel(heads, features, trunk_hbm, branch_hbm, square_ref, other_ref, trunk_out, branch_out, held, done, in_sems, out_sems):
    rows = BLK * heads
    width = held.shape[1]
    trunk_blocks = trunk_hbm.shape[0] // rows
    branch_blocks = branch_hbm.shape[0] // rows

    def arrive(src, block, slot):
        return pltpu.make_async_copy(
            src.at[pl.ds(block * rows, rows)], held.at[pl.ds(slot * rows, rows)], in_sems.at[slot]
        )

    def leave(dst, block, slot):
        return pltpu.make_async_copy(
            done.at[pl.ds(slot * rows, rows)], dst.at[pl.ds(block * rows, rows)], out_sems.at[slot]
        )

    parts = ((branch_hbm, branch_out, 0, branch_blocks), (trunk_hbm, trunk_out, branch_blocks, trunk_blocks))
    for src, _, first, blocks in parts:
        for b in range(blocks):
            arrive(src, b, first + b).start()
    for src, dst, first, blocks in parts:

        def one_block(b, carry):
            slot = first + b
            arrive(src, b, slot).wait()
            at = pl.ds(pl.multiple_of(slot * rows, rows), rows)
            square = square_ref[slot, 0:1, :] + other_ref[slot, 0:1, :]
            scale = lax.rsqrt(square / features + 1e-06)
            scale = jnp.broadcast_to(scale, (width, BLK)).T
            full = held[at, :].reshape(BLK, heads, width)
            done[at, :] = (full * scale[:, None, :]).astype(BF16).reshape(rows, width)
            leave(dst, b, slot).start()
            return carry

        lax.fori_loop(0, blocks, one_block, 0)
    for _, dst, first, blocks in parts:
        for b in range(blocks):
            leave(dst, b, first + b).wait()


def normalize(trunk, branch, square, other, heads, features):
    total = trunk.shape[0] + branch.shape[0]
    slots = total // (BLK * heads)
    return pl.pallas_call(
        functools.partial(norm_kernel, heads, features),
        in_specs=[hbm(), hbm(), vmem(), vmem()],
        out_specs=[hbm(), hbm()],
        out_shape=[jax.ShapeDtypeStruct(trunk.shape, BF16), jax.ShapeDtypeStruct(branch.shape, BF16)],
        scratch_shapes=[
            pltpu.VMEM((total, trunk.shape[1]), F32),
            pltpu.VMEM((total, trunk.shape[1]), BF16),
            pltpu.SemaphoreType.DMA((slots,)),
            pltpu.SemaphoreType.DMA((slots,)),
        ],
        compiler_params=params(),
        cost_estimate=pl.CostEstimate(
            flops=2 * (trunk.size + branch.size), bytes_accessed=6 * (trunk.size + branch.size), transcendentals=0
        ),
        name="normalize",
    )(trunk, branch, square, other)


def shards(
    trunk_query,
    trunk_key,
    trunk_value,
    trunk_wquery,
    trunk_wkey,
    trunk_wvalue,
    branch_query,
    branch_wquery,
    branch_wkey,
    branch_wvalue,
    level_gain,
    fork_block,
):
    tokens, heads, width = trunk_query.shape
    groups = trunk_wkey.shape[1]
    depth = (tokens // BLK).bit_length() - 1
    count = lax.axis_size("seq")
    planes = count // COLS
    features = heads * lax.axis_size("head") * width
    me = lax.axis_index("seq")
    column, plane = me % COLS, me // COLS
    where = me.astype(jnp.int32).reshape(1)
    root = count - 1
    top = planes - 1

    def flat(x):
        return x.reshape(x.shape[0] * x.shape[1], x.shape[2])

    tq, tk, tv, twq = flat(trunk_query), flat(trunk_key), flat(trunk_value), flat(trunk_wquery)
    twk, twv = flat(trunk_wkey), flat(trunk_wvalue)
    bq, bwq, bwk, bwv = flat(branch_query), flat(branch_wquery), flat(branch_wkey), flat(branch_wvalue)

    def send(x, pairs):
        return lax.ppermute(x, "seq", pairs)

    def down_step(x, step):
        starts = [p for p in range(planes) if (top - p) % (2 * step) == 0 and p >= step]
        pairs = [(p * COLS + c, (p - step) * COLS + c) for p in starts for c in range(COLS)]
        got = send(x, pairs)
        hit = functools.reduce(jnp.logical_or, [plane == p - step for p in starts])
        return jnp.where(hit, got, x)

    def down_first(x):
        return down_step(x, planes // 2)

    def down_rest(x):
        step = planes // 4
        while step:
            x = down_step(x, step)
            step //= 2
        return x

    def around(x):
        return [x] + [send(x, [(i, i ^ d) for i in range(count)]) for d in range(1, COLS)]

    def in_groups(x, groups_of):
        return lax.all_to_all(x, "seq", 0, 0, tiled=True, axis_index_groups=groups_of)

    in_one_plane = [[p * COLS + c for c in range(COLS)] for p in range(planes)]
    in_one_column = [[p * COLS + c for p in range(planes)] for c in range(COLS)]
    tie = lax.optimization_barrier

    def down(x):
        return down_rest(down_first(x))

    half = COLS // 2
    got = send(twv, [(root - i, root - i - half) for i in range(half)])
    kv = down(jnp.where(column >= half, twk, got))
    before_kv = send(jnp.concatenate([twk, twv], axis=0), [(i, i + 1) for i in range(count - 1)])

    *pieces, local, shard_sum = block_sums(level_gain, tk, tv, heads, depth)
    mine = pieces[COLS - 1]
    for c in range(COLS - 1):
        mine = jnp.where(column == c, send(pieces[c], [(root, root - (COLS - 1) + c)]), mine)
    sums = in_groups(shard_sum, in_one_plane)
    plane_sum, ends = plane_sums(where, level_gain, sums, mine, planes, depth)
    plane_sum = in_groups(plane_sum, in_one_column)
    ends = down(ends)
    cross, above = cross_sums(where, level_gain, sums, plane_sum, depth)
    cross = in_groups(cross, in_one_plane)

    far = far_attention(bwq, bwk, bwv, heads, groups)
    kv, far = tie((kv, far))
    kvs = around(kv)
    ends = around((ends.astype(F32) + above).astype(BF16))
    trunk_full, trunk_square = trunk_attention(
        where, level_gain, tq, tk, tv, twq, before_kv, twk, twv, local, cross, heads, groups, 0, tokens // BLK
    )
    trunk_full, bwq = tie((trunk_full, bwq))
    near = near_attention(where, fork_block, bwq, bwk, bwv, kvs, heads, groups)
    branch_full, square = branch_linear(where, fork_block, trunk_square, bq, near, far, ends, heads)
    other = lax.ppermute(square, "head", [(0, 1), (1, 0)])
    trunk_out, branch_out = normalize(trunk_full, branch_full, square, other, heads, features)
    return trunk_out.reshape(trunk_query.shape), branch_out.reshape(branch_query.shape)


def solution(mesh):
    rows = P("seq", "head", None)
    return jax.shard_map(
        shards,
        mesh=mesh,
        in_specs=(rows,) * 10 + (P("head", None), P("seq")),
        out_specs=(rows, rows),
        check_vma=False,
    )
```

```python
import functools
import math

import jax
import jax.numpy as jnp
from jax import lax
from jax.experimental import pallas as pl
from jax.experimental.pallas import tpu as pltpu
from jax.sharding import PartitionSpec as P

BLK = 128
WIN = 512
COLS = 4
MASKED = -1e30
CHUNK = 32
F32 = jnp.float32
BF16 = jnp.bfloat16
VMEM_BYTES = 60 * 1024 * 1024
SMALL_BYTES = 28 * 1024 * 1024


def params(limit=VMEM_BYTES):
    return pltpu.CompilerParams(vmem_limit_bytes=limit)


def hbm():
    return pl.BlockSpec(memory_space=pltpu.HBM)


def vmem():
    return pl.BlockSpec(memory_space=pltpu.VMEM)


def block_copy(src, dst, sems, block, rows, src_block=None):
    src_block = block if src_block is None else src_block
    return pltpu.make_async_copy(
        src.at[pl.ds(src_block * rows, rows)], dst.at[pl.ds(block * rows, rows)], sems.at[block]
    )


def smem():
    return pl.BlockSpec(memory_space=pltpu.SMEM)


def gain_factor(level, width):
    return 1.0 / math.sqrt(width * BLK * 2 ** max(level - 1, 0))


def every(rows_ref, wide, count, each):
    return wide[pl.ds(each, rows_ref.shape[0] // count, stride=count), :].astype(BF16)


def state_kernel(depth, heads, gain_ref, k_hbm, v_hbm, *rest):
    piece_refs = rest[:COLS]
    local_ref, sum_ref, keys, values, kf, vf, levels, key_sems, value_sems = rest[COLS:]
    rows, width = kf.shape
    each = heads // COLS
    copies = [
        (block_copy(k_hbm, keys, key_sems, b, rows), block_copy(v_hbm, values, value_sems, b, rows))
        for b in range(1 << depth)
    ]
    for pair in copies:
        for copy in pair:
            copy.start()
    for b, pair in enumerate(copies):
        for copy in pair:
            copy.wait()
        kf[...] = keys[b * rows : (b + 1) * rows].astype(F32)
        vf[...] = values[b * rows : (b + 1) * rows].astype(F32)
        for h in range(heads):
            k = kf[pl.ds(h, BLK, stride=heads), :].astype(BF16)
            v = vf[pl.ds(h, BLK, stride=heads), :].astype(BF16)
            merged = lax.dot_general(k, v, (((0,), (0,)), ((), ())), preferred_element_type=F32)
            before = None
            for bit in range(depth):
                if b >> bit & 1:
                    part = levels[bit, h] * (gain_ref[h, bit + 1] * gain_factor(bit + 1, width))
                    before = part if before is None else before + part
            carry = 0
            while b >> carry & 1:
                merged = merged + levels[carry, h]
                carry += 1
            if before is not None:
                before = before.astype(BF16)
                local_ref[b - 1, h] = before
                piece_refs[h // each][b - 1, h % each] = before
            if carry < depth:
                levels[carry, h] = merged
            else:
                sum_ref[h // each, h % each] = merged.astype(BF16)


def block_sums(gain, keys, values, heads, depth):
    blocks = 1 << depth
    width = keys.shape[1]
    each = heads // COLS
    return pl.pallas_call(
        functools.partial(state_kernel, depth, heads),
        in_specs=[smem(), hbm(), hbm()],
        out_specs=[vmem()] * (COLS + 2),
        out_shape=[jax.ShapeDtypeStruct((blocks - 1, each, width, width), BF16)] * COLS
        + [
            jax.ShapeDtypeStruct((blocks - 1, heads, width, width), BF16),
            jax.ShapeDtypeStruct((COLS, each, width, width), BF16),
        ],
        scratch_shapes=[
            pltpu.VMEM(keys.shape, BF16),
            pltpu.VMEM(values.shape, BF16),
            pltpu.VMEM((keys.shape[0] // blocks, width), F32),
            pltpu.VMEM((keys.shape[0] // blocks, width), F32),
            pltpu.VMEM((depth, heads, width, width), F32),
            pltpu.SemaphoreType.DMA((blocks,)),
            pltpu.SemaphoreType.DMA((blocks,)),
        ],
        compiler_params=params(),
        cost_estimate=pl.CostEstimate(
            flops=2 * keys.size * width, bytes_accessed=4 * keys.size + 2 * heads * width * width * blocks, transcendentals=0
        ),
        name="block_sums",
    )(gain, keys, values)


def in_plane(sums, column, weight):
    total = None
    for bit in range(COLS.bit_length() - 1):
        if column >> bit & 1:
            first = ((column >> bit) ^ 1) << bit
            part = functools.reduce(jnp.add, sums[first : first + (1 << bit)]) * weight(bit)
            total = part if total is None else total + part
    return total


def level_weight(gain_ref, head, depth, width, bit):
    return gain_ref[head, depth + bit + 1] * gain_factor(depth + bit + 1, width)


def plane_kernel(depth, where_ref, gain_ref, sums_ref, plane_ref, before_ref):
    each, width = sums_ref.shape[1], sums_ref.shape[2]
    first = (where_ref[0] & (COLS - 1)) * each
    for j in range(each):
        sums = [sums_ref[c, j].astype(F32) for c in range(COLS)]
        whole = functools.reduce(jnp.add, sums).astype(BF16)
        for p in range(plane_ref.shape[0]):
            plane_ref[p, j] = whole
        before_ref[j] = in_plane(sums, COLS - 1, lambda bit: level_weight(gain_ref, first + j, depth, width, bit))


def plane_sums(where, gain, sums, planes, depth):
    quarter = sums.shape[1:]
    return pl.pallas_call(
        functools.partial(plane_kernel, depth),
        in_specs=[smem(), smem(), vmem()],
        out_specs=[vmem(), vmem()],
        out_shape=[jax.ShapeDtypeStruct((planes, *quarter), BF16), jax.ShapeDtypeStruct(quarter, F32)],
        compiler_params=params(SMALL_BYTES),
        cost_estimate=pl.CostEstimate(flops=4 * sums.size, bytes_accessed=8 * sums.size, transcendentals=0),
        name="plane_sums",
    )(where, gain, sums)


def cross_kernel(depth, where_ref, gain_ref, sums_ref, planes_ref, out_ref, top_ref):
    each, width = sums_ref.shape[1], sums_ref.shape[2]
    planes = planes_ref.shape[0]
    col_bits = COLS.bit_length() - 1
    plane = where_ref[0] >> col_bits
    first = (where_ref[0] & (COLS - 1)) * each
    for j in range(each):
        sums = [sums_ref[c, j].astype(F32) for c in range(COLS)]
        above = jnp.zeros((width, width), F32)
        top = jnp.zeros((width, width), F32)
        for s in range(planes - 1):
            state = planes_ref[s, j].astype(F32)
            share = jnp.float32(0.0)
            for bit in range(planes.bit_length() - 1):
                weight = level_weight(gain_ref, first + j, depth, width, col_bits + bit)
                held = jnp.logical_and((plane >> bit) & 1 == 1, (plane >> bit) ^ 1 == s >> bit)
                share = share + jnp.where(held, weight, 0.0)
                if ((planes - 1) >> bit) ^ 1 == s >> bit:
                    top = top + state * weight
            above = above + state * share
        top_ref[j] = top
        for c in range(COLS):
            before = in_plane(sums, c, lambda bit: level_weight(gain_ref, first + j, depth, width, bit))
            out_ref[c, j] = (above if before is None else above + before).astype(BF16)


def cross_sums(where, gain, sums, planes, depth):
    return pl.pallas_call(
        functools.partial(cross_kernel, depth),
        in_specs=[smem(), smem(), vmem(), vmem()],
        out_specs=[vmem(), vmem()],
        out_shape=[jax.ShapeDtypeStruct(sums.shape, BF16), jax.ShapeDtypeStruct(sums.shape[1:], F32)],
        compiler_params=params(SMALL_BYTES),
        cost_estimate=pl.CostEstimate(flops=20 * sums.size, bytes_accessed=8 * sums.size, transcendentals=0),
        name="cross_sums",
    )(where, gain, sums, planes)


def place(src_ref, wide, dst, start, groups):
    tokens = src_ref.shape[0] // groups
    wide[...] = src_ref[...].astype(F32)
    for g in range(groups):
        part = wide[pl.ds(g, tokens, stride=groups), :].astype(BF16)
        dst[g, pl.ds(start, tokens), : src_ref.shape[1]] = part


def split_groups(wide):
    rows, width = wide.shape
    pairs = wide.reshape(rows // 16, 16, width)
    low, high = pairs[:, :8], pairs[:, 8:]
    upper = lax.broadcasted_iota(jnp.int32, low.shape, 1) < 4
    first = jnp.where(upper, low, pltpu.roll(high, 4, 1))
    second = jnp.where(upper, pltpu.roll(low, 4, 1), high)
    return [part.reshape(rows // 2, width) for part in (first, second)]


def join_groups(first, second):
    rows, width = first.shape
    first, second = (part.reshape(rows // 8, 8, width) for part in (first, second))
    upper = lax.broadcasted_iota(jnp.int32, first.shape, 1) < 4
    low = jnp.where(upper, first, pltpu.roll(second, 4, 1))
    high = jnp.where(upper, pltpu.roll(first, 4, 1), second)
    return jnp.concatenate([low, high], axis=1).reshape(2 * rows, width)


def window_block(q_ref, kh, vh, logits, weights, base, groups, bias=None):
    width = q_ref.shape[1]
    span = WIN + BLK
    share = q_ref.shape[0] // BLK // groups
    parts = [part.astype(BF16) for part in split_groups(q_ref[...].astype(F32))]
    scale = math.log2(math.e) / math.sqrt(width)
    for g in range(groups):
        logits[g] = lax.dot_general(
            parts[g], kh[g, pl.ds(base, span), :], (((1,), (1,)), ((), ())), preferred_element_type=F32
        )
    row = lax.broadcasted_iota(jnp.int32, (CHUNK, BLK), 0) // share
    ahead = lax.broadcasted_iota(jnp.int32, (CHUNK, BLK), 1) - row
    outs = []
    for g in range(groups):
        for r in range(0, BLK * share, CHUNK):
            late = ahead > r // share
            first = jnp.where(late, logits[g, r : r + CHUNK, :BLK], MASKED)
            last = jnp.where(late, MASKED, logits[g, r : r + CHUNK, WIN:])
            now = jnp.concatenate([first, logits[g, r : r + CHUNK, BLK:WIN], last], axis=1)
            if bias is not None:
                now = now + bias
            top = jnp.max(now, axis=1, keepdims=True)
            weights[g, r : r + CHUNK, :] = jnp.exp2((now - top) * scale).astype(BF16)
        both = jnp.dot(weights[g], vh[g, pl.ds(base, span), :], preferred_element_type=F32)
        outs.append(both[:, :width] / both[:, width:])
    return join_groups(*outs)


def window_scratch(heads, groups):
    rows = BLK * heads // groups
    return [pltpu.VMEM((groups, rows, WIN + BLK), F32), pltpu.VMEM((groups, rows, WIN + BLK), BF16)]


def token_rows(tokens, heads):
    row = lax.broadcasted_iota(jnp.int32, (tokens, tokens * heads), 1) // heads
    return (row == lax.broadcasted_iota(jnp.int32, (tokens, tokens * heads), 0)).astype(F32).astype(BF16)


def square_sums(full, mine):
    sums = jnp.dot(mine, (full * full).astype(BF16), preferred_element_type=F32)
    ones = jnp.ones((8, full.shape[1]), F32)
    return lax.dot_general(
        ones, sums, (((1,), (1,)), ((), ())), precision=lax.Precision.HIGHEST, preferred_element_type=F32
    )


def far_kernel(heads, groups, q_ref, pk_ref, pv_ref, ck_ref, cv_ref, out_ref, kf, kh, vh, logits, weights):
    step = pl.program_id(0)
    width = q_ref.shape[1]

    @pl.when(step == 0)
    def _():
        vh[:, :, width:] = jnp.ones((groups, vh.shape[1], width), BF16)
        place(pk_ref, kf, kh, 0, groups)
        place(ck_ref, kf, kh, WIN, groups)
        place(pv_ref, kf, vh, 0, groups)
        place(cv_ref, kf, vh, WIN, groups)

    out_ref[...] = window_block(q_ref, kh, vh, logits, weights, pl.multiple_of(step * BLK, BLK), groups).astype(BF16)


def attention_cost(tokens, heads, width, extra=0):
    span = WIN + BLK
    return pl.CostEstimate(
        flops=6 * tokens * heads * span * width + extra,
        bytes_accessed=12 * tokens * heads * width,
        transcendentals=tokens * heads * span,
    )


def far_attention(queries, keys, values, heads, groups):
    width = queries.shape[1]
    steps = queries.shape[0] // (BLK * heads) - WIN // BLK
    skip = WIN // BLK
    at_first = pl.BlockSpec((WIN * groups, width), lambda i: (0, 0))
    at_next = pl.BlockSpec((WIN * groups, width), lambda i: (1, 0))
    return pl.pallas_call(
        functools.partial(far_kernel, heads, groups),
        grid=(steps,),
        in_specs=[
            pl.BlockSpec((BLK * heads, width), lambda i: (i + skip, 0)),
            at_first,
            at_first,
            at_next,
            at_next,
        ],
        out_specs=pl.BlockSpec((BLK * heads, width), lambda i: (i, 0)),
        out_shape=jax.ShapeDtypeStruct((steps * BLK * heads, width), BF16),
        scratch_shapes=[
            pltpu.VMEM((WIN * groups, width), F32),
            pltpu.VMEM((groups, 2 * WIN, width), BF16),
            pltpu.VMEM((groups, 2 * WIN, 2 * width), BF16),
            *window_scratch(heads, groups),
        ],
        compiler_params=params(),
        cost_estimate=attention_cost(steps * BLK, heads, width),
        name="far_attention",
    )(queries, keys, values, keys, values)


def trunk_kernel(heads, groups, first, where_ref, gain_ref, q_ref, k_ref, v_ref, wq_ref, pk_ref, pv_ref, ck_ref, cv_ref, local_ref, cross_ref, out_ref, square_ref, nf, tf, sf, kf, kh, vh, of, mine, logits, weights):
    block = pl.program_id(0) + first
    width = q_ref.shape[1]

    @pl.when(pl.program_id(0) == 0)
    def _():
        vh[:, :, width:] = jnp.ones((groups, vh.shape[1], width), BF16)
        place(pk_ref, kf, kh, 0, groups)
        place(ck_ref, kf, kh, WIN, groups)
        place(pv_ref, kf, vh, 0, groups)
        place(cv_ref, kf, vh, WIN, groups)
        mine[...] = token_rows(BLK, heads)

    nf[...] = q_ref[...].astype(F32)
    tf[...] = k_ref[...].astype(F32)
    sf[...] = v_ref[...].astype(F32)
    base = pl.multiple_of(block * BLK, BLK)
    reach = jnp.where(where_ref[0] == 0, WIN - block * BLK, 0)
    bias = jnp.where(lax.broadcasted_iota(jnp.int32, (1, WIN + BLK), 1) < reach, MASKED, 0.0).astype(F32)
    row = lax.broadcasted_iota(jnp.int32, (BLK, BLK), 0)
    col = lax.broadcasted_iota(jnp.int32, (BLK, BLK), 1)
    inner = (block > 0).astype(F32).astype(BF16)
    each = heads // COLS
    q = [every(q_ref, nf, heads, h) for h in range(heads)]
    inside = [
        lax.dot_general(q[h], every(k_ref, tf, heads, h), (((1,), (1,)), ((), ())), preferred_element_type=F32)
        for h in range(heads)
    ]
    for h in range(heads):
        weight = jnp.where(col <= row, inside[h], 0.0) * (gain_ref[h, 0] * gain_factor(0, width))
        left = jnp.concatenate([weight.astype(BF16), q[h], q[h]], axis=1)
        cross = cross_ref[h // each, h % each]
        right = jnp.concatenate([every(v_ref, sf, heads, h), cross, local_ref[0, h] * inner], axis=0)
        of[pl.ds(h, BLK, stride=heads), :] = jnp.dot(left, right, preferred_element_type=F32)
    full = window_block(wq_ref, kh, vh, logits, weights, base, groups, bias) + of[...]
    out_ref[...] = full
    square_ref[0] = square_sums(full, mine[...])


def trunk_attention(where, gain, q, k, v, wq, before_kv, ck, cv, local, cross, heads, groups, first, steps):
    width = q.shape[1]
    rows = BLK * heads
    at_block = pl.BlockSpec((rows, width), lambda i: (i + first, 0))
    whole = pl.BlockSpec((WIN * groups, width), lambda i: (0, 0))
    second = pl.BlockSpec((WIN * groups, width), lambda i: (1, 0))
    before = pl.BlockSpec((1, heads, width, width), lambda i: (jnp.maximum(i + first - 1, 0), 0, 0, 0))
    wide = pltpu.VMEM((rows, width), F32)
    return pl.pallas_call(
        functools.partial(trunk_kernel, heads, groups, first),
        grid=(steps,),
        in_specs=[smem(), smem()] + [at_block] * 4 + [whole, second, whole, whole, before, pl.BlockSpec(cross.shape, lambda i: (0, 0, 0, 0))],
        out_specs=[pl.BlockSpec((rows, width), lambda i: (i, 0)), pl.BlockSpec((1, 8, BLK), lambda i: (i, 0, 0))],
        out_shape=[
            jax.ShapeDtypeStruct((steps * rows, width), F32),
            jax.ShapeDtypeStruct((steps, 8, BLK), F32),
        ],
        scratch_shapes=[
            wide,
            wide,
            wide,
            pltpu.VMEM((WIN * groups, width), F32),
            pltpu.VMEM((groups, 2 * WIN, width), BF16),
            pltpu.VMEM((groups, 2 * WIN, 2 * width), BF16),
            wide,
            pltpu.VMEM((BLK, rows), BF16),
            *window_scratch(heads, groups),
        ],
        compiler_params=params(),
        cost_estimate=attention_cost(steps * BLK, heads, width, 2 * steps * BLK * BLK * heads * 3 * width),
        name="trunk_attention",
    )(where, gain, q, k, v, wq, before_kv, before_kv, ck, cv, local, cross)


def near_kernel(groups, where_ref, fork_ref, q_ref, ck_ref, cv_ref, *rest):
    kv_refs, out_ref = rest[:COLS], rest[COLS]
    kf, kh, vh, kt, logits, weights = rest[COLS + 1 :]
    step = pl.program_id(0)
    width = q_ref.shape[1]
    column = where_ref[0] & (COLS - 1)
    start = pl.multiple_of(fork_ref[0] * BLK, BLK)

    @pl.when(step == 0)
    def _():
        for i in range(COLS):
            kt[column ^ i] = kv_refs[i][...]
        vh[:, :, width:] = jnp.ones((groups, vh.shape[1], width), BF16)
        place(kt.at[0], kf, vh, 0, groups)
        place(kt.at[1], kf, vh, WIN, groups)
        place(kt.at[2], kf, kh, 0, groups)
        place(kt.at[3], kf, kh, WIN, groups)
        place(ck_ref, kf, kh, pl.multiple_of(start + WIN, BLK), groups)
        place(cv_ref, kf, vh, pl.multiple_of(start + WIN, BLK), groups)

    base = pl.multiple_of(start + step * BLK, BLK)
    out_ref[...] = window_block(q_ref, kh, vh, logits, weights, base, groups).astype(BF16)


def near_attention(where, fork, wq, ck, cv, kvs, heads, groups):
    width = wq.shape[1]
    steps = WIN // BLK
    at_block = pl.BlockSpec((BLK * heads, width), lambda i: (i, 0))
    whole = pl.BlockSpec((WIN * groups, width), lambda i: (0, 0))
    return pl.pallas_call(
        functools.partial(near_kernel, groups),
        grid=(steps,),
        in_specs=[smem(), smem(), at_block, whole, whole] + [whole] * COLS,
        out_specs=at_block,
        out_shape=jax.ShapeDtypeStruct((steps * BLK * heads, width), BF16),
        scratch_shapes=[
            pltpu.VMEM((WIN * groups, width), F32),
            pltpu.VMEM((groups, 3 * WIN, width), BF16),
            pltpu.VMEM((groups, 3 * WIN, 2 * width), BF16),
            pltpu.VMEM((COLS, WIN * groups, width), BF16),
            *window_scratch(heads, groups),
        ],
        compiler_params=params(),
        cost_estimate=attention_cost(steps * BLK, heads, width),
        name="near_attention",
    )(where, fork, wq, ck, cv, *kvs)


def branch_kernel(heads, where_ref, fork_ref, trunk_square, q_hbm, near_hbm, far_hbm, *rest):
    end_hbms, (full_hbm, square_ref, qs, ws, nf, of, fs, es, mine) = rest[:COLS], rest[COLS : COLS + 9]
    q_sems, w_sems, f_sems, e_sems = rest[COLS + 9 :]
    rows = BLK * heads
    blocks = ws.shape[0] // rows
    near = near_hbm.shape[0] // rows
    each = heads // COLS
    column = where_ref[0] & (COLS - 1)
    states = [
        pltpu.make_async_copy(end_hbms[i].at[fork_ref[0]], es.at[column ^ i], e_sems.at[i]) for i in range(COLS)
    ]
    for copy in states:
        copy.start()
    for b in range(blocks):
        block_copy(q_hbm, qs, q_sems, b, rows).start()
        if b < near:
            block_copy(near_hbm, ws, w_sems, b, rows).start()
        else:
            block_copy(far_hbm, ws, w_sems, b, rows, b - near).start()
    mine[...] = token_rows(BLK, heads)
    square_ref[blocks:] = trunk_square[...]
    for copy in states:
        copy.wait()

    def one_block(b, carry):
        block_copy(q_hbm, qs, q_sems, b, rows).wait()
        block_copy(near_hbm, ws, w_sems, b, rows, 0).wait()
        at = pl.ds(pl.multiple_of(b * rows, rows), rows)
        nf[...] = qs[at, :].astype(F32)
        for h in range(heads):
            q = nf[pl.ds(h, BLK, stride=heads), :].astype(BF16)
            of[pl.ds(h, BLK, stride=heads), :] = jnp.dot(q, es[h // each, h % each], preferred_element_type=F32)
        full = ws[at, :].astype(F32) + of[...]
        fs[at, :] = full
        block_copy(fs, full_hbm, f_sems, b, rows).start()
        square_ref[b] = square_sums(full, mine[...])
        return carry

    lax.fori_loop(0, blocks, one_block, 0)
    for b in range(blocks):
        block_copy(fs, full_hbm, f_sems, b, rows).wait()


def branch_linear(where, fork, trunk_square, q, near, far, ends, heads):
    width = q.shape[1]
    rows = BLK * heads
    blocks = q.shape[0] // rows
    return pl.pallas_call(
        functools.partial(branch_kernel, heads),
        in_specs=[smem(), smem(), vmem()] + [hbm()] * (3 + COLS),
        out_specs=[hbm(), vmem()],
        out_shape=[jax.ShapeDtypeStruct(q.shape, F32), jax.ShapeDtypeStruct((blocks + trunk_square.shape[0], 8, BLK), F32)],
        scratch_shapes=[
            pltpu.VMEM(q.shape, BF16),
            pltpu.VMEM(q.shape, BF16),
            pltpu.VMEM((rows, width), F32),
            pltpu.VMEM((rows, width), F32),
            pltpu.VMEM(q.shape, F32),
            pltpu.VMEM((COLS, heads // COLS, width, width), BF16),
            pltpu.VMEM((BLK, rows), BF16),
            pltpu.SemaphoreType.DMA((blocks,)),
            pltpu.SemaphoreType.DMA((blocks,)),
            pltpu.SemaphoreType.DMA((blocks,)),
            pltpu.SemaphoreType.DMA((COLS,)),
        ],
        compiler_params=params(),
        cost_estimate=pl.CostEstimate(flops=4 * q.size * width, bytes_accessed=8 * q.size, transcendentals=0),
        name="branch_linear",
    )(where, fork, trunk_square, q, near, far, *ends)


def norm_kernel(heads, features, trunk_hbm, branch_hbm, square_ref, other_ref, trunk_out, branch_out, held, done, in_sems, out_sems):
    rows = BLK * heads
    width = held.shape[1]
    trunk_blocks = trunk_hbm.shape[0] // rows
    branch_blocks = branch_hbm.shape[0] // rows

    def arrive(src, block, slot):
        return pltpu.make_async_copy(
            src.at[pl.ds(block * rows, rows)], held.at[pl.ds(slot * rows, rows)], in_sems.at[slot]
        )

    def leave(dst, block, slot):
        return pltpu.make_async_copy(
            done.at[pl.ds(slot * rows, rows)], dst.at[pl.ds(block * rows, rows)], out_sems.at[slot]
        )

    parts = ((branch_hbm, branch_out, 0, branch_blocks), (trunk_hbm, trunk_out, branch_blocks, trunk_blocks))
    for src, _, first, blocks in parts:
        for b in range(blocks):
            arrive(src, b, first + b).start()
    for src, dst, first, blocks in parts:

        def one_block(b, carry):
            slot = first + b
            arrive(src, b, slot).wait()
            at = pl.ds(pl.multiple_of(slot * rows, rows), rows)
            square = square_ref[slot, 0:1, :] + other_ref[slot, 0:1, :]
            scale = lax.rsqrt(square / features + 1e-06)
            scale = jnp.broadcast_to(scale, (width, BLK)).T
            full = held[at, :].reshape(BLK, heads, width)
            done[at, :] = (full * scale[:, None, :]).astype(BF16).reshape(rows, width)
            leave(dst, b, slot).start()
            return carry

        lax.fori_loop(0, blocks, one_block, 0)
    for _, dst, first, blocks in parts:
        for b in range(blocks):
            leave(dst, b, first + b).wait()


def normalize(trunk, branch, square, other, heads, features):
    total = trunk.shape[0] + branch.shape[0]
    slots = total // (BLK * heads)
    return pl.pallas_call(
        functools.partial(norm_kernel, heads, features),
        in_specs=[hbm(), hbm(), vmem(), vmem()],
        out_specs=[hbm(), hbm()],
        out_shape=[jax.ShapeDtypeStruct(trunk.shape, BF16), jax.ShapeDtypeStruct(branch.shape, BF16)],
        scratch_shapes=[
            pltpu.VMEM((total, trunk.shape[1]), F32),
            pltpu.VMEM((total, trunk.shape[1]), BF16),
            pltpu.SemaphoreType.DMA((slots,)),
            pltpu.SemaphoreType.DMA((slots,)),
        ],
        compiler_params=params(),
        cost_estimate=pl.CostEstimate(
            flops=2 * (trunk.size + branch.size), bytes_accessed=6 * (trunk.size + branch.size), transcendentals=0
        ),
        name="normalize",
    )(trunk, branch, square, other)


def shards(
    trunk_query,
    trunk_key,
    trunk_value,
    trunk_wquery,
    trunk_wkey,
    trunk_wvalue,
    branch_query,
    branch_wquery,
    branch_wkey,
    branch_wvalue,
    level_gain,
    fork_block,
):
    tokens, heads, width = trunk_query.shape
    groups = trunk_wkey.shape[1]
    depth = (tokens // BLK).bit_length() - 1
    count = lax.axis_size("seq")
    planes = count // COLS
    features = heads * lax.axis_size("head") * width
    me = lax.axis_index("seq")
    column, plane = me % COLS, me // COLS
    where = me.astype(jnp.int32).reshape(1)
    root = count - 1
    top = planes - 1

    def flat(x):
        return x.reshape(x.shape[0] * x.shape[1], x.shape[2])

    tq, tk, tv, twq = flat(trunk_query), flat(trunk_key), flat(trunk_value), flat(trunk_wquery)
    twk, twv = flat(trunk_wkey), flat(trunk_wvalue)
    bq, bwq, bwk, bwv = flat(branch_query), flat(branch_wquery), flat(branch_wkey), flat(branch_wvalue)

    def send(x, pairs):
        return lax.ppermute(x, "seq", pairs)

    def down_step(x, step):
        starts = [p for p in range(planes) if (top - p) % (2 * step) == 0 and p >= step]
        pairs = [(p * COLS + c, (p - step) * COLS + c) for p in starts for c in range(COLS)]
        got = send(x, pairs)
        hit = functools.reduce(jnp.logical_or, [plane == p - step for p in starts])
        return jnp.where(hit, got, x)

    def down_first(x):
        return down_step(x, planes // 2)

    def down_rest(x):
        step = planes // 4
        while step:
            x = down_step(x, step)
            step //= 2
        return x

    def around(x):
        return [x] + [send(x, [(i, i ^ d) for i in range(count)]) for d in range(1, COLS)]

    def in_groups(x, groups_of):
        return lax.all_to_all(x, "seq", 0, 0, tiled=True, axis_index_groups=groups_of)

    in_one_plane = [[p * COLS + c for c in range(COLS)] for p in range(planes)]
    in_one_column = [[p * COLS + c for p in range(planes)] for c in range(COLS)]
    tie = lax.optimization_barrier

    def down(x):
        return down_rest(down_first(x))

    half = COLS // 2
    got = send(twv, [(root - i, root - i - half) for i in range(half)])
    before_kv = send(jnp.concatenate([twk, twv], axis=0), [(i, i + 1) for i in range(count - 1)])

    *pieces, local, shard_sum = block_sums(level_gain, tk, tv, heads, depth)
    gots = [send(pieces[c], [(root, root - (COLS - 1) + c)]) for c in range(COLS - 1)]
    sums = in_groups(shard_sum, in_one_plane)
    kv = jnp.where(column >= half, twk, got)
    sums, kv = tie((sums, kv))
    kv = down_first(kv)
    plane_sum, before = plane_sums(where, level_gain, sums, planes, depth)
    plane_sum = in_groups(plane_sum, in_one_column)
    gots, plane_sum, kv = tie((gots, plane_sum, kv))
    kv = down_rest(kv)
    mine = pieces[COLS - 1]
    for c in range(COLS - 1):
        mine = jnp.where(column == c, gots[c], mine)
    ends = jnp.concatenate([jnp.zeros_like(mine[:1]), mine], axis=0)
    ends = down((before[None] + ends.astype(F32)).astype(BF16))
    cross, above = cross_sums(where, level_gain, sums, plane_sum, depth)
    cross = in_groups(cross, in_one_plane)

    far = far_attention(bwq, bwk, bwv, heads, groups)
    kv, far = tie((kv, far))
    kvs = around(kv)
    ends = around((ends.astype(F32) + above).astype(BF16))
    trunk_full, trunk_square = trunk_attention(
        where, level_gain, tq, tk, tv, twq, before_kv, twk, twv, local, cross, heads, groups, 0, tokens // BLK
    )
    trunk_full, bwq = tie((trunk_full, bwq))
    near = near_attention(where, fork_block, bwq, bwk, bwv, kvs, heads, groups)
    branch_full, square = branch_linear(where, fork_block, trunk_square, bq, near, far, ends, heads)
    other = lax.ppermute(square, "head", [(0, 1), (1, 0)])
    trunk_out, branch_out = normalize(trunk_full, branch_full, square, other, heads, features)
    return trunk_out.reshape(trunk_query.shape), branch_out.reshape(branch_query.shape)


def solution(mesh):
    rows = P("seq", "head", None)
    return jax.shard_map(
        shards,
        mesh=mesh,
        in_specs=(rows,) * 10 + (P("head", None), P("seq")),
        out_specs=(rows, rows),
        check_vma=False,
    )
```
